512 devices in a mesh: dp: 64 (over z, x), tensor: 8 (over y, core).
Axes of the slice: x: 4, y: 4, z: 16, core: 2. Of those that a mesh axis runs over, the one named last changes fastest.
Arguments:
- states: float32 [256, 64, 128, 128], P('dp', 'tensor'), may hold values from -90 to 90
- from_shard: int32 [128], replicated, may hold values from 0 to 63, as said below
- from_slot: int32 [128], replicated, may hold values from 0 to 3
- projected: bfloat16 [3, 128, 4, 8192], P(None, 'dp', None, 'tensor'), may hold values from -6 to 6
- decay_rate: float32 [64], P('tensor'), may hold values from 0.01 to 1
- norm_gain: float32 [8192], P('tensor'), may hold values from 0.5 to 1.5
Outputs:
- attended: bfloat16 [3, 128, 8192], P(None, 'dp', 'tensor')
- final_states: float32 [128, 64, 128, 128], P('dp', 'tensor')
The draws below stay inside these ranges and needn't reach their ends.
Inputs may be any that keep to these rules, and one draw needn't show every extreme that they name: Row r belongs to dp shard r // 2. No pair (from_shard, from_slot) repeats. from_shard[r] lies within 2 shards of r // 2 along dp, counted around the cycle. At most 1 row of one shard comes from any one other shard; in every draw some shard takes 1 row from each of the two shards above it, and another takes 1 from each of the two below it.
All inputs are finite; a program needn't handle non-finite values.
Results may differ from the reference program's by a relative error of at most 0.0014.
Values sent between devices are 32-bit elements; how exact they have to be, the bound alone decides.
No kernel may reach another device: no remote copies, remote signals or barrier semaphores. Data moves between devices by JAX's collectives and lax.ppermute only.
A program may use at most 64 MiB of HBM per device.

```python
import math
import jax
import jax.numpy as jnp
from jax import lax

H = 64
DH = 128
LIVE = 2
STEPS = 3
HID = 8192
SLOTS = 4
ROWS = 128
CAPACITY = 256


def stride_column(stride):
    return jnp.where(stride < 0, stride + 2, stride + 1)


def migration_plan(key):
    shards = ROWS // LIVE
    per_pair = LIVE // 2
    stride_key, order_key, anchor_key, slot_key = jax.random.split(key, 4)
    stride_table = jnp.array([0, -2, -1, 1, 2, -1, 1, 0], jnp.int32)
    wanted = stride_table[jax.random.randint(stride_key, (ROWS,), 0, 8)]
    anchor = jax.random.randint(anchor_key, (), 0, shards)
    row_ids = jnp.arange(ROWS, dtype=jnp.int32)
    target = row_ids // LIVE
    within = row_ids % LIVE
    near_end = target == anchor
    far_end = target == (anchor + 4) % shards
    wanted = jnp.where(near_end, jnp.where(within < per_pair, -2, -1), jnp.where(far_end, jnp.where(within < per_pair, 1, 2), wanted))
    forced = near_end | far_end
    forced_ones = forced.astype(jnp.int32)
    roots = (target - jnp.where(forced, wanted, 0)) % shards
    send_load = jnp.zeros((shards,), jnp.int32).at[roots].add(forced_ones)
    pair_load = jnp.zeros((shards, 4), jnp.int32).at[roots, stride_column(wanted)].add(forced_ones)
    visit = jax.random.permutation(order_key, ROWS)

    def settle(visit_idx, loop_state):
        send_load, pair_load, roots = loop_state
        current = visit[visit_idx]
        stride = wanted[current]
        source = (target[current] - stride) % shards
        column = stride_column(stride)
        accept = jnp.logical_not(forced[current]) & (stride != 0) & (send_load[source] < LIVE) & (pair_load[source, column] < per_pair)
        gained = accept.astype(jnp.int32)
        send_load = send_load.at[source].add(gained)
        pair_load = pair_load.at[source, column].add(gained)
        roots = roots.at[current].set(jnp.where(accept, source, roots[current]))
        return (send_load, pair_load, roots)
    send_load, pair_load, roots = lax.fori_loop(0, ROWS, settle, (send_load, pair_load, roots))
    earlier = row_ids[:, None] > row_ids[None, :]
    slot_rank = jnp.sum(((roots[:, None] == roots[None, :]) & earlier).astype(jnp.int32), axis=1)

    def shuffled(sub_key):
        return jax.random.permutation(sub_key, SLOTS)
    slot_orders = jax.vmap(shuffled)(jax.random.split(slot_key, shards))
    slots = slot_orders[roots, slot_rank]
    return (roots.astype(jnp.int32), slots.astype(jnp.int32))


def draw_from_shard(key, part):
    plan = migration_plan(key)
    return plan[0]


def draw_from_slot(key, part):
    plan = migration_plan(key)
    return plan[1]


def draw_states(key, part):
    key = jax.random.fold_in(key, 11)
    entry_key, spread_key = jax.random.split(key, 2)
    dims_all = (CAPACITY, H, DH, DH)
    position = jnp.arange(H, dtype=jnp.float32) / max(H - 1, 1)
    entries = jnp.clip(jax.random.normal(entry_key, dims_all, jnp.float32), -4.0, 4.0)
    head_scale = math.sqrt(3.0) ** position * jnp.exp(math.log(6.0) * jax.random.uniform(spread_key, (H,), jnp.float32))
    return entries * head_scale[None, :, None, None]


def level_of(stream_key, shape, cuts, low, high):
    gain = 1.0
    for dim, blocks in cuts:
        steps = jax.random.uniform(jax.random.fold_in(jax.random.fold_in(stream_key, 6), dim), (blocks,), jnp.float32, low / len(cuts), high / len(cuts))
        gain = gain * jnp.repeat(jnp.exp(steps), shape[dim] // blocks).reshape((-1,) + (1,) * (len(shape) - 1 - dim))
    return gain


def noise(key, extent, deviation, most, cuts=(), held_as=jnp.bfloat16):
    gain = level_of(key, extent, cuts, -0.22, 0.18) if cuts else 1.0
    values = jax.random.normal(key, extent, jnp.float32) * deviation * gain
    return jnp.minimum(jnp.maximum(values, -most), most).astype(held_as)


def setup_inputs(seed: int = 0) -> dict:
    streams_of = jax.random.split(jax.random.key(seed), 7)
    return {
        "states": draw_states(jax.random.fold_in(streams_of[6], 71), 0),
        "from_shard": draw_from_shard(jax.random.fold_in(streams_of[6], 71), 0),
        "from_slot": draw_from_slot(jax.random.fold_in(streams_of[6], 71), 0),
        "projected": noise(streams_of[3], (STEPS, ROWS, 4, HID), 1.0, 6.0, ((1, 64), (3, 8))),
        "decay_rate": jnp.clip(jnp.exp(math.log(1.0) - 4.6051702 * jax.random.uniform(streams_of[4], (H,), jnp.float32) ** level_of(streams_of[4], (H,), ((0, 8),), -0.2, 0.2)), 0.01, 1.0),
        "norm_gain": jnp.clip(1.0 + 0.1 * jax.random.normal(streams_of[5], (HID,), jnp.float32), 0.5, 1.5),
    }


def reference(states, from_shard, from_slot, projected, decay_rate, norm_gain):
    flat_index = (from_shard * SLOTS + from_slot).astype(jnp.int32)
    activity = projected.astype(jnp.float32)
    retain = jnp.exp(-decay_rate)

    def one_row(row_idx):
        running = lax.dynamic_index_in_dim(states, flat_index[row_idx], 0, keepdims=False)
        row_activity = lax.dynamic_index_in_dim(activity, row_idx, 1, keepdims=False)
        collected = []
        for step_idx in range(STEPS):
            queries = jax.nn.silu(row_activity[step_idx, 0]).reshape(H, DH)
            keys_now = jax.nn.silu(row_activity[step_idx, 1]).reshape(H, DH)
            values_now = jax.nn.silu(row_activity[step_idx, 2]).reshape(H, DH)
            gates = jax.nn.sigmoid(row_activity[step_idx, 3])
            running = retain[:, None, None] * running + keys_now[:, :, None] * values_now[:, None, :]
            attn_now = jnp.einsum('hi,hij->hj', queries, running, precision=lax.Precision.HIGHEST).reshape(H * DH)
            scale = lax.rsqrt(jnp.mean(attn_now * attn_now) + 1e-05)
            collected.append((attn_now * scale * norm_gain * gates).astype(jnp.bfloat16))
        return (jnp.stack(collected), running)
    attended, final_states = lax.map(one_row, jnp.arange(ROWS, dtype=jnp.int32))
    return (jnp.transpose(attended, (1, 0, 2)), final_states)
```

```python
import functools
import jax
import jax.numpy as jnp
from jax import lax
from jax.experimental import pallas as pl
from jax.experimental.pallas import tpu as pltpu
from jax.sharding import PartitionSpec as P

EPS = 1e-05


def shifted(block, axis, distance):
    size = lax.axis_size(axis)
    route = [((i - distance) % size, i) for i in range(size)]
    return lax.ppermute(block, axis, route)


def split(x):
    high = lax.reduce_precision(x, 8, 7)
    return high.astype(jnp.bfloat16), (x - high).astype(jnp.bfloat16)


def pick_kernel(shards, live, strides, place, shard_ref, slot_ref, states, *refs):
    outs, sems = refs[:-1], refs[-1]
    device = place[0]
    copies = []
    for n, stride in enumerate(strides):
        target = lax.rem(device + stride + shards, shards)
        slot = jnp.int32(0)
        for row in range(live):
            mine = shard_ref[target * live + row] == device
            slot = jnp.where(mine, slot_ref[target * live + row], slot)
        copy = pltpu.make_async_copy(states.at[slot], outs[n], sems.at[n])
        copy.start()
        copies.append(copy)
    for copy in copies:
        copy.wait()


def pick(place, from_shard, from_slot, states, shards, live, strides):
    row = jax.ShapeDtypeStruct(states.shape[1:], states.dtype)
    smem = pl.BlockSpec(memory_space=pltpu.SMEM)
    return pl.pallas_call(
        functools.partial(pick_kernel, shards, live, strides),
        out_shape=[row] * len(strides),
        in_specs=[smem] * 3 + [pl.BlockSpec(memory_space=pltpu.HBM)],
        out_specs=[pl.BlockSpec(memory_space=pl.ANY)] * len(strides),
        scratch_shapes=[pltpu.SemaphoreType.DMA((len(strides),))],
        name="pick_rows",
    )(place, from_shard, from_slot, states)


def step_kernel(
    shards, live, strides, place, shard_ref, slot_ref, states, *refs
):
    n = len(strides)
    arrived = refs[:n]
    qs, ks, vs, base, decay, final, raw, sums, held, made, sem_in, sem_out = refs[n:]
    device = place[0]
    heads = held.shape[1]
    half = heads // 2

    def fetch(row, part):
        owner = shard_ref[device * live + row]
        slot = slot_ref[device * live + row]
        gap = lax.rem(device - owner + shards, shards)
        span = pl.ds(part * half, half)
        target = held.at[row, span]
        sem = sem_in.at[row, part]

        @pl.when(gap == 0)
        def _():
            pltpu.make_async_copy(states.at[slot, span], target, sem).start()

        for k, stride in enumerate(strides):

            @pl.when(gap == stride % shards)
            def _():
                pltpu.make_async_copy(arrived[k].at[span], target, sem).start()

    parts = [(row, part) for row in range(live) for part in range(2)]
    for row, part in parts:
        fetch(row, part)
    out_copies = []
    for row, part in parts:
        span = pl.ds(part * half, half)
        pltpu.make_async_copy(
            arrived[0].at[span], held.at[row, span], sem_in.at[row, part]
        ).wait()
        for head in range(part * half, (part + 1) * half):
            state = held[row, head]
            high = state.astype(jnp.bfloat16)
            low = (state - high.astype(jnp.float32)).astype(jnp.bfloat16)
            q = qs[row, head]
            first = jnp.dot(q, high, preferred_element_type=jnp.float32)
            second = jnp.dot(q, low, preferred_element_type=jnp.float32)
            raw[row, head] = first[:8] + first[8:] + second[:8] + base[row, head]
            outer = lax.dot_general(
                ks[row, head],
                vs[row, head],
                (((0,), (0,)), ((), ())),
                preferred_element_type=jnp.float32,
            )
            made[row, head] = decay[row, head] * state + outer
        copy = pltpu.make_async_copy(
            made.at[row, span], final.at[row, span], sem_out.at[row, part]
        )
        copy.start()
        out_copies.append(copy)
    for row in range(live):
        total = raw[row, 0] * raw[row, 0]
        for head in range(1, heads):
            total = total + raw[row, head] * raw[row, head]
        sums[row] = jnp.broadcast_to(jnp.sum(total, axis=1, keepdims=True), sums.shape[1:])
    for copy in out_copies:
        copy.wait()


def run_steps(place, from_shard, from_slot, states, arrived, small, shards, live, strides):
    heads, dim = states.shape[1], states.shape[2]
    smem = pl.BlockSpec(memory_space=pltpu.SMEM)
    hbm = pl.BlockSpec(memory_space=pl.ANY)
    vmem = pl.BlockSpec(memory_space=pltpu.VMEM)
    f32 = jnp.float32
    return pl.pallas_call(
        functools.partial(step_kernel, shards, live, strides),
        out_shape=[
            jax.ShapeDtypeStruct((live, heads, dim, dim), f32),
            jax.ShapeDtypeStruct((live, heads, 8, dim), f32),
            jax.ShapeDtypeStruct((live, 8, dim), f32),
        ],
        in_specs=[smem] * 3 + [pl.BlockSpec(memory_space=pltpu.HBM)] + [hbm] * len(strides) + [vmem] * len(small),
        out_specs=[hbm, vmem, vmem],
        scratch_shapes=[
            pltpu.VMEM((live, heads, dim, dim), f32),
            pltpu.VMEM((live, heads, dim, dim), f32),
            pltpu.SemaphoreType.DMA((live, 2)),
            pltpu.SemaphoreType.DMA((live, 2)),
        ],
        compiler_params=pltpu.CompilerParams(vmem_limit_bytes=16 * 1024 * 1024),
        name="decode_steps",
    )(place, from_shard, from_slot, states, *arrived, *small)


def on_device(states, from_shard, from_slot, projected, decay_rate, norm_gain):
    shards = lax.axis_size("dp")
    steps, live = projected.shape[:2]
    heads, dim = states.shape[1], states.shape[2]
    features = heads * dim * lax.axis_size("tensor")
    place = lax.axis_index("dp").astype(jnp.int32).reshape(1)
    strides = (2, -2, 1, -1)
    rows = pick(place, from_shard, from_slot, states, shards, live, strides)
    near_up, near_down = shifted(rows[0], "dp", 1), shifted(rows[1], "dp", -1)
    up, down = shifted(rows[2], "dp", 1), shifted(rows[3], "dp", -1)
    far_up, far_down = shifted(near_up, "dp", 1), shifted(near_down, "dp", -1)
    arrived = [far_up, far_down, up, down]

    activity = projected.astype(jnp.float32)
    by_head = jnp.transpose(
        activity.reshape(steps, live, 4, heads, dim), (2, 1, 3, 0, 4)
    )
    queries, keys, values = (jax.nn.silu(by_head[i]) for i in range(3))
    gates = jax.nn.sigmoid(by_head[3])
    retain = jnp.exp(-decay_rate)
    power = [jnp.ones_like(retain)]
    for _ in range(steps):
        power.append(power[-1] * retain)
    grown = queries * jnp.stack(power[1:], axis=1)[None, :, :, None]
    faded = keys * jnp.stack(power[steps - 1 :: -1], axis=1)[None, :, :, None]
    base = []
    for t in range(steps):
        total = 0.0
        for u in range(t + 1):
            match = jnp.sum(queries[:, :, t] * keys[:, :, u], axis=-1, keepdims=True)
            total = total + power[t - u][None, :, None] * match * values[:, :, u]
        base.append(total)

    def rows_of(parts, count):
        whole = jnp.concatenate(parts, axis=2)
        return jnp.pad(whole, ((0, 0), (0, 0), (0, count - whole.shape[2]), (0, 0)))

    q_high, q_low = split(grown)
    k_high, k_low = split(faded)
    v_high, v_low = split(values)
    small = [
        jnp.concatenate([rows_of([q_high], 8), rows_of([q_low], 8)], axis=2),
        rows_of([k_high, k_low, k_high], 16),
        rows_of([v_high, v_high, v_low], 16),
        rows_of([jnp.stack(base, axis=2)], 8),
        jnp.broadcast_to(power[steps][None, :, None, None], (live, heads, 1, dim)),
    ]
    final, raw, sums = run_steps(
        place, from_shard, from_slot, states, arrived, small, shards, live, strides
    )
    group = lax.axis_size("tensor")
    mine = sums[:, :steps, 0].reshape(1, live * steps)
    mine = jnp.pad(mine, ((0, 0), (0, dim - live * steps)))
    everyone = lax.all_to_all(
        jnp.broadcast_to(mine[None], (group, 1, dim)), "tensor", 0, 0
    )
    totals = jnp.sum(everyone, axis=0)[0, : live * steps].reshape(live, 1, steps, 1)
    scale = lax.rsqrt(totals / features + EPS)
    gain = norm_gain.reshape(1, heads, 1, dim)
    attended = raw[:, :, :steps] * scale * gain * gates
    attended = jnp.transpose(attended, (2, 0, 1, 3)).reshape(steps, live, heads * dim)
    return attended.astype(jnp.bfloat16), final


def solution(mesh):
    return jax.shard_map(
        on_device,
        mesh=mesh,
        in_specs=(
            P("dp", "tensor", None, None),
            P(),
            P(),
            P(None, "dp", None, "tensor"),
            P("tensor"),
            P("tensor"),
        ),
        out_specs=(P(None, "dp", "tensor"), P("dp", "tensor", None, None)),
        check_vma=False,
    )
```

```python
import functools
import jax
import jax.numpy as jnp
from jax import lax
from jax.experimental import pallas as pl
from jax.experimental.pallas import tpu as pltpu
from jax.sharding import PartitionSpec as P

EPS = 1e-05


def shifted(block, axis, distance):
    size = lax.axis_size(axis)
    route = [((i - distance) % size, i) for i in range(size)]
    return lax.ppermute(block, axis, route)


def split(x):
    high = lax.reduce_precision(x, 8, 7)
    return high.astype(jnp.bfloat16), (x - high).astype(jnp.bfloat16)


def pick_kernel(shards, live, strides, place, shard_ref, slot_ref, states, *refs):
    outs, sems = refs[:-1], refs[-1]
    device = place[0]
    copies = []
    for n, stride in enumerate(strides):
        target = lax.rem(device + stride + shards, shards)
        slot = jnp.int32(0)
        for row in range(live):
            mine = shard_ref[target * live + row] == device
            slot = jnp.where(mine, slot_ref[target * live + row], slot)
        copy = pltpu.make_async_copy(states.at[slot], outs[n], sems.at[n])
        copy.start()
        copies.append(copy)
    for copy in copies:
        copy.wait()


def pick(place, from_shard, from_slot, states, shards, live, strides):
    row = jax.ShapeDtypeStruct(states.shape[1:], states.dtype)
    smem = pl.BlockSpec(memory_space=pltpu.SMEM)
    return pl.pallas_call(
        functools.partial(pick_kernel, shards, live, strides),
        out_shape=[row] * len(strides),
        in_specs=[smem] * 3 + [pl.BlockSpec(memory_space=pltpu.HBM)],
        out_specs=[pl.BlockSpec(memory_space=pl.ANY)] * len(strides),
        scratch_shapes=[pltpu.SemaphoreType.DMA((len(strides),))],
        compiler_params=pltpu.CompilerParams(vmem_limit_bytes=1024 * 1024),
        name="pick_rows",
    )(place, from_shard, from_slot, states)


def step_kernel(
    shards, live, strides, place, shard_ref, slot_ref, states, *refs
):
    n = len(strides)
    arrived = refs[:n]
    qs, ks, vs, base, decay, final, raw, sums, held, made, sem_in, sem_out = refs[n:]
    device = place[0]
    heads = held.shape[1]
    half = heads // 2

    def fetch(row, part):
        owner = shard_ref[device * live + row]
        slot = slot_ref[device * live + row]
        gap = lax.rem(device - owner + shards, shards)
        span = pl.ds(part * half, half)
        target = held.at[row, span]
        sem = sem_in.at[row, part]

        @pl.when(gap == 0)
        def _():
            pltpu.make_async_copy(states.at[slot, span], target, sem).start()

        for k, stride in enumerate(strides):

            @pl.when(gap == stride % shards)
            def _():
                pltpu.make_async_copy(arrived[k].at[span], target, sem).start()

    parts = [(row, part) for row in range(live) for part in range(2)]
    for row, part in parts:
        fetch(row, part)
    out_copies = []
    for row, part in parts:
        span = pl.ds(part * half, half)
        pltpu.make_async_copy(
            arrived[0].at[span], held.at[row, span], sem_in.at[row, part]
        ).wait()
        for head in range(part * half, (part + 1) * half):
            state = held[row, head]
            high = state.astype(jnp.bfloat16)
            low = (state - high.astype(jnp.float32)).astype(jnp.bfloat16)
            q = qs[row, head]
            first = jnp.dot(q, high, preferred_element_type=jnp.float32)
            second = jnp.dot(q, low, preferred_element_type=jnp.float32)
            raw[row, head] = first[:8] + first[8:] + second[:8] + base[row, head]
            outer = lax.dot_general(
                ks[row, head],
                vs[row, head],
                (((0,), (0,)), ((), ())),
                preferred_element_type=jnp.float32,
            )
            made[row, head] = decay[row, head] * state + outer
        copy = pltpu.make_async_copy(
            made.at[row, span], final.at[row, span], sem_out.at[row, part]
        )
        copy.start()
        out_copies.append(copy)
    for row in range(live):
        total = raw[row, 0] * raw[row, 0]
        for head in range(1, heads):
            total = total + raw[row, head] * raw[row, head]
        sums[row] = jnp.broadcast_to(jnp.sum(total, axis=1, keepdims=True), sums.shape[1:])
    for copy in out_copies:
        copy.wait()


def run_steps(place, from_shard, from_slot, states, arrived, small, shards, live, strides):
    heads, dim = states.shape[1], states.shape[2]
    smem = pl.BlockSpec(memory_space=pltpu.SMEM)
    hbm = pl.BlockSpec(memory_space=pl.ANY)
    vmem = pl.BlockSpec(memory_space=pltpu.VMEM)
    f32 = jnp.float32
    return pl.pallas_call(
        functools.partial(step_kernel, shards, live, strides),
        out_shape=[
            jax.ShapeDtypeStruct((live, heads, dim, dim), f32),
            jax.ShapeDtypeStruct((live, heads, 8, dim), f32),
            jax.ShapeDtypeStruct((live, 8, dim), f32),
        ],
        in_specs=[smem] * 3 + [pl.BlockSpec(memory_space=pltpu.HBM)] + [hbm] * len(strides) + [vmem] * len(small),
        out_specs=[hbm, vmem, vmem],
        scratch_shapes=[
            pltpu.VMEM((live, heads, dim, dim), f32),
            pltpu.VMEM((live, heads, dim, dim), f32),
            pltpu.SemaphoreType.DMA((live, 2)),
            pltpu.SemaphoreType.DMA((live, 2)),
        ],
        compiler_params=pltpu.CompilerParams(vmem_limit_bytes=16 * 1024 * 1024),
        name="decode_steps",
    )(place, from_shard, from_slot, states, *arrived, *small)


def on_device(states, from_shard, from_slot, projected, decay_rate, norm_gain):
    shards = lax.axis_size("dp")
    steps, live = projected.shape[:2]
    heads, dim = states.shape[1], states.shape[2]
    features = heads * dim * lax.axis_size("tensor")
    place = lax.axis_index("dp").astype(jnp.int32).reshape(1)
    strides = (2, -2, 1, -1)
    rows = pick(place, from_shard, from_slot, states, shards, live, strides)
    near_up, near_down = shifted(rows[0], "dp", 1), shifted(rows[1], "dp", -1)
    up, down = shifted(rows[2], "dp", 1), shifted(rows[3], "dp", -1)
    far_up, far_down = shifted(near_up, "dp", 1), shifted(near_down, "dp", -1)
    arrived = [far_up, far_down, up, down]

    activity = projected.astype(jnp.float32)
    by_head = jnp.transpose(
        activity.reshape(steps, live, 4, heads, dim), (2, 1, 3, 0, 4)
    )
    queries, keys, values = (jax.nn.silu(by_head[i]) for i in range(3))
    gates = jax.nn.sigmoid(by_head[3])
    retain = jnp.exp(-decay_rate)
    power = [jnp.ones_like(retain)]
    for _ in range(steps):
        power.append(power[-1] * retain)
    grown = queries * jnp.stack(power[1:], axis=1)[None, :, :, None]
    faded = keys * jnp.stack(power[steps - 1 :: -1], axis=1)[None, :, :, None]
    base = []
    for t in range(steps):
        total = 0.0
        for u in range(t + 1):
            match = jnp.sum(queries[:, :, t] * keys[:, :, u], axis=-1, keepdims=True)
            total = total + power[t - u][None, :, None] * match * values[:, :, u]
        base.append(total)

    def rows_of(parts, count):
        whole = jnp.concatenate(parts, axis=2)
        return jnp.pad(whole, ((0, 0), (0, 0), (0, count - whole.shape[2]), (0, 0)))

    q_high, q_low = split(grown)
    k_high, k_low = split(faded)
    v_high, v_low = split(values)
    small = [
        jnp.concatenate([rows_of([q_high], 8), rows_of([q_low], 8)], axis=2),
        rows_of([k_high, k_low, k_high], 16),
        rows_of([v_high, v_high, v_low], 16),
        rows_of([jnp.stack(base, axis=2)], 8),
        jnp.broadcast_to(power[steps][None, :, None, None], (live, heads, 1, dim)),
    ]
    final, raw, sums = run_steps(
        place, from_shard, from_slot, states, arrived, small, shards, live, strides
    )
    group = lax.axis_size("tensor")
    mine = sums[:, :steps, 0].reshape(1, live * steps)
    mine = jnp.pad(mine, ((0, 0), (0, dim - live * steps)))
    everyone = lax.all_to_all(
        jnp.broadcast_to(mine[None], (group, 1, dim)), "tensor", 0, 0
    )
    totals = jnp.sum(everyone, axis=0)[0, : live * steps].reshape(live, 1, steps, 1)
    scale = lax.rsqrt(totals / features + EPS)
    gain = norm_gain.reshape(1, heads, 1, dim)
    attended = raw[:, :, :steps] * scale * gain * gates
    attended = jnp.transpose(attended, (2, 0, 1, 3)).reshape(steps, live, heads * dim)
    return attended.astype(jnp.bfloat16), final


def solution(mesh):
    return jax.shard_map(
        on_device,
        mesh=mesh,
        in_specs=(
            P("dp", "tensor", None, None),
            P(),
            P(),
            P(None, "dp", None, "tensor"),
            P("tensor"),
            P("tensor"),
        ),
        out_specs=(P(None, "dp", "tensor"), P("dp", "tensor", None, None)),
        check_vma=False,
    )
```

```python
import functools
import jax
import jax.numpy as jnp
from jax import lax
from jax.experimental import pallas as pl
from jax.experimental.pallas import tpu as pltpu
from jax.sharding import PartitionSpec as P

EPS = 1e-05


def swapped(block, axis, first):
    size = lax.axis_size(axis)
    pairs = [((first + i) % size, (first + i + 1) % size) for i in range(0, size, 2)]
    return lax.ppermute(block, axis, pairs + [(b, a) for a, b in pairs])


def side_of(device):
    return 2 * lax.rem(device, 2) - 1


def split(x):
    high = lax.reduce_precision(x, 8, 7)
    return high.astype(jnp.bfloat16), (x - high).astype(jnp.bfloat16)


def pick_kernel(shards, live, strides, place, shard_hbm, slot_hbm, states, *refs):
    outs, (shard_ref, slot_ref, sems) = refs[: len(strides)], refs[len(strides) :]
    device = place[0]
    plan = [
        pltpu.make_async_copy(shard_hbm, shard_ref, sems.at[len(strides)]),
        pltpu.make_async_copy(slot_hbm, slot_ref, sems.at[len(strides) + 1]),
    ]
    for copy in plan:
        copy.start()
    for copy in plan:
        copy.wait()
    copies = []
    for n, stride in enumerate(strides):
        target = lax.rem(device + stride * side_of(device) + shards, shards)
        slot = jnp.int32(0)
        for row in range(live):
            mine = shard_ref[target * live + row] == device
            slot = jnp.where(mine, slot_ref[target * live + row], slot)
        copy = pltpu.make_async_copy(states.at[slot], outs[n], sems.at[n])
        copy.start()
        copies.append(copy)
    for copy in copies:
        copy.wait()


def pick(place, from_shard, from_slot, states, shards, live, strides):
    row = pltpu.VMEM(states.shape[1:], states.dtype)
    fixed = [
        pltpu.with_memory_space_constraint(x, pltpu.HBM)
        for x in (from_shard, from_slot, states)
    ]
    return pl.pallas_call(
        functools.partial(pick_kernel, shards, live, strides),
        out_shape=[row] * len(strides),
        in_specs=[pl.BlockSpec(memory_space=pltpu.SMEM)]
        + [pl.BlockSpec(memory_space=pltpu.HBM)] * 3,
        out_specs=[pl.BlockSpec(memory_space=pl.ANY)] * len(strides),
        scratch_shapes=[
            pltpu.SMEM(from_shard.shape, jnp.int32),
            pltpu.SMEM(from_slot.shape, jnp.int32),
            pltpu.SemaphoreType.DMA((len(strides) + 2,)),
        ],
        compiler_params=pltpu.CompilerParams(vmem_limit_bytes=1024 * 1024),
        name="pick_rows",
    )(place, *fixed)


def step_kernel(
    shards, live, strides, place, shard_ref, slot_ref, states, *refs
):
    n = len(strides)
    arrived = refs[:n]
    qs, ks, vs, base, decay, final, raw, sums, held, made, sem_in, sem_out = refs[n:]
    device = place[0]
    heads = held.shape[1]
    half = heads // 2

    def fetch(row, part):
        owner = shard_ref[device * live + row]
        slot = slot_ref[device * live + row]
        gap = lax.rem(device - owner + shards, shards)
        span = pl.ds(part * half, half)
        target = held.at[row, span]
        sem = sem_in.at[row, part]

        @pl.when(gap == 0)
        def _():
            pltpu.make_async_copy(states.at[slot, span], target, sem).start()

        for k, stride in enumerate(strides):

            @pl.when(gap == lax.rem(stride * side_of(device) + shards, shards))
            def _():
                pltpu.make_async_copy(arrived[k].at[span], target, sem).start()

    parts = [(row, part) for row in range(live) for part in range(2)]
    for row, part in parts:
        fetch(row, part)
    out_copies = []
    for row, part in parts:
        span = pl.ds(part * half, half)
        pltpu.make_async_copy(
            arrived[0].at[span], held.at[row, span], sem_in.at[row, part]
        ).wait()
        for head in range(part * half, (part + 1) * half):
            state = held[row, head]
            high = state.astype(jnp.bfloat16)
            low = (state - high.astype(jnp.float32)).astype(jnp.bfloat16)
            q = qs[row, head]
            first = jnp.dot(q, high, preferred_element_type=jnp.float32)
            second = jnp.dot(q, low, preferred_element_type=jnp.float32)
            raw[row, head] = first[:8] + first[8:] + second[:8] + base[row, head]
            outer = lax.dot_general(
                ks[row, head],
                vs[row, head],
                (((0,), (0,)), ((), ())),
                preferred_element_type=jnp.float32,
            )
            made[row, head] = decay[row, head] * state + outer
        copy = pltpu.make_async_copy(
            made.at[row, span], final.at[row, span], sem_out.at[row, part]
        )
        copy.start()
        out_copies.append(copy)
    for row in range(live):
        total = raw[row, 0] * raw[row, 0]
        for head in range(1, heads):
            total = total + raw[row, head] * raw[row, head]
        sums[row] = jnp.broadcast_to(jnp.sum(total, axis=1, keepdims=True), sums.shape[1:])
    for copy in out_copies:
        copy.wait()


def run_steps(place, from_shard, from_slot, states, arrived, small, shards, live, strides):
    heads, dim = states.shape[1], states.shape[2]
    smem = pl.BlockSpec(memory_space=pltpu.SMEM)
    hbm = pl.BlockSpec(memory_space=pl.ANY)
    vmem = pl.BlockSpec(memory_space=pltpu.VMEM)
    f32 = jnp.float32
    return pl.pallas_call(
        functools.partial(step_kernel, shards, live, strides),
        out_shape=[
            jax.ShapeDtypeStruct((live, heads, dim, dim), f32),
            jax.ShapeDtypeStruct((live, heads, 8, dim), f32),
            jax.ShapeDtypeStruct((live, 8, dim), f32),
        ],
        in_specs=[smem] * 3 + [pl.BlockSpec(memory_space=pltpu.HBM)] + [hbm] * len(strides) + [vmem] * len(small),
        out_specs=[hbm, vmem, vmem],
        scratch_shapes=[
            pltpu.VMEM((live, heads, dim, dim), f32),
            pltpu.VMEM((live, heads, dim, dim), f32),
            pltpu.SemaphoreType.DMA((live, 2)),
            pltpu.SemaphoreType.DMA((live, 2)),
        ],
        compiler_params=pltpu.CompilerParams(vmem_limit_bytes=16 * 1024 * 1024),
        name="decode_steps",
    )(place, from_shard, from_slot, states, *arrived, *small)


def on_device(states, from_shard, from_slot, projected, decay_rate, norm_gain):
    shards = lax.axis_size("dp")
    steps, live = projected.shape[:2]
    heads, dim = states.shape[1], states.shape[2]
    features = heads * dim * lax.axis_size("tensor")
    place = lax.axis_index("dp").astype(jnp.int32).reshape(1)
    rows = pick(place, from_shard, from_slot, states, shards, live, (-2, 2, -1, 1))
    half_way_0, half_way_1 = swapped(rows[0], "dp", 0), swapped(rows[1], "dp", 1)
    next_0, next_1 = swapped(rows[2], "dp", 0), swapped(rows[3], "dp", 1)
    far_1, far_0 = swapped(half_way_0, "dp", 1), swapped(half_way_1, "dp", 0)
    strides = (2, -2, 1, -1)
    arrived = [far_0, far_1, next_0, next_1]

    activity = projected.astype(jnp.float32)
    by_head = jnp.transpose(
        activity.reshape(steps, live, 4, heads, dim), (2, 1, 3, 0, 4)
    )
    queries, keys, values = (jax.nn.silu(by_head[i]) for i in range(3))
    gates = jax.nn.sigmoid(by_head[3])
    retain = jnp.exp(-decay_rate)
    power = [jnp.ones_like(retain)]
    for _ in range(steps):
        power.append(power[-1] * retain)
    grown = queries * jnp.stack(power[1:], axis=1)[None, :, :, None]
    faded = keys * jnp.stack(power[steps - 1 :: -1], axis=1)[None, :, :, None]
    base = []
    for t in range(steps):
        total = 0.0
        for u in range(t + 1):
            match = jnp.sum(queries[:, :, t] * keys[:, :, u], axis=-1, keepdims=True)
            total = total + power[t - u][None, :, None] * match * values[:, :, u]
        base.append(total)

    def rows_of(parts, count):
        whole = jnp.concatenate(parts, axis=2)
        return jnp.pad(whole, ((0, 0), (0, 0), (0, count - whole.shape[2]), (0, 0)))

    q_high, q_low = split(grown)
    k_high, k_low = split(faded)
    v_high, v_low = split(values)
    small = [
        jnp.concatenate([rows_of([q_high], 8), rows_of([q_low], 8)], axis=2),
        rows_of([k_high, k_low, k_high], 16),
        rows_of([v_high, v_high, v_low], 16),
        rows_of([jnp.stack(base, axis=2)], 8),
        jnp.broadcast_to(power[steps][None, :, None, None], (live, heads, 1, dim)),
    ]
    final, raw, sums = run_steps(
        place, from_shard, from_slot, states, arrived, small, shards, live, strides
    )
    group = lax.axis_size("tensor")
    mine = sums[:, :steps, 0].reshape(1, live * steps)
    mine = jnp.pad(mine, ((0, 0), (0, dim - live * steps)))
    everyone = lax.all_to_all(
        jnp.broadcast_to(mine[None], (group, 1, dim)), "tensor", 0, 0
    )
    totals = jnp.sum(everyone, axis=0)[0, : live * steps].reshape(live, 1, steps, 1)
    scale = lax.rsqrt(totals / features + EPS)
    gain = norm_gain.reshape(1, heads, 1, dim)
    attended = raw[:, :, :steps] * scale * gain * gates
    attended = jnp.transpose(attended, (2, 0, 1, 3)).reshape(steps, live, heads * dim)
    return attended.astype(jnp.bfloat16), final


def solution(mesh):
    return jax.shard_map(
        on_device,
        mesh=mesh,
        in_specs=(
            P("dp", "tensor", None, None),
            P(),
            P(),
            P(None, "dp", None, "tensor"),
            P("tensor"),
            P("tensor"),
        ),
        out_specs=(P(None, "dp", "tensor"), P("dp", "tensor", None, None)),
        check_vma=False,
    )
```

```python
import functools
import jax
import jax.numpy as jnp
from jax import lax
from jax.experimental import pallas as pl
from jax.experimental.pallas import tpu as pltpu
from jax.sharding import PartitionSpec as P

EPS = 1e-05


def swapped(block, axis, first):
    size = lax.axis_size(axis)
    pairs = [((first + i) % size, (first + i + 1) % size) for i in range(0, size, 2)]
    return lax.ppermute(block, axis, pairs + [(b, a) for a, b in pairs])


def side_of(device):
    return 2 * lax.rem(device, 2) - 1


def split(x):
    high = lax.reduce_precision(x, 8, 7)
    return high.astype(jnp.bfloat16), (x - high).astype(jnp.bfloat16)


def pick_kernel(shards, live, strides, place, shard_hbm, slot_hbm, states, *refs):
    n_rows = len(strides)
    outs, (shard_ref, slot_ref, held, sems, sems_out) = refs[:n_rows], refs[n_rows:]
    device = place[0]
    plan = [
        pltpu.make_async_copy(shard_hbm, shard_ref, sems.at[n_rows]),
        pltpu.make_async_copy(slot_hbm, slot_ref, sems.at[n_rows + 1]),
    ]
    for copy in plan:
        copy.start()
    for copy in plan:
        copy.wait()
    copies = []
    for n, stride in enumerate(strides):
        target = lax.rem(device + stride * side_of(device) + shards, shards)
        slot = jnp.int32(0)
        for row in range(live):
            mine = shard_ref[target * live + row] == device
            slot = jnp.where(mine, slot_ref[target * live + row], slot)
        copy = pltpu.make_async_copy(states.at[slot], held.at[n], sems.at[n])
        copy.start()
        copies.append(copy)
    copies_out = []
    for n, copy in enumerate(copies):
        copy.wait()
        copy_out = pltpu.make_async_copy(held.at[n], outs[n], sems_out.at[n])
        copy_out.start()
        copies_out.append(copy_out)
    for copy_out in copies_out:
        copy_out.wait()


def pick(place, from_shard, from_slot, states, shards, live, strides):
    row = jax.ShapeDtypeStruct(states.shape[1:], states.dtype)
    fixed = [
        pltpu.with_memory_space_constraint(x, pltpu.HBM)
        for x in (from_shard, from_slot, states)
    ]
    return pl.pallas_call(
        functools.partial(pick_kernel, shards, live, strides),
        out_shape=[row] * len(strides),
        in_specs=[pl.BlockSpec(memory_space=pltpu.SMEM)]
        + [pl.BlockSpec(memory_space=pltpu.HBM)] * 3,
        out_specs=[pl.BlockSpec(memory_space=pl.ANY)] * len(strides),
        scratch_shapes=[
            pltpu.SMEM(from_shard.shape, jnp.int32),
            pltpu.SMEM(from_slot.shape, jnp.int32),
            pltpu.VMEM((len(strides),) + states.shape[1:], states.dtype),
            pltpu.SemaphoreType.DMA((len(strides) + 2,)),
            pltpu.SemaphoreType.DMA((len(strides),)),
        ],
        compiler_params=pltpu.CompilerParams(vmem_limit_bytes=4 * 1024 * 1024),
        name="pick_rows",
    )(place, *fixed)


def step_kernel(
    shards, live, strides, place, shard_ref, slot_ref, states, *refs
):
    n = len(strides)
    arrived = refs[:n]
    qs, ks, vs, base, decay, final, raw, sums, held, made, sem_in, sem_out = refs[n:]
    device = place[0]
    heads = held.shape[1]
    half = heads // 2

    def fetch(row, part):
        owner = shard_ref[device * live + row]
        slot = slot_ref[device * live + row]
        gap = lax.rem(device - owner + shards, shards)
        span = pl.ds(part * half, half)
        target = held.at[row, span]
        sem = sem_in.at[row, part]

        @pl.when(gap == 0)
        def _():
            pltpu.make_async_copy(states.at[slot, span], target, sem).start()

        for k, stride in enumerate(strides):

            @pl.when(gap == lax.rem(stride * side_of(device) + shards, shards))
            def _():
                pltpu.make_async_copy(arrived[k].at[span], target, sem).start()

    parts = [(row, part) for row in range(live) for part in range(2)]
    for row, part in parts:
        fetch(row, part)
    out_copies = []
    for row, part in parts:
        span = pl.ds(part * half, half)
        pltpu.make_async_copy(
            arrived[0].at[span], held.at[row, span], sem_in.at[row, part]
        ).wait()
        for head in range(part * half, (part + 1) * half):
            state = held[row, head]
            high = state.astype(jnp.bfloat16)
            low = (state - high.astype(jnp.float32)).astype(jnp.bfloat16)
            q = qs[row, head]
            first = jnp.dot(q, high, preferred_element_type=jnp.float32)
            second = jnp.dot(q, low, preferred_element_type=jnp.float32)
            raw[row, head] = first[:8] + first[8:] + second[:8] + base[row, head]
            outer = lax.dot_general(
                ks[row, head],
                vs[row, head],
                (((0,), (0,)), ((), ())),
                preferred_element_type=jnp.float32,
            )
            made[row, head] = decay[row, head] * state + outer
        copy = pltpu.make_async_copy(
            made.at[row, span], final.at[row, span], sem_out.at[row, part]
        )
        copy.start()
        out_copies.append(copy)
    for row in range(live):
        total = raw[row, 0] * raw[row, 0]
        for head in range(1, heads):
            total = total + raw[row, head] * raw[row, head]
        sums[row] = jnp.broadcast_to(jnp.sum(total, axis=1, keepdims=True), sums.shape[1:])
    for copy in out_copies:
        copy.wait()


def run_steps(place, from_shard, from_slot, states, arrived, small, shards, live, strides):
    heads, dim = states.shape[1], states.shape[2]
    smem = pl.BlockSpec(memory_space=pltpu.SMEM)
    hbm = pl.BlockSpec(memory_space=pl.ANY)
    vmem = pl.BlockSpec(memory_space=pltpu.VMEM)
    f32 = jnp.float32
    return pl.pallas_call(
        functools.partial(step_kernel, shards, live, strides),
        out_shape=[
            jax.ShapeDtypeStruct((live, heads, dim, dim), f32),
            jax.ShapeDtypeStruct((live, heads, 8, dim), f32),
            jax.ShapeDtypeStruct((live, 8, dim), f32),
        ],
        in_specs=[smem] * 3 + [pl.BlockSpec(memory_space=pltpu.HBM)] + [hbm] * len(strides) + [vmem] * len(small),
        out_specs=[hbm, vmem, vmem],
        scratch_shapes=[
            pltpu.VMEM((live, heads, dim, dim), f32),
            pltpu.VMEM((live, heads, dim, dim), f32),
            pltpu.SemaphoreType.DMA((live, 2)),
            pltpu.SemaphoreType.DMA((live, 2)),
        ],
        compiler_params=pltpu.CompilerParams(vmem_limit_bytes=16 * 1024 * 1024),
        name="decode_steps",
    )(place, from_shard, from_slot, states, *arrived, *small)


def on_device(states, from_shard, from_slot, projected, decay_rate, norm_gain):
    shards = lax.axis_size("dp")
    steps, live = projected.shape[:2]
    heads, dim = states.shape[1], states.shape[2]
    features = heads * dim * lax.axis_size("tensor")
    place = lax.axis_index("dp").astype(jnp.int32).reshape(1)
    rows = pick(place, from_shard, from_slot, states, shards, live, (-2, 2, -1, 1))
    half_way_0, half_way_1 = swapped(rows[0], "dp", 0), swapped(rows[1], "dp", 1)
    next_0, next_1 = swapped(rows[2], "dp", 0), swapped(rows[3], "dp", 1)
    far_1, far_0 = swapped(half_way_0, "dp", 1), swapped(half_way_1, "dp", 0)
    strides = (2, -2, 1, -1)
    arrived = [far_0, far_1, next_0, next_1]

    activity = projected.astype(jnp.float32)
    by_head = jnp.transpose(
        activity.reshape(steps, live, 4, heads, dim), (2, 1, 3, 0, 4)
    )
    queries, keys, values = (jax.nn.silu(by_head[i]) for i in range(3))
    gates = jax.nn.sigmoid(by_head[3])
    retain = jnp.exp(-decay_rate)
    power = [jnp.ones_like(retain)]
    for _ in range(steps):
        power.append(power[-1] * retain)
    grown = queries * jnp.stack(power[1:], axis=1)[None, :, :, None]
    faded = keys * jnp.stack(power[steps - 1 :: -1], axis=1)[None, :, :, None]
    base = []
    for t in range(steps):
        total = 0.0
        for u in range(t + 1):
            match = jnp.sum(queries[:, :, t] * keys[:, :, u], axis=-1, keepdims=True)
            total = total + power[t - u][None, :, None] * match * values[:, :, u]
        base.append(total)

    def rows_of(parts, count):
        whole = jnp.concatenate(parts, axis=2)
        return jnp.pad(whole, ((0, 0), (0, 0), (0, count - whole.shape[2]), (0, 0)))

    q_high, q_low = split(grown)
    k_high, k_low = split(faded)
    v_high, v_low = split(values)
    small = [
        jnp.concatenate([rows_of([q_high], 8), rows_of([q_low], 8)], axis=2),
        rows_of([k_high, k_low, k_high], 16),
        rows_of([v_high, v_high, v_low], 16),
        rows_of([jnp.stack(base, axis=2)], 8),
        jnp.broadcast_to(power[steps][None, :, None, None], (live, heads, 1, dim)),
    ]
    final, raw, sums = run_steps(
        place, from_shard, from_slot, states, arrived, small, shards, live, strides
    )
    group = lax.axis_size("tensor")
    mine = sums[:, :steps, 0].reshape(1, live * steps)
    mine = jnp.pad(mine, ((0, 0), (0, dim - live * steps)))
    everyone = lax.all_to_all(
        jnp.broadcast_to(mine[None], (group, 1, dim)), "tensor", 0, 0
    )
    totals = jnp.sum(everyone, axis=0)[0, : live * steps].reshape(live, 1, steps, 1)
    scale = lax.rsqrt(totals / features + EPS)
    gain = norm_gain.reshape(1, heads, 1, dim)
    attended = raw[:, :, :steps] * scale * gain * gates
    attended = jnp.transpose(attended, (2, 0, 1, 3)).reshape(steps, live, heads * dim)
    return attended.astype(jnp.bfloat16), final


def solution(mesh):
    return jax.shard_map(
        on_device,
        mesh=mesh,
        in_specs=(
            P("dp", "tensor", None, None),
            P(),
            P(),
            P(None, "dp", None, "tensor"),
            P("tensor"),
            P("tensor"),
        ),
        out_specs=(P(None, "dp", "tensor"), P("dp", "tensor", None, None)),
        check_vma=False,
    )
```

```python
import functools
import jax
import jax.numpy as jnp
from jax import lax
from jax.experimental import pallas as pl
from jax.experimental.pallas import tpu as pltpu
from jax.sharding import PartitionSpec as P

EPS = 1e-05
F32 = jnp.float32
BF16 = jnp.bfloat16
EARLY = 2
TILE = 8
MIB = 1024 * 1024


def swapped(block, axis, first):
    size = lax.axis_size(axis)
    pairs = [((first + i) % size, (first + i + 1) % size) for i in range(0, size, 2)]
    return lax.ppermute(block, axis, pairs + [(b, a) for a, b in pairs])


def side_of(device):
    return 2 * lax.rem(device, 2) - 1


def start_all(copies):
    for copy in copies:
        copy.start()


def wait_all(copies):
    for copy in copies:
        copy.wait()


def products(query, state):
    q_high = query.astype(BF16).astype(F32)
    both = jnp.concatenate([q_high, query - q_high], axis=0).astype(BF16)
    high = state.astype(BF16)
    low = (state - high.astype(F32)).astype(BF16)
    first = jnp.dot(both, high, preferred_element_type=F32)
    second = jnp.dot(both, low, preferred_element_type=F32)
    return first[:TILE] + first[TILE:] + second[:TILE]


def pick_kernel(shards, live, strides, place, shard_hbm, slot_hbm, query, states, *refs):
    n_rows = len(strides)
    outs = refs[:n_rows]
    shard_ref, slot_ref, held, tiles, sems, sems_out = refs[n_rows:]
    rows, dim = held.shape[1:]
    device = place[0]
    plan = [
        pltpu.make_async_copy(shard_hbm, shard_ref, sems.at[n_rows]),
        pltpu.make_async_copy(slot_hbm, slot_ref, sems.at[n_rows + 1]),
    ]
    start_all(plan)
    for head in range(rows // dim):
        tiles[head * TILE : (head + 1) * TILE] = query[:, head * dim : (head + 1) * dim]
    copies_out = [
        pltpu.make_async_copy(
            tiles, outs[n].at[rows : rows + tiles.shape[0]], sems_out.at[n_rows + n]
        )
        for n in range(2)
    ]
    start_all(copies_out)
    wait_all(plan)
    copies = []
    for n, stride in enumerate(strides):
        target = lax.rem(device + stride * side_of(device) + shards, shards)
        slot = jnp.int32(0)
        for row in range(live):
            mine = shard_ref[target * live + row] == device
            slot = jnp.where(mine, slot_ref[target * live + row], slot)
        copy = pltpu.make_async_copy(states.at[slot], held.at[n], sems.at[n])
        copy.start()
        copies.append(copy)
    for n, copy in enumerate(copies):
        copy.wait()
        copy_out = pltpu.make_async_copy(
            held.at[n], outs[n].at[0:rows], sems_out.at[n]
        )
        copy_out.start()
        copies_out.append(copy_out)
    wait_all(copies_out)


def pick(place, from_shard, from_slot, query, states, shards, live, strides):
    rows, dim = states.shape[1:]
    tile_rows = rows // dim * TILE
    fixed = [
        pltpu.with_memory_space_constraint(x, pltpu.HBM)
        for x in (from_shard, from_slot, states)
    ]
    hbm = pl.BlockSpec(memory_space=pltpu.HBM)
    return pl.pallas_call(
        functools.partial(pick_kernel, shards, live, strides),
        out_shape=[jax.ShapeDtypeStruct((rows + tile_rows, dim), F32)] * 2
        + [jax.ShapeDtypeStruct((rows, dim), F32)] * (len(strides) - 2),
        in_specs=[
            pl.BlockSpec(memory_space=pltpu.SMEM),
            hbm,
            hbm,
            pl.BlockSpec(memory_space=pltpu.VMEM),
            hbm,
        ],
        out_specs=[pl.BlockSpec(memory_space=pl.ANY)] * len(strides),
        scratch_shapes=[
            pltpu.SMEM(from_shard.shape, jnp.int32),
            pltpu.SMEM(from_slot.shape, jnp.int32),
            pltpu.VMEM((len(strides), rows, dim), F32),
            pltpu.VMEM((tile_rows, dim), F32),
            pltpu.SemaphoreType.DMA((len(strides) + 2,)),
            pltpu.SemaphoreType.DMA((len(strides) + 2,)),
        ],
        compiler_params=pltpu.CompilerParams(vmem_limit_bytes=6 * MIB),
        name="pick_rows",
    )(place, fixed[0], fixed[1], query, fixed[2])


def relay_kernel(from_1, from_0, lead_1, lead_0, rest_1, rest_0, held, made, sems, sems_out):
    dim = held.shape[2]
    heads = rest_0.shape[0] // dim + EARLY
    rows, early = heads * dim, EARLY * dim
    tile_rows = heads * TILE
    copies = [
        pltpu.make_async_copy(source, held.at[n], sems.at[n])
        for n, source in enumerate((from_0, from_1))
    ]
    start_all(copies)
    copies_out = []

    def send(source, target):
        copy = pltpu.make_async_copy(source, target, sems_out.at[len(copies_out)])
        copy.start()
        copies_out.append(copy)

    wait_all(copies)
    for n, (lead, rest) in enumerate(((lead_1, rest_1), (lead_0, rest_0))):
        send(held.at[n, early:rows], rest)
        send(held.at[n, 0:early], lead.at[tile_rows : tile_rows + early])
    for n, lead in enumerate((lead_1, lead_0)):
        for head in range(heads):
            query = held[1 - n, rows + head * TILE : rows + (head + 1) * TILE]
            state = held[n, head * dim : (head + 1) * dim]
            made[n, head * TILE : (head + 1) * TILE] = products(query, state)
        send(made.at[n], lead.at[0:tile_rows])
    wait_all(copies_out)


def relay(from_1, from_0, heads):
    dim = from_0.shape[1]
    lead = jax.ShapeDtypeStruct((heads * TILE + EARLY * dim, dim), F32)
    rest = jax.ShapeDtypeStruct(((heads - EARLY) * dim, dim), F32)
    anywhere = pl.BlockSpec(memory_space=pl.ANY)
    return pl.pallas_call(
        relay_kernel,
        out_shape=[lead, lead, rest, rest],
        in_specs=[anywhere] * 2,
        out_specs=[anywhere] * 4,
        scratch_shapes=[
            pltpu.VMEM((2,) + from_0.shape, F32),
            pltpu.VMEM((2, heads * TILE, dim), F32),
            pltpu.SemaphoreType.DMA((2,)),
            pltpu.SemaphoreType.DMA((6,)),
        ],
        compiler_params=pltpu.CompilerParams(vmem_limit_bytes=6 * MIB),
        name="relay_rows",
    )(from_1, from_0)


def gap_of(row, shards, live, place, shard_ref):
    device = place[0]
    return lax.rem(device - shard_ref[device * live + row] + shards, shards)


def at_stride(gap, stride, shards, place):
    return gap == lax.rem(stride * side_of(place[0]) + shards, shards)


def raw_kernel(
    shards, live, place, shard_ref, slot_ref, states, lead_1, lead_0, near_1, near_0,
    query, grown, base, raw, sums, held, made, sem_row, sem_tile,
):
    rows, dim = held.shape[1:]
    heads = rows // dim
    tile_rows = heads * TILE
    device = place[0]
    late = []
    for row in range(live):
        gap = gap_of(row, shards, live, place, shard_ref)
        slot = slot_ref[device * live + row]
        sources = [
            (gap == 0, states.at[slot]),
            (at_stride(gap, 1, shards, place), near_0),
            (at_stride(gap, -1, shards, place), near_1),
        ]
        for here, source in sources:

            @pl.when(here)
            def _():
                pltpu.make_async_copy(source, held.at[row], sem_row.at[row]).start()

        far_0 = at_stride(gap, 2, shards, place)
        far_1 = at_stride(gap, -2, shards, place)
        for here, lead in ((far_0, lead_0), (far_1, lead_1)):

            @pl.when(here)
            def _():
                pltpu.make_async_copy(
                    lead.at[0:tile_rows], made.at[row], sem_tile.at[row]
                ).start()

        late.append(jnp.logical_or(far_0, far_1))
    for row in range(live):

        @pl.when(late[row])
        def _():
            pltpu.make_async_copy(
                lead_0.at[0:tile_rows], made.at[row], sem_tile.at[row]
            ).wait()

        @pl.when(jnp.logical_not(late[row]))
        def _():
            pltpu.make_async_copy(near_0, held.at[row], sem_row.at[row]).wait()
            for head in range(heads):
                span = slice(head * dim, (head + 1) * dim)
                made[row, head * TILE : (head + 1) * TILE] = products(
                    query[:, span], held[row, span]
                )

    which = lax.rem(lax.broadcasted_iota(jnp.int32, (TILE, dim), 0), live)
    total = jnp.zeros((TILE, dim), F32)
    for head in range(heads):
        span = slice(head * dim, (head + 1) * dim)
        tile = made[0, head * TILE : (head + 1) * TILE]
        for row in range(1, live):
            other = made[row, head * TILE : (head + 1) * TILE]
            tile = jnp.where(which == row, other, tile)
        tile = tile * grown[:, span] + base[:, span]
        raw[:, span] = tile
        total = total + tile * tile
    total = jnp.broadcast_to(jnp.sum(total, axis=1, keepdims=True), (TILE, dim))
    for peer in range(sums.shape[0]):
        sums[peer] = total


def raw_of(place, from_shard, from_slot, states, arrived, small, shards, live, group):
    rows, dim = states.shape[1:]
    smem = pl.BlockSpec(memory_space=pltpu.SMEM)
    vmem = pl.BlockSpec(memory_space=pltpu.VMEM)
    anywhere = pl.BlockSpec(memory_space=pl.ANY)
    return pl.pallas_call(
        functools.partial(raw_kernel, shards, live),
        out_shape=[
            jax.ShapeDtypeStruct((TILE, rows), F32),
            jax.ShapeDtypeStruct((group, TILE, dim), F32),
        ],
        in_specs=[smem] * 3 + [anywhere] * (1 + len(arrived)) + [vmem] * len(small),
        out_specs=[vmem] * 2,
        scratch_shapes=[
            pltpu.VMEM((live, rows, dim), F32),
            pltpu.VMEM((live, rows // dim * TILE, dim), F32),
            pltpu.SemaphoreType.DMA((live,)),
            pltpu.SemaphoreType.DMA((live,)),
        ],
        compiler_params=pltpu.CompilerParams(vmem_limit_bytes=6 * MIB),
        cost_estimate=pl.CostEstimate(flops=10**12, bytes_accessed=MIB, transcendentals=0),
        name="raw_rows",
    )(place, from_shard, from_slot, states, *arrived, *small)


def final_kernel(
    shards, live, features, place, shard_ref, slot_ref, states, lead_1, lead_0,
    near_1, near_0, rest_1, rest_0, totals, raw, gated, keys, values, decay,
    attended, final, held, made, sem_in, sem_out,
):
    rows, dim = held.shape[1:]
    heads = rows // dim
    early, tile_rows = EARLY * dim, heads * TILE
    device = place[0]
    spans = (slice(0, early), slice(early, rows))
    for row in range(live):
        gap = gap_of(row, shards, live, place, shard_ref)
        slot = slot_ref[device * live + row]
        lead_span = slice(tile_rows, tile_rows + early)
        sources = [
            (gap == 0, [states.at[slot, span] for span in spans]),
            (at_stride(gap, 1, shards, place), [near_0.at[span] for span in spans]),
            (at_stride(gap, -1, shards, place), [near_1.at[span] for span in spans]),
            (at_stride(gap, 2, shards, place), [lead_0.at[lead_span], rest_0]),
            (at_stride(gap, -2, shards, place), [lead_1.at[lead_span], rest_1]),
        ]
        for here, parts in sources:

            @pl.when(here)
            def _():
                for part, source in enumerate(parts):
                    pltpu.make_async_copy(
                        source, held.at[row, spans[part]], sem_in.at[row, part]
                    ).start()

    total = totals[0]
    for peer in range(1, totals.shape[0]):
        total = total + totals[peer]
    scale = lax.rsqrt(total / features + EPS)
    for head in range(heads):
        span = slice(head * dim, (head + 1) * dim)
        tile = raw[:, span] * scale * gated[:, span]
        for step in range(attended.shape[0]):
            attended[step, :, span] = tile[step * live : (step + 1) * live].astype(BF16)
    copies_out = []
    for row in range(live):
        for part, span in enumerate(spans):
            pltpu.make_async_copy(
                near_0.at[span], held.at[row, span], sem_in.at[row, part]
            ).wait()
            for head in range(span.start // dim, span.stop // dim):
                block = slice(head * dim, (head + 1) * dim)
                outer = lax.dot_general(
                    keys[row, :, block],
                    values[row, :, block],
                    (((0,), (0,)), ((), ())),
                    preferred_element_type=F32,
                )
                made[row, block] = decay[:, block] * held[row, block] + outer
            copy = pltpu.make_async_copy(
                made.at[row, span], final.at[row, span], sem_out.at[row, part]
            )
            copy.start()
            copies_out.append(copy)
    wait_all(copies_out)


def final_of(
    place, from_shard, from_slot, states, arrived, small, shards, live, steps, features
):
    rows, dim = states.shape[1:]
    smem = pl.BlockSpec(memory_space=pltpu.SMEM)
    vmem = pl.BlockSpec(memory_space=pltpu.VMEM)
    anywhere = pl.BlockSpec(memory_space=pl.ANY)
    return pl.pallas_call(
        functools.partial(final_kernel, shards, live, features),
        out_shape=[
            jax.ShapeDtypeStruct((steps, live, rows), BF16),
            jax.ShapeDtypeStruct((live, rows, dim), F32),
        ],
        in_specs=[smem] * 3 + [anywhere] * (1 + len(arrived)) + [vmem] * len(small),
        out_specs=[vmem, anywhere],
        scratch_shapes=[
            pltpu.VMEM((live, rows, dim), F32),
            pltpu.VMEM((live, rows, dim), F32),
            pltpu.SemaphoreType.DMA((live, 2)),
            pltpu.SemaphoreType.DMA((live, 2)),
        ],
        compiler_params=pltpu.CompilerParams(vmem_limit_bytes=8 * MIB),
        name="final_rows",
    )(place, from_shard, from_slot, states, *arrived, *small)


def split(x):
    high = lax.reduce_precision(x, 8, 7)
    return high.astype(BF16), (x - high).astype(BF16)


def on_device(states, from_shard, from_slot, projected, decay_rate, norm_gain):
    shards, group = lax.axis_size("dp"), lax.axis_size("tensor")
    steps, live = projected.shape[:2]
    slots, heads, dim = states.shape[:3]
    width = heads * dim
    place = lax.axis_index("dp").astype(jnp.int32).reshape(1)
    states = states.reshape(slots, width, dim)
    activity = projected.astype(F32)

    def tile(x):
        flat = x.reshape(steps * live, width)
        return jnp.pad(flat, ((0, TILE - steps * live), (0, 0)))

    queries, keys, values = (jax.nn.silu(activity[:, :, i]) for i in range(3))
    query = tile(queries)

    rows = pick(
        place, from_shard, from_slot, query, states, shards, live, (-2, 2, -1, 1)
    )
    half_1, half_0 = swapped(rows[1], "dp", 1), swapped(rows[0], "dp", 0)
    near_1, near_0 = swapped(rows[3], "dp", 1), swapped(rows[2], "dp", 0)
    sent = relay(half_1, half_0, heads)
    lead_1, lead_0 = swapped(sent[0], "dp", 1), swapped(sent[1], "dp", 0)
    rest_1, rest_0 = swapped(sent[2], "dp", 1), swapped(sent[3], "dp", 0)

    retain = jnp.repeat(jnp.exp(-decay_rate), dim)
    power = [jnp.ones_like(retain)]
    for _ in range(steps):
        power.append(power[-1] * retain)
    base = []
    for t in range(steps):
        total = 0.0
        for u in range(t + 1):
            match = (queries[t] * keys[u]).reshape(live, heads, dim)
            match = jnp.broadcast_to(jnp.sum(match, axis=-1, keepdims=True), match.shape)
            total = total + power[t - u] * match.reshape(live, width) * values[u]
        base.append(total)
    base = tile(jnp.stack(base))
    by_step = (steps, live, width)
    grown = tile(jnp.broadcast_to(jnp.stack(power[1:])[:, None], by_step))
    gated = tile(jax.nn.sigmoid(activity[:, :, 3]) * norm_gain)
    faded = keys * jnp.stack(power[steps - 1 :: -1])[:, None]

    def stacked(*parts):
        whole = jnp.concatenate([jnp.swapaxes(part, 0, 1) for part in parts], axis=1)
        return jnp.pad(whole, ((0, 0), (0, 16 - whole.shape[1]), (0, 0)))

    k_high, k_low = split(faded)
    v_high, v_low = split(values)
    raw, sums = raw_of(
        place, from_shard, from_slot, states, (lead_1, lead_0, near_1, near_0),
        (query, grown, base), shards, live, group,
    )
    totals = lax.all_to_all(sums, "tensor", 0, 0)
    attended, final = final_of(
        place, from_shard, from_slot, states,
        (lead_1, lead_0, near_1, near_0, rest_1, rest_0),
        (
            totals,
            raw,
            gated,
            stacked(k_high, k_low, k_high),
            stacked(v_high, v_high, v_low),
            power[steps].reshape(1, width),
        ),
        shards, live, steps, width * group,
    )
    return attended, final.reshape(live, heads, dim, dim)


def solution(mesh):
    return jax.shard_map(
        on_device,
        mesh=mesh,
        in_specs=(
            P("dp", "tensor", None, None),
            P(),
            P(),
            P(None, "dp", None, "tensor"),
            P("tensor"),
            P("tensor"),
        ),
        out_specs=(P(None, "dp", "tensor"), P("dp", "tensor", None, None)),
        check_vma=False,
    )
```

```python
import functools
import jax
import jax.numpy as jnp
from jax import lax
from jax.experimental import pallas as pl
from jax.experimental.pallas import tpu as pltpu
from jax.sharding import PartitionSpec as P

EPS = 1e-05
F32 = jnp.float32
BF16 = jnp.bfloat16
EARLY = 2
TILE = 8
MIB = 1024 * 1024
SMEM = pl.BlockSpec(memory_space=pltpu.SMEM)
VMEM = pl.BlockSpec(memory_space=pltpu.VMEM)
HBM = pl.BlockSpec(memory_space=pltpu.HBM)


def swapped(block, axis, first):
    size = lax.axis_size(axis)
    pairs = [((first + i) % size, (first + i + 1) % size) for i in range(0, size, 2)]
    return lax.ppermute(block, axis, pairs + [(b, a) for a, b in pairs])


def side_of(device):
    return 2 * lax.rem(device, 2) - 1


def start_all(copies):
    for copy in copies:
        copy.start()


def wait_all(copies):
    for copy in copies:
        copy.wait()


def in_hbm(*arrays):
    return [pltpu.with_memory_space_constraint(x, pltpu.HBM) for x in arrays]


def products(query, state):
    q_high = query.astype(BF16).astype(F32)
    both = jnp.concatenate([q_high, query - q_high], axis=0).astype(BF16)
    high = state.astype(BF16)
    low = (state - high.astype(F32)).astype(BF16)
    first = jnp.dot(both, high, preferred_element_type=F32)
    second = jnp.dot(both, low, preferred_element_type=F32)
    return first[:TILE] + first[TILE:] + second[:TILE]


def pick_kernel(shards, live, strides, place, shard_hbm, slot_hbm, projected, states, *refs):
    n_rows = len(strides)
    outs = refs[:n_rows]
    shard_ref, slot_ref, inputs, sems = refs[n_rows:]
    rows, dim = outs[-1].shape
    device = place[0]
    plan = [
        pltpu.make_async_copy(shard_hbm, shard_ref, sems.at[n_rows]),
        pltpu.make_async_copy(slot_hbm, slot_ref, sems.at[n_rows + 1]),
    ]
    load = pltpu.make_async_copy(projected, inputs, sems.at[n_rows + 2])
    start_all(plan)
    load.start()
    wait_all(plan)
    copies = []
    for n, stride in enumerate(strides):
        target = lax.rem(device + stride * side_of(device) + shards, shards)
        slot = jnp.int32(0)
        for row in range(live):
            mine = shard_ref[target * live + row] == device
            slot = jnp.where(mine, slot_ref[target * live + row], slot)
        copies.append(
            pltpu.make_async_copy(states.at[slot], outs[n].at[0:rows], sems.at[n])
        )
    start_all(copies)
    load.wait()
    tile_rows = rows // dim * TILE
    for n in range(2):
        outs[n][rows : rows + tile_rows] = jnp.zeros((tile_rows, dim), F32)
    for step in range(inputs.shape[0]):
        for row in range(live):
            query = jax.nn.silu(inputs[step, row].astype(F32))[0:1]
            for head in range(rows // dim):
                at = rows + head * TILE + step * live + row
                part = query[:, head * dim : (head + 1) * dim]
                for n in range(2):
                    outs[n][at : at + 1] = part
    wait_all(copies)


def pick(place, from_shard, from_slot, projected, states, shards, live, strides):
    rows, dim = states.shape[1:]
    tile_rows = rows // dim * TILE
    return pl.pallas_call(
        functools.partial(pick_kernel, shards, live, strides),
        out_shape=[jax.ShapeDtypeStruct((rows + tile_rows, dim), F32)] * 2
        + [jax.ShapeDtypeStruct((rows, dim), F32)] * (len(strides) - 2),
        in_specs=[SMEM] + [HBM] * 4,
        out_specs=[VMEM] * len(strides),
        scratch_shapes=[
            pltpu.SMEM(from_shard.shape, jnp.int32),
            pltpu.SMEM(from_slot.shape, jnp.int32),
            pltpu.VMEM(projected.shape, projected.dtype),
            pltpu.SemaphoreType.DMA((len(strides) + 3,)),
        ],
        compiler_params=pltpu.CompilerParams(vmem_limit_bytes=6 * MIB),
        name="pick_rows",
    )(place, *in_hbm(from_shard, from_slot, projected, states))


def relay_kernel(from_1, from_0, _, lead_1, lead_0, rest_1, rest_0):
    dim = from_1.shape[1]
    heads = rest_0.shape[0] // dim + EARLY
    rows, early = heads * dim, EARLY * dim
    tile_rows = heads * TILE
    for source, other, lead, rest in (
        (from_0, from_1, lead_1, rest_1),
        (from_1, from_0, lead_0, rest_0),
    ):
        for head in range(heads):
            part = slice(head * TILE, (head + 1) * TILE)
            query = other[rows + head * TILE : rows + (head + 1) * TILE]
            state = source[head * dim : (head + 1) * dim]
            lead[part] = products(query, state)
            if head < EARLY:
                lead[tile_rows + head * dim : tile_rows + (head + 1) * dim] = state
            else:
                rest[(head - EARLY) * dim : (head - EARLY + 1) * dim] = state


def relay(from_1, from_0, after, heads):
    dim = from_0.shape[1]
    lead = jax.ShapeDtypeStruct((heads * TILE + EARLY * dim, dim), F32)
    rest = jax.ShapeDtypeStruct(((heads - EARLY) * dim, dim), F32)
    return pl.pallas_call(
        relay_kernel,
        out_shape=[lead, lead, rest, rest],
        in_specs=[VMEM] * 3,
        out_specs=[VMEM] * 4,
        compiler_params=pltpu.CompilerParams(vmem_limit_bytes=6 * MIB),
        name="relay_rows",
    )(from_1, from_0, after)


def gap_of(row, shards, live, place, shard_ref):
    device = place[0]
    return lax.rem(device - shard_ref[device * live + row] + shards, shards)


def at_stride(gap, stride, shards, place):
    return gap == lax.rem(stride * side_of(place[0]) + shards, shards)


def prepare_kernel(
    live, place, slot_ref, projected, rate, gain, states,
    query, grown, base, gated, decay, made, here, outer, parts, sems,
):
    rows, dim = here.shape[1:]
    heads = rows // dim
    steps = projected.shape[0]
    copies = [
        pltpu.make_async_copy(
            states.at[slot_ref[place[0] * live + row]], here.at[row], sems.at[row]
        )
        for row in range(live)
    ]
    start_all(copies)
    parts[...] = jnp.zeros_like(parts)
    for step in range(steps):
        for row in range(live):
            block = projected[step, row].astype(F32)
            at = step * live + row
            for n in range(parts.shape[0]):
                parts[n, at : at + 1] = block[n : n + 1]
    queries, keys, values = (jax.nn.silu(parts[n]) for n in range(3))
    index = lax.broadcasted_iota(jnp.int32, queries.shape, 0)
    step_of = (index // live).astype(F32)
    rates = jnp.broadcast_to(rate[...], queries.shape)
    query[...] = queries
    gated[...] = jax.nn.sigmoid(parts[3]) * gain[...]
    grown[...] = jnp.exp(-rates * (step_of + 1.0))
    decay[...] = jnp.exp(-steps * rate[...])
    faded = keys * jnp.exp(-rates * jnp.maximum(steps - 1.0 - step_of, 0.0))
    later = lambda x, count: jnp.concatenate(
        [jnp.zeros((count, rows), F32), x[: TILE - count]], axis=0
    )
    total = jnp.zeros_like(queries)
    for lag in range(steps):
        key = later(keys, lag * live) if lag else keys
        value = later(values, lag * live) if lag else values
        product = queries * key
        match = jnp.concatenate(
            [
                jnp.broadcast_to(
                    jnp.sum(
                        product[:, head * dim : (head + 1) * dim], axis=1, keepdims=True
                    ),
                    (TILE, dim),
                )
                for head in range(heads)
            ],
            axis=1,
        )
        total = total + jnp.exp(-rates * float(lag)) * match * value
    base[...] = total

    def halves(x):
        high = x.astype(BF16).astype(F32)
        return high, x - high

    nothing = jnp.zeros_like(queries)
    v_high, v_low = halves(values)
    right = jnp.concatenate([v_high, v_high, v_low, nothing], axis=0).astype(BF16)
    for row in range(live):
        k_high, k_low = halves(jnp.where(lax.rem(index, live) == row, faded, 0.0))
        left = jnp.concatenate([k_high, k_low, k_high, nothing], axis=0).astype(BF16)
        for head in range(heads):
            span = slice(head * dim, (head + 1) * dim)
            outer[row, span] = lax.dot_general(
                left[:, span],
                right[:, span],
                (((0,), (0,)), ((), ())),
                preferred_element_type=F32,
            )
    wait_all(copies)
    for row in range(live):
        for head in range(heads):
            span = slice(head * dim, (head + 1) * dim)
            made[row, head * TILE : (head + 1) * TILE] = products(
                queries[:, span], here[row, span]
            )


def prepare(place, from_slot, projected, rate, gain, states, live):
    rows, dim = states.shape[1:]
    tile = jax.ShapeDtypeStruct((TILE, rows), F32)
    whole = jax.ShapeDtypeStruct((live, rows, dim), F32)
    return pl.pallas_call(
        functools.partial(prepare_kernel, live),
        out_shape=[tile] * 4
        + [
            jax.ShapeDtypeStruct((1, rows), F32),
            jax.ShapeDtypeStruct((live, rows // dim * TILE, dim), F32),
            whole,
            whole,
        ],
        in_specs=[SMEM] * 2 + [VMEM] * 3 + [HBM],
        out_specs=[VMEM] * 8,
        scratch_shapes=[
            pltpu.VMEM((projected.shape[2], TILE, rows), F32),
            pltpu.SemaphoreType.DMA((live,)),
        ],
        compiler_params=pltpu.CompilerParams(vmem_limit_bytes=6 * MIB),
        name="prepare_rows",
    )(place, from_slot, projected, rate, gain, *in_hbm(states))


def diagonal(dim):
    row = lax.broadcasted_iota(jnp.int32, (TILE, dim), 0)
    return row == lax.broadcasted_iota(jnp.int32, (TILE, dim), 1)


def raw_kernel(
    shards, live, place, shard_ref, lead_1, lead_0, near_1, near_0,
    local, query, grown, base, raw, sums, made,
):
    rows, dim = near_0.shape
    heads = rows // dim
    tile_rows = heads * TILE
    for row in range(live):
        made[row] = local[row]
    for n, near in enumerate((near_1, near_0)):
        for head in range(heads):
            span = slice(head * dim, (head + 1) * dim)
            made[live + n, head * TILE : (head + 1) * TILE] = products(
                query[:, span], near[span]
            )
    for n, lead in enumerate((lead_1, lead_0)):
        made[live + 2 + n] = lead[0:tile_rows]
    picks = []
    for row in range(live):
        gap = gap_of(row, shards, live, place, shard_ref)
        index = jnp.int32(row)
        for n, stride in enumerate((-1, 1, -2, 2)):
            index = jnp.where(at_stride(gap, stride, shards, place), live + n, index)
        picks.append(index)
    which = lax.rem(lax.broadcasted_iota(jnp.int32, (TILE, dim), 0), live)
    total = jnp.zeros((TILE, dim), F32)
    for head in range(heads):
        span = slice(head * dim, (head + 1) * dim)
        part = slice(head * TILE, (head + 1) * TILE)
        tile = made[picks[0], part]
        for row in range(1, live):
            tile = jnp.where(which == row, made[picks[row], part], tile)
        tile = tile * grown[:, span] + base[:, span]
        raw[:, span] = tile
        total = total + tile * tile
    total = jnp.broadcast_to(jnp.sum(total, axis=1, keepdims=True), (TILE, dim))
    total = jnp.sum(jnp.where(diagonal(dim), total, 0.0), axis=0, keepdims=True)
    for peer in range(sums.shape[0]):
        sums[peer] = total


def raw_of(place, from_shard, arrived, small, shards, live, group):
    rows, dim = arrived[-1].shape
    return pl.pallas_call(
        functools.partial(raw_kernel, shards, live),
        out_shape=[
            jax.ShapeDtypeStruct((TILE, rows), F32),
            jax.ShapeDtypeStruct((group, 1, dim), F32),
        ],
        in_specs=[SMEM] * 2 + [VMEM] * (len(arrived) + len(small)),
        out_specs=[VMEM] * 2,
        scratch_shapes=[pltpu.VMEM((live + 4, rows // dim * TILE, dim), F32)],
        compiler_params=pltpu.CompilerParams(vmem_limit_bytes=6 * MIB),
        cost_estimate=pl.CostEstimate(flops=10**12, bytes_accessed=MIB, transcendentals=0),
        name="raw_rows",
    )(place, from_shard, *arrived, *small)


def final_kernel(
    shards, live, place, shard_ref, here, near_1, near_0, lead_1, lead_0,
    rest_1, rest_0, outer, decay, final, made, sems,
):
    rows, dim = here.shape[1:]
    heads = rows // dim
    tile_rows = heads * TILE
    copies = []
    for row in range(live):
        gap = gap_of(row, shards, live, place, shard_ref)

        def at(ref, head):
            return lambda: ref[head * dim : (head + 1) * dim]

        def relayed(lead, rest, head):
            if head < EARLY:
                start = tile_rows + head * dim
                return lambda: lead[start : start + dim]
            return at(rest, head - EARLY)

        for half in range(2):
            span = range(half * heads // 2, (half + 1) * heads // 2)
            sources = [
                (gap == 0, [at(here.at[row], head) for head in span]),
                (at_stride(gap, 1, shards, place), [at(near_0, head) for head in span]),
                (at_stride(gap, -1, shards, place), [at(near_1, head) for head in span]),
                (
                    at_stride(gap, 2, shards, place),
                    [relayed(lead_0, rest_0, head) for head in span],
                ),
                (
                    at_stride(gap, -2, shards, place),
                    [relayed(lead_1, rest_1, head) for head in span],
                ),
            ]
            for found, states in sources:

                @pl.when(found)
                def _():
                    for head, state in zip(span, states):
                        block = slice(head * dim, (head + 1) * dim)
                        made[row, block] = decay[:, block] * state() + outer[row, block]

            block = slice(span.start * dim, span.stop * dim)
            copy = pltpu.make_async_copy(
                made.at[row, block], final.at[row, block], sems.at[row, half]
            )
            copy.start()
            copies.append(copy)
    wait_all(copies)


def final_of(place, from_shard, sources, shards, live):
    rows, dim = sources[0].shape[1:]
    return pl.pallas_call(
        functools.partial(final_kernel, shards, live),
        out_shape=jax.ShapeDtypeStruct((live, rows, dim), F32),
        in_specs=[SMEM] * 2 + [VMEM] * len(sources),
        out_specs=pl.BlockSpec(memory_space=pl.ANY),
        scratch_shapes=[
            pltpu.VMEM((live, rows, dim), F32),
            pltpu.SemaphoreType.DMA((live, 2)),
        ],
        compiler_params=pltpu.CompilerParams(vmem_limit_bytes=9 * MIB),
        name="final_rows",
    )(place, from_shard, *sources)


def attend_kernel(live, features, totals, raw, gated, attended):
    dim = totals.shape[2]
    total = totals[0]
    for peer in range(1, totals.shape[0]):
        total = total + totals[peer]
    total = jnp.where(diagonal(dim), jnp.broadcast_to(total, (TILE, dim)), 0.0)
    total = jnp.sum(total, axis=1, keepdims=True)
    scale = jnp.broadcast_to(lax.rsqrt(total / features + EPS), raw.shape)
    tile = raw[...] * scale * gated[...]
    for step in range(attended.shape[0]):
        attended[step] = tile[step * live : (step + 1) * live].astype(BF16)


def attend(totals, raw, gated, live, steps, features):
    return pl.pallas_call(
        functools.partial(attend_kernel, live, features),
        out_shape=jax.ShapeDtypeStruct((steps, live, raw.shape[1]), BF16),
        in_specs=[VMEM] * 3,
        out_specs=VMEM,
        compiler_params=pltpu.CompilerParams(vmem_limit_bytes=4 * MIB),
        name="attend_rows",
    )(totals, raw, gated)


def on_device(states, from_shard, from_slot, projected, decay_rate, norm_gain):
    shards, group = lax.axis_size("dp"), lax.axis_size("tensor")
    steps, live = projected.shape[:2]
    slots, heads, dim = states.shape[:3]
    width = heads * dim
    place = lax.axis_index("dp").astype(jnp.int32).reshape(1)
    states = states.reshape(slots, width, dim)

    rate = jnp.repeat(decay_rate, dim).reshape(1, width)
    gain = norm_gain.reshape(1, width)
    query, grown, base, gated, decay, local, here, outer = prepare(
        place, from_slot, projected, rate, gain, states, live
    )

    rows = pick(
        place, from_shard, from_slot, projected, states, shards, live, (-2, 2, -1, 1)
    )
    half_1, half_0 = swapped(rows[1], "dp", 1), swapped(rows[0], "dp", 0)
    near_1, near_0 = swapped(rows[3], "dp", 1), swapped(rows[2], "dp", 0)
    sent = relay(half_1, half_0, decay, heads)
    lead_1, lead_0 = swapped(sent[0], "dp", 1), swapped(sent[1], "dp", 0)
    rest_1, rest_0 = swapped(sent[2], "dp", 1), swapped(sent[3], "dp", 0)

    raw, sums = raw_of(
        place, from_shard, (lead_1, lead_0, near_1, near_0),
        (local, query, grown, base), shards, live, group,
    )
    totals = lax.all_to_all(sums, "tensor", 0, 0)
    final = final_of(
        place, from_shard,
        (here, near_1, near_0, lead_1, lead_0, rest_1, rest_0, outer, decay),
        shards, live,
    )
    attended = attend(totals, raw, gated, live, steps, width * group)
    return attended, final.reshape(live, heads, dim, dim)


def solution(mesh):
    return jax.shard_map(
        on_device,
        mesh=mesh,
        in_specs=(
            P("dp", "tensor", None, None),
            P(),
            P(),
            P(None, "dp", None, "tensor"),
            P("tensor"),
            P("tensor"),
        ),
        out_specs=(P(None, "dp", "tensor"), P("dp", "tensor", None, None)),
        check_vma=False,
    )
```

```python
import functools
import jax
import jax.numpy as jnp
from jax import lax
from jax.experimental import pallas as pl
from jax.experimental.pallas import tpu as pltpu
from jax.sharding import PartitionSpec as P

EPS = 1e-05
F32 = jnp.float32
BF16 = jnp.bfloat16
EARLY = 2
TILE = 8
MIB = 1024 * 1024
SMEM = pl.BlockSpec(memory_space=pltpu.SMEM)
VMEM = pl.BlockSpec(memory_space=pltpu.VMEM)
HBM = pl.BlockSpec(memory_space=pltpu.HBM)


def swapped(block, axis, first):
    size = lax.axis_size(axis)
    pairs = [((first + i) % size, (first + i + 1) % size) for i in range(0, size, 2)]
    return lax.ppermute(block, axis, pairs + [(b, a) for a, b in pairs])


def side_of(device):
    return 2 * lax.rem(device, 2) - 1


def start_all(copies):
    for copy in copies:
        copy.start()


def wait_all(copies):
    for copy in copies:
        copy.wait()


def in_hbm(*arrays):
    return [pltpu.with_memory_space_constraint(x, pltpu.HBM) for x in arrays]


def products(query, state):
    q_high = query.astype(BF16).astype(F32)
    both = jnp.concatenate([q_high, query - q_high], axis=0).astype(BF16)
    high = state.astype(BF16)
    low = (state - high.astype(F32)).astype(BF16)
    first = jnp.dot(both, high, preferred_element_type=F32)
    second = jnp.dot(both, low, preferred_element_type=F32)
    return first[:TILE] + first[TILE:] + second[:TILE]


def pick_kernel(shards, live, strides, place, shard_hbm, slot_hbm, projected, states, *refs):
    n_rows = len(strides)
    outs = refs[:n_rows]
    shard_ref, slot_ref, inputs, sems = refs[n_rows:]
    rows, dim = outs[-1].shape
    device = place[0]
    plan = [
        pltpu.make_async_copy(shard_hbm, shard_ref, sems.at[n_rows]),
        pltpu.make_async_copy(slot_hbm, slot_ref, sems.at[n_rows + 1]),
    ]
    load = pltpu.make_async_copy(projected, inputs, sems.at[n_rows + 2])
    start_all(plan)
    load.start()
    wait_all(plan)
    copies = []
    for n, stride in enumerate(strides):
        target = lax.rem(device + stride * side_of(device) + shards, shards)
        slot = jnp.int32(0)
        for row in range(live):
            mine = shard_ref[target * live + row] == device
            slot = jnp.where(mine, slot_ref[target * live + row], slot)
        copies.append(
            pltpu.make_async_copy(states.at[slot], outs[n].at[0:rows], sems.at[n])
        )
    start_all(copies)
    load.wait()
    tile_rows = rows // dim * TILE
    for n in range(2):
        outs[n][rows : rows + tile_rows] = jnp.zeros((tile_rows, dim), F32)
    for step in range(inputs.shape[0]):
        for row in range(live):
            query = jax.nn.silu(inputs[step, row].astype(F32))[0:1]
            for head in range(rows // dim):
                at = rows + head * TILE + step * live + row
                part = query[:, head * dim : (head + 1) * dim]
                for n in range(2):
                    outs[n][at : at + 1] = part
    wait_all(copies)


def pick(place, from_shard, from_slot, projected, states, shards, live, strides):
    rows, dim = states.shape[1:]
    tile_rows = rows // dim * TILE
    return pl.pallas_call(
        functools.partial(pick_kernel, shards, live, strides),
        out_shape=[jax.ShapeDtypeStruct((rows + tile_rows, dim), F32)] * 2
        + [jax.ShapeDtypeStruct((rows, dim), F32)] * (len(strides) - 2),
        in_specs=[SMEM] + [HBM] * 4,
        out_specs=[VMEM] * len(strides),
        scratch_shapes=[
            pltpu.SMEM(from_shard.shape, jnp.int32),
            pltpu.SMEM(from_slot.shape, jnp.int32),
            pltpu.VMEM(projected.shape, projected.dtype),
            pltpu.SemaphoreType.DMA((len(strides) + 3,)),
        ],
        compiler_params=pltpu.CompilerParams(vmem_limit_bytes=6 * MIB),
        name="pick_rows",
    )(place, *in_hbm(from_shard, from_slot, projected, states))


def relay_kernel(from_1, from_0, _, lead_1, lead_0, rest_1, rest_0):
    dim = from_1.shape[1]
    heads = rest_0.shape[0] // dim + EARLY
    rows, early = heads * dim, EARLY * dim
    tile_rows = heads * TILE
    for source, other, lead, rest in (
        (from_0, from_1, lead_1, rest_1),
        (from_1, from_0, lead_0, rest_0),
    ):
        for head in range(heads):
            part = slice(head * TILE, (head + 1) * TILE)
            query = other[rows + head * TILE : rows + (head + 1) * TILE]
            state = source[head * dim : (head + 1) * dim]
            lead[part] = products(query, state)
            if head < EARLY:
                lead[tile_rows + head * dim : tile_rows + (head + 1) * dim] = state
            else:
                rest[(head - EARLY) * dim : (head - EARLY + 1) * dim] = state


def relay(from_1, from_0, after, heads):
    dim = from_0.shape[1]
    lead = jax.ShapeDtypeStruct((heads * TILE + EARLY * dim, dim), F32)
    rest = jax.ShapeDtypeStruct(((heads - EARLY) * dim, dim), F32)
    return pl.pallas_call(
        relay_kernel,
        out_shape=[lead, lead, rest, rest],
        in_specs=[VMEM] * 3,
        out_specs=[VMEM] * 4,
        compiler_params=pltpu.CompilerParams(vmem_limit_bytes=6 * MIB),
        name="relay_rows",
    )(from_1, from_0, after)


def gap_of(row, shards, live, place, shard_ref):
    device = place[0]
    return lax.rem(device - shard_ref[device * live + row] + shards, shards)


def at_stride(gap, stride, shards, place):
    return gap == lax.rem(stride * side_of(place[0]) + shards, shards)


def prepare_kernel(
    live, place, slot_ref, projected, rate, gain, states,
    query, grown, base, gated, decay, made, here, outer, parts, sems,
):
    rows, dim = here.shape[1:]
    heads = rows // dim
    steps = projected.shape[0]
    copies = [
        pltpu.make_async_copy(
            states.at[slot_ref[place[0] * live + row]], here.at[row], sems.at[row]
        )
        for row in range(live)
    ]
    start_all(copies)
    parts[...] = jnp.zeros_like(parts)
    for step in range(steps):
        for row in range(live):
            block = projected[step, row].astype(F32)
            at = step * live + row
            for n in range(parts.shape[0]):
                parts[n, at : at + 1] = block[n : n + 1]
    queries, keys, values = (jax.nn.silu(parts[n]) for n in range(3))
    index = lax.broadcasted_iota(jnp.int32, queries.shape, 0)
    step_of = (index // live).astype(F32)
    rates = jnp.broadcast_to(rate[...], queries.shape)
    query[...] = queries
    gated[...] = jax.nn.sigmoid(parts[3]) * gain[...]
    grown[...] = jnp.exp(-rates * (step_of + 1.0))
    decay[...] = jnp.exp(-steps * rate[...])
    faded = keys * jnp.exp(-rates * jnp.maximum(steps - 1.0 - step_of, 0.0))
    later = lambda x, count: jnp.concatenate(
        [jnp.zeros((count, rows), F32), x[: TILE - count]], axis=0
    )
    total = jnp.zeros_like(queries)
    for lag in range(steps):
        key = later(keys, lag * live) if lag else keys
        value = later(values, lag * live) if lag else values
        product = queries * key
        match = jnp.concatenate(
            [
                jnp.broadcast_to(
                    jnp.sum(
                        product[:, head * dim : (head + 1) * dim], axis=1, keepdims=True
                    ),
                    (TILE, dim),
                )
                for head in range(heads)
            ],
            axis=1,
        )
        total = total + jnp.exp(-rates * float(lag)) * match * value
    base[...] = total

    def halves(x):
        high = x.astype(BF16).astype(F32)
        return high, x - high

    nothing = jnp.zeros_like(queries)
    v_high, v_low = halves(values)
    right = jnp.concatenate([v_high, v_high, v_low, nothing], axis=0).astype(BF16)
    for row in range(live):
        k_high, k_low = halves(jnp.where(lax.rem(index, live) == row, faded, 0.0))
        left = jnp.concatenate([k_high, k_low, k_high, nothing], axis=0).astype(BF16)
        for head in range(heads):
            span = slice(head * dim, (head + 1) * dim)
            outer[row, span] = lax.dot_general(
                left[:, span],
                right[:, span],
                (((0,), (0,)), ((), ())),
                preferred_element_type=F32,
            )
    wait_all(copies)
    for row in range(live):
        for head in range(heads):
            span = slice(head * dim, (head + 1) * dim)
            made[row, head * TILE : (head + 1) * TILE] = products(
                queries[:, span], here[row, span]
            )


def prepare(place, from_slot, projected, rate, gain, states, live):
    rows, dim = states.shape[1:]
    tile = jax.ShapeDtypeStruct((TILE, rows), F32)
    whole = jax.ShapeDtypeStruct((live, rows, dim), F32)
    return pl.pallas_call(
        functools.partial(prepare_kernel, live),
        out_shape=[tile] * 4
        + [
            jax.ShapeDtypeStruct((1, rows), F32),
            jax.ShapeDtypeStruct((live, rows // dim * TILE, dim), F32),
            whole,
            whole,
        ],
        in_specs=[SMEM] * 2 + [VMEM] * 3 + [HBM],
        out_specs=[VMEM] * 8,
        scratch_shapes=[
            pltpu.VMEM((projected.shape[2], TILE, rows), F32),
            pltpu.SemaphoreType.DMA((live,)),
        ],
        compiler_params=pltpu.CompilerParams(vmem_limit_bytes=6 * MIB),
        name="prepare_rows",
    )(place, from_slot, projected, rate, gain, *in_hbm(states))


def diagonal(dim):
    row = lax.broadcasted_iota(jnp.int32, (TILE, dim), 0)
    return row == lax.broadcasted_iota(jnp.int32, (TILE, dim), 1)


def raw_kernel(
    shards, live, place, shard_ref, lead_1, lead_0, near_0, near_1,
    local, query, grown, base, raw, sums, made, tiles, sem,
):
    rows, dim = near_0.shape
    heads = rows // dim
    tile_rows = heads * TILE
    for row in range(live):
        made[row] = local[row]
    for n, near in enumerate((near_1, near_0)):
        for head in range(heads):
            span = slice(head * dim, (head + 1) * dim)
            made[live + n, head * TILE : (head + 1) * TILE] = products(
                query[:, span], near[span]
            )
    for n, lead in enumerate((lead_1, lead_0)):
        made[live + 2 + n] = lead[0:tile_rows]
    picks = []
    for row in range(live):
        gap = gap_of(row, shards, live, place, shard_ref)
        index = jnp.int32(row)
        for n, stride in enumerate((-1, 1, -2, 2)):
            index = jnp.where(at_stride(gap, stride, shards, place), live + n, index)
        picks.append(index)
    which = lax.rem(lax.broadcasted_iota(jnp.int32, (TILE, dim), 0), live)
    total = jnp.zeros((TILE, dim), F32)
    for head in range(heads):
        span = slice(head * dim, (head + 1) * dim)
        part = slice(head * TILE, (head + 1) * TILE)
        tile = made[picks[0], part]
        for row in range(1, live):
            tile = jnp.where(which == row, made[picks[row], part], tile)
        tile = tile * grown[:, span] + base[:, span]
        raw[:, span] = tile
        total = total + tile * tile
    total = jnp.broadcast_to(jnp.sum(total, axis=1, keepdims=True), (TILE, dim))
    total = jnp.sum(jnp.where(diagonal(dim), total, 0.0), axis=0, keepdims=True)
    for peer in range(sums.shape[0]):
        tiles[peer] = total
    copy = pltpu.make_async_copy(tiles, sums, sem)
    copy.start()
    copy.wait()


def raw_of(place, from_shard, arrived, small, shards, live, group):
    rows, dim = arrived[-1].shape
    return pl.pallas_call(
        functools.partial(raw_kernel, shards, live),
        out_shape=[
            jax.ShapeDtypeStruct((TILE, rows), F32),
            jax.ShapeDtypeStruct((group, 1, dim), F32),
        ],
        in_specs=[SMEM] * 2 + [VMEM] * (len(arrived) + len(small)),
        out_specs=[VMEM, HBM],
        scratch_shapes=[
            pltpu.VMEM((live + 4, rows // dim * TILE, dim), F32),
            pltpu.VMEM((group, 1, dim), F32),
            pltpu.SemaphoreType.DMA(()),
        ],
        compiler_params=pltpu.CompilerParams(vmem_limit_bytes=6 * MIB),
        cost_estimate=pl.CostEstimate(flops=10**12, bytes_accessed=MIB, transcendentals=0),
        name="raw_rows",
    )(place, from_shard, *arrived, *small)


def final_kernel(
    shards, live, place, shard_ref, here, lead_1, lead_0, near_0, near_1,
    rest_0, rest_1, outer, decay, final, token, made, sems,
):
    rows, dim = here.shape[1:]
    token[...] = jnp.zeros_like(token)
    heads = rows // dim
    tile_rows = heads * TILE
    copies = []
    for row in range(live):
        gap = gap_of(row, shards, live, place, shard_ref)

        def at(ref, head):
            return lambda: ref[head * dim : (head + 1) * dim]

        def relayed(lead, rest, head):
            if head < EARLY:
                start = tile_rows + head * dim
                return lambda: lead[start : start + dim]
            return at(rest, head - EARLY)

        for half in range(2):
            span = range(half * heads // 2, (half + 1) * heads // 2)
            sources = [
                (gap == 0, [at(here.at[row], head) for head in span]),
                (at_stride(gap, 1, shards, place), [at(near_0, head) for head in span]),
                (at_stride(gap, -1, shards, place), [at(near_1, head) for head in span]),
                (
                    at_stride(gap, 2, shards, place),
                    [relayed(lead_0, rest_0, head) for head in span],
                ),
                (
                    at_stride(gap, -2, shards, place),
                    [relayed(lead_1, rest_1, head) for head in span],
                ),
            ]
            for found, states in sources:

                @pl.when(found)
                def _():
                    for head, state in zip(span, states):
                        block = slice(head * dim, (head + 1) * dim)
                        made[row, block] = decay[:, block] * state() + outer[row, block]

            block = slice(span.start * dim, span.stop * dim)
            copy = pltpu.make_async_copy(
                made.at[row, block], final.at[row, block], sems.at[row, half]
            )
            copy.start()
            copies.append(copy)
    wait_all(copies)


def final_of(place, from_shard, sources, shards, live):
    rows, dim = sources[0].shape[1:]
    return pl.pallas_call(
        functools.partial(final_kernel, shards, live),
        out_shape=[
            jax.ShapeDtypeStruct((live, rows, dim), F32),
            jax.ShapeDtypeStruct((TILE, dim), F32),
        ],
        in_specs=[SMEM] * 2 + [VMEM] * len(sources),
        out_specs=[pl.BlockSpec(memory_space=pl.ANY), VMEM],
        scratch_shapes=[
            pltpu.VMEM((live, rows, dim), F32),
            pltpu.SemaphoreType.DMA((live, 2)),
        ],
        compiler_params=pltpu.CompilerParams(vmem_limit_bytes=9 * MIB),
        cost_estimate=pl.CostEstimate(flops=10**10, bytes_accessed=MIB, transcendentals=0),
        name="final_rows",
    )(place, from_shard, *sources)


def attend_kernel(live, features, totals, raw, gated, _, attended):
    dim = totals.shape[2]
    total = totals[0]
    for peer in range(1, totals.shape[0]):
        total = total + totals[peer]
    total = jnp.where(diagonal(dim), jnp.broadcast_to(total, (TILE, dim)), 0.0)
    total = jnp.sum(total, axis=1, keepdims=True)
    scale = jnp.broadcast_to(lax.rsqrt(total / features + EPS), raw.shape)
    tile = raw[...] * scale * gated[...]
    for step in range(attended.shape[0]):
        attended[step] = tile[step * live : (step + 1) * live].astype(BF16)


def attend(totals, raw, gated, after, live, steps, features):
    return pl.pallas_call(
        functools.partial(attend_kernel, live, features),
        out_shape=jax.ShapeDtypeStruct((steps, live, raw.shape[1]), BF16),
        in_specs=[VMEM] * 4,
        out_specs=VMEM,
        compiler_params=pltpu.CompilerParams(vmem_limit_bytes=4 * MIB),
        name="attend_rows",
    )(totals, raw, gated, after)


def on_device(states, from_shard, from_slot, projected, decay_rate, norm_gain):
    shards, group = lax.axis_size("dp"), lax.axis_size("tensor")
    steps, live = projected.shape[:2]
    slots, heads, dim = states.shape[:3]
    width = heads * dim
    place = lax.axis_index("dp").astype(jnp.int32).reshape(1)
    states = states.reshape(slots, width, dim)

    rate = jnp.repeat(decay_rate, dim).reshape(1, width)
    gain = norm_gain.reshape(1, width)
    query, grown, base, gated, decay, local, here, outer = prepare(
        place, from_slot, projected, rate, gain, states, live
    )

    rows = pick(
        place, from_shard, from_slot, projected, states, shards, live, (-2, 2, -1, 1)
    )
    half_1, half_0 = swapped(rows[1], "dp", 1), swapped(rows[0], "dp", 0)
    near_1, near_0 = swapped(rows[3], "dp", 1), swapped(rows[2], "dp", 0)
    sent = relay(half_1, half_0, decay, heads)
    lead_1, lead_0 = swapped(sent[0], "dp", 1), swapped(sent[1], "dp", 0)
    rest_1, rest_0 = swapped(sent[2], "dp", 1), swapped(sent[3], "dp", 0)

    raw, sums = raw_of(
        place, from_shard, (lead_1, lead_0, near_0, near_1),
        (local, query, grown, base), shards, live, group,
    )
    totals = lax.all_to_all(sums, "tensor", 0, 0)
    final, token = final_of(
        place, from_shard,
        (here, lead_1, lead_0, near_0, near_1, rest_0, rest_1, outer, decay),
        shards, live,
    )
    attended = attend(totals, raw, gated, token, live, steps, width * group)
    return attended, final.reshape(live, heads, dim, dim)


def solution(mesh):
    return jax.shard_map(
        on_device,
        mesh=mesh,
        in_specs=(
            P("dp", "tensor", None, None),
            P(),
            P(),
            P(None, "dp", None, "tensor"),
            P("tensor"),
            P("tensor"),
        ),
        out_specs=(P(None, "dp", "tensor"), P("dp", "tensor", None, None)),
        check_vma=False,
    )
```

```python
import functools
import jax
import jax.numpy as jnp
from jax import lax
from jax.experimental import pallas as pl
from jax.experimental.pallas import tpu as pltpu
from jax.sharding import PartitionSpec as P

EPS = 1e-05
F32 = jnp.float32
BF16 = jnp.bfloat16
EARLY = 3
TILE = 8
MIB = 1024 * 1024
SMEM = pl.BlockSpec(memory_space=pltpu.SMEM)
VMEM = pl.BlockSpec(memory_space=pltpu.VMEM)
HBM = pl.BlockSpec(memory_space=pltpu.HBM)


def swapped(block, axis, first):
    size = lax.axis_size(axis)
    pairs = [((first + i) % size, (first + i + 1) % size) for i in range(0, size, 2)]
    return lax.ppermute(block, axis, pairs + [(b, a) for a, b in pairs])


def side_of(device):
    return 2 * lax.rem(device, 2) - 1


def start_all(copies):
    for copy in copies:
        copy.start()


def wait_all(copies):
    for copy in copies:
        copy.wait()


def in_hbm(*arrays):
    return [pltpu.with_memory_space_constraint(x, pltpu.HBM) for x in arrays]


def products(query, state):
    q_high = query.astype(BF16).astype(F32)
    both = jnp.concatenate([q_high, query - q_high], axis=0).astype(BF16)
    high = state.astype(BF16)
    low = (state - high.astype(F32)).astype(BF16)
    first = jnp.dot(both, high, preferred_element_type=F32)
    second = jnp.dot(both, low, preferred_element_type=F32)
    return first[:TILE] + first[TILE:] + second[:TILE]


def pick_kernel(shards, live, strides, place, shard_hbm, slot_hbm, projected, states, *refs):
    n_rows = len(strides)
    outs = refs[:n_rows]
    shard_ref, slot_ref, inputs, sems = refs[n_rows:]
    rows, dim = outs[-1].shape
    device = place[0]
    plan = [
        pltpu.make_async_copy(shard_hbm, shard_ref, sems.at[n_rows]),
        pltpu.make_async_copy(slot_hbm, slot_ref, sems.at[n_rows + 1]),
    ]
    load = pltpu.make_async_copy(projected, inputs, sems.at[n_rows + 2])
    start_all(plan)
    load.start()
    wait_all(plan)
    copies = []
    for n, stride in enumerate(strides):
        target = lax.rem(device + stride * side_of(device) + shards, shards)
        slot = jnp.int32(0)
        for row in range(live):
            mine = shard_ref[target * live + row] == device
            slot = jnp.where(mine, slot_ref[target * live + row], slot)
        copies.append(
            pltpu.make_async_copy(states.at[slot], outs[n].at[0:rows], sems.at[n])
        )
    start_all(copies)
    load.wait()
    tile_rows = rows // dim * TILE
    for n in range(2):
        outs[n][rows : rows + tile_rows] = jnp.zeros((tile_rows, dim), F32)
    for step in range(inputs.shape[0]):
        for row in range(live):
            query = jax.nn.silu(inputs[step, row].astype(F32))[0:1]
            for head in range(rows // dim):
                at = rows + head * TILE + step * live + row
                part = query[:, head * dim : (head + 1) * dim]
                for n in range(2):
                    outs[n][at : at + 1] = part
    wait_all(copies)


def pick(place, from_shard, from_slot, projected, states, shards, live, strides):
    rows, dim = states.shape[1:]
    tile_rows = rows // dim * TILE
    return pl.pallas_call(
        functools.partial(pick_kernel, shards, live, strides),
        out_shape=[jax.ShapeDtypeStruct((rows + tile_rows, dim), F32)] * 2
        + [jax.ShapeDtypeStruct((rows, dim), F32)] * (len(strides) - 2),
        in_specs=[SMEM] + [HBM] * 4,
        out_specs=[VMEM] * len(strides),
        scratch_shapes=[
            pltpu.SMEM(from_shard.shape, jnp.int32),
            pltpu.SMEM(from_slot.shape, jnp.int32),
            pltpu.VMEM(projected.shape, projected.dtype),
            pltpu.SemaphoreType.DMA((len(strides) + 3,)),
        ],
        compiler_params=pltpu.CompilerParams(vmem_limit_bytes=6 * MIB),
        name="pick_rows",
    )(place, *in_hbm(from_shard, from_slot, projected, states))


def relay_kernel(from_0, from_1, _, lead_1, lead_0, rest_1, rest_0):
    dim = from_1.shape[1]
    heads = rest_0.shape[0] // dim + EARLY
    rows, early = heads * dim, EARLY * dim
    tile_rows = heads * TILE
    for source, other, lead, rest in (
        (from_0, from_1, lead_1, rest_1),
        (from_1, from_0, lead_0, rest_0),
    ):
        for head in range(heads):
            part = slice(head * TILE, (head + 1) * TILE)
            query = other[rows + head * TILE : rows + (head + 1) * TILE]
            state = source[head * dim : (head + 1) * dim]
            lead[part] = products(query, state)
            if head < EARLY:
                lead[tile_rows + head * dim : tile_rows + (head + 1) * dim] = state
            else:
                rest[(head - EARLY) * dim : (head - EARLY + 1) * dim] = state


def relay(from_0, from_1, after, heads):
    dim = from_0.shape[1]
    lead = jax.ShapeDtypeStruct((heads * TILE + EARLY * dim, dim), F32)
    rest = jax.ShapeDtypeStruct(((heads - EARLY) * dim, dim), F32)
    return pl.pallas_call(
        relay_kernel,
        out_shape=[lead, lead, rest, rest],
        in_specs=[VMEM] * 3,
        out_specs=[VMEM] * 4,
        compiler_params=pltpu.CompilerParams(vmem_limit_bytes=6 * MIB),
        name="relay_rows",
    )(from_0, from_1, after)


def gap_of(row, shards, live, place, shard_ref):
    device = place[0]
    return lax.rem(device - shard_ref[device * live + row] + shards, shards)


def at_stride(gap, stride, shards, place):
    return gap == lax.rem(stride * side_of(place[0]) + shards, shards)


def prepare_kernel(
    live, place, slot_ref, projected, rate, gain, states,
    query, grown, base, gated, decay, made, here, outer, parts, sems,
):
    rows, dim = here.shape[1:]
    heads = rows // dim
    steps = projected.shape[0]
    copies = [
        pltpu.make_async_copy(
            states.at[slot_ref[place[0] * live + row]], here.at[row], sems.at[row]
        )
        for row in range(live)
    ]
    start_all(copies)
    parts[...] = jnp.zeros_like(parts)
    for step in range(steps):
        for row in range(live):
            block = projected[step, row].astype(F32)
            at = step * live + row
            for n in range(parts.shape[0]):
                parts[n, at : at + 1] = block[n : n + 1]
    queries, keys, values = (jax.nn.silu(parts[n]) for n in range(3))
    index = lax.broadcasted_iota(jnp.int32, queries.shape, 0)
    step_of = (index // live).astype(F32)
    rates = jnp.broadcast_to(rate[...], queries.shape)
    query[...] = queries
    gated[...] = jax.nn.sigmoid(parts[3]) * gain[...]
    grown[...] = jnp.exp(-rates * (step_of + 1.0))
    decay[...] = jnp.exp(-steps * rate[...])
    faded = keys * jnp.exp(-rates * jnp.maximum(steps - 1.0 - step_of, 0.0))
    later = lambda x, count: jnp.concatenate(
        [jnp.zeros((count, rows), F32), x[: TILE - count]], axis=0
    )
    total = jnp.zeros_like(queries)
    for lag in range(steps):
        key = later(keys, lag * live) if lag else keys
        value = later(values, lag * live) if lag else values
        product = queries * key
        match = jnp.concatenate(
            [
                jnp.broadcast_to(
                    jnp.sum(
                        product[:, head * dim : (head + 1) * dim], axis=1, keepdims=True
                    ),
                    (TILE, dim),
                )
                for head in range(heads)
            ],
            axis=1,
        )
        total = total + jnp.exp(-rates * float(lag)) * match * value
    base[...] = total

    def halves(x):
        high = x.astype(BF16).astype(F32)
        return high, x - high

    nothing = jnp.zeros_like(queries)
    v_high, v_low = halves(values)
    right = jnp.concatenate([v_high, v_high, v_low, nothing], axis=0).astype(BF16)
    for row in range(live):
        k_high, k_low = halves(jnp.where(lax.rem(index, live) == row, faded, 0.0))
        left = jnp.concatenate([k_high, k_low, k_high, nothing], axis=0).astype(BF16)
        for head in range(heads):
            span = slice(head * dim, (head + 1) * dim)
            outer[row, span] = lax.dot_general(
                left[:, span],
                right[:, span],
                (((0,), (0,)), ((), ())),
                preferred_element_type=F32,
            )
    wait_all(copies)
    for row in range(live):
        for head in range(heads):
            span = slice(head * dim, (head + 1) * dim)
            made[row, head * TILE : (head + 1) * TILE] = products(
                queries[:, span], here[row, span]
            )


def prepare(place, from_slot, projected, rate, gain, states, live):
    rows, dim = states.shape[1:]
    tile = jax.ShapeDtypeStruct((TILE, rows), F32)
    whole = jax.ShapeDtypeStruct((live, rows, dim), F32)
    return pl.pallas_call(
        functools.partial(prepare_kernel, live),
        out_shape=[tile] * 4
        + [
            jax.ShapeDtypeStruct((1, rows), F32),
            jax.ShapeDtypeStruct((live, rows // dim * TILE, dim), F32),
            whole,
            whole,
        ],
        in_specs=[SMEM] * 2 + [VMEM] * 3 + [HBM],
        out_specs=[VMEM] * 8,
        scratch_shapes=[
            pltpu.VMEM((projected.shape[2], TILE, rows), F32),
            pltpu.SemaphoreType.DMA((live,)),
        ],
        compiler_params=pltpu.CompilerParams(vmem_limit_bytes=6 * MIB),
        name="prepare_rows",
    )(place, from_slot, projected, rate, gain, *in_hbm(states))


def diagonal(dim):
    row = lax.broadcasted_iota(jnp.int32, (TILE, dim), 0)
    return row == lax.broadcasted_iota(jnp.int32, (TILE, dim), 1)


def raw_kernel(
    shards, live, place, shard_ref, lead_0, lead_1, near_1, near_0,
    local, query, grown, base, raw, sums, made, tiles, sem,
):
    rows, dim = near_0.shape
    heads = rows // dim
    tile_rows = heads * TILE
    for row in range(live):
        made[row] = local[row]
    for n, near in enumerate((near_1, near_0)):
        for head in range(heads):
            span = slice(head * dim, (head + 1) * dim)
            made[live + n, head * TILE : (head + 1) * TILE] = products(
                query[:, span], near[span]
            )
    for n, lead in enumerate((lead_1, lead_0)):
        made[live + 2 + n] = lead[0:tile_rows]
    picks = []
    for row in range(live):
        gap = gap_of(row, shards, live, place, shard_ref)
        index = jnp.int32(row)
        for n, stride in enumerate((-1, 1, -2, 2)):
            index = jnp.where(at_stride(gap, stride, shards, place), live + n, index)
        picks.append(index)
    which = lax.rem(lax.broadcasted_iota(jnp.int32, (TILE, dim), 0), live)
    total = jnp.zeros((TILE, dim), F32)
    for head in range(heads):
        span = slice(head * dim, (head + 1) * dim)
        part = slice(head * TILE, (head + 1) * TILE)
        tile = made[picks[0], part]
        for row in range(1, live):
            tile = jnp.where(which == row, made[picks[row], part], tile)
        tile = tile * grown[:, span] + base[:, span]
        raw[:, span] = tile
        total = total + tile * tile
    total = jnp.broadcast_to(jnp.sum(total, axis=1, keepdims=True), (TILE, dim))
    total = jnp.sum(jnp.where(diagonal(dim), total, 0.0), axis=0, keepdims=True)
    for peer in range(sums.shape[0]):
        tiles[peer] = total
    copy = pltpu.make_async_copy(tiles, sums, sem)
    copy.start()
    copy.wait()


def raw_of(place, from_shard, arrived, small, shards, live, group):
    rows, dim = arrived[-1].shape
    return pl.pallas_call(
        functools.partial(raw_kernel, shards, live),
        out_shape=[
            jax.ShapeDtypeStruct((TILE, rows), F32),
            jax.ShapeDtypeStruct((group, 1, dim), F32),
        ],
        in_specs=[SMEM] * 2 + [VMEM] * (len(arrived) + len(small)),
        out_specs=[VMEM, HBM],
        scratch_shapes=[
            pltpu.VMEM((live + 4, rows // dim * TILE, dim), F32),
            pltpu.VMEM((group, 1, dim), F32),
            pltpu.SemaphoreType.DMA(()),
        ],
        compiler_params=pltpu.CompilerParams(vmem_limit_bytes=6 * MIB),
        cost_estimate=pl.CostEstimate(flops=10**12, bytes_accessed=MIB, transcendentals=0),
        name="raw_rows",
    )(place, from_shard, *arrived, *small)


def final_kernel(
    shards, live, place, shard_ref, here, lead_0, lead_1, near_1, near_0,
    rest_1, rest_0, outer, decay, final, token, held, made, sems_in, sems,
):
    rows, dim = here.shape[1:]
    heads = rows // dim
    early, tile_rows = EARLY * dim, heads * TILE
    token[...] = jnp.zeros_like(token)

    def loads(row, lead, rest):
        return [
            pltpu.make_async_copy(
                lead.at[tile_rows : tile_rows + early],
                held.at[row, 0:early],
                sems_in.at[row, 0],
            ),
            pltpu.make_async_copy(rest, held.at[row, early:rows], sems_in.at[row, 1]),
        ]

    cases = []
    for row in range(live):
        gap = gap_of(row, shards, live, place, shard_ref)
        far_0 = at_stride(gap, 2, shards, place)
        far_1 = at_stride(gap, -2, shards, place)
        for found, lead, rest in ((far_0, lead_0, rest_0), (far_1, lead_1, rest_1)):

            @pl.when(found)
            def _():
                start_all(loads(row, lead, rest))

        cases.append(
            [
                (gap == 0, here.at[row]),
                (at_stride(gap, 1, shards, place), near_0),
                (at_stride(gap, -1, shards, place), near_1),
                (jnp.logical_or(far_0, far_1), held.at[row]),
            ]
        )
    copies = []
    for row in range(live):

        @pl.when(cases[row][3][0])
        def _():
            wait_all(loads(row, lead_0, rest_0))

        for half in range(2):
            span = range(half * heads // 2, (half + 1) * heads // 2)
            for found, source in cases[row]:

                @pl.when(found)
                def _():
                    for head in span:
                        block = slice(head * dim, (head + 1) * dim)
                        made[row, block] = (
                            decay[:, block] * source[block] + outer[row, block]
                        )

            block = slice(span.start * dim, span.stop * dim)
            copy = pltpu.make_async_copy(
                made.at[row, block], final.at[row, block], sems.at[row, half]
            )
            copy.start()
            copies.append(copy)
    wait_all(copies)


def final_of(place, from_shard, here, lead, near, rest, small, shards, live):
    rows, dim = here.shape[1:]
    return pl.pallas_call(
        functools.partial(final_kernel, shards, live),
        out_shape=[
            jax.ShapeDtypeStruct((live, rows, dim), F32),
            jax.ShapeDtypeStruct((TILE, dim), F32),
        ],
        in_specs=[SMEM] * 2 + [VMEM] + [HBM] * 2 + [VMEM] * 2 + [HBM] * 2 + [VMEM] * 2,
        out_specs=[pl.BlockSpec(memory_space=pl.ANY), VMEM],
        scratch_shapes=[
            pltpu.VMEM((live, rows, dim), F32),
            pltpu.VMEM((live, rows, dim), F32),
            pltpu.SemaphoreType.DMA((live, 2)),
            pltpu.SemaphoreType.DMA((live, 2)),
        ],
        compiler_params=pltpu.CompilerParams(vmem_limit_bytes=8 * MIB),
        cost_estimate=pl.CostEstimate(flops=10**10, bytes_accessed=MIB, transcendentals=0),
        name="final_rows",
    )(place, from_shard, here, *in_hbm(*lead), *near, *in_hbm(*rest), *small)


def attend_kernel(live, features, totals, raw, gated, _, attended):
    dim = totals.shape[2]
    total = totals[0]
    for peer in range(1, totals.shape[0]):
        total = total + totals[peer]
    total = jnp.where(diagonal(dim), jnp.broadcast_to(total, (TILE, dim)), 0.0)
    total = jnp.sum(total, axis=1, keepdims=True)
    scale = jnp.broadcast_to(lax.rsqrt(total / features + EPS), raw.shape)
    tile = raw[...] * scale * gated[...]
    for step in range(attended.shape[0]):
        attended[step] = tile[step * live : (step + 1) * live].astype(BF16)


def attend(totals, raw, gated, after, live, steps, features):
    return pl.pallas_call(
        functools.partial(attend_kernel, live, features),
        out_shape=jax.ShapeDtypeStruct((steps, live, raw.shape[1]), BF16),
        in_specs=[VMEM] * 4,
        out_specs=VMEM,
        compiler_params=pltpu.CompilerParams(vmem_limit_bytes=4 * MIB),
        name="attend_rows",
    )(totals, raw, gated, after)


def on_device(states, from_shard, from_slot, projected, decay_rate, norm_gain):
    shards, group = lax.axis_size("dp"), lax.axis_size("tensor")
    steps, live = projected.shape[:2]
    slots, heads, dim = states.shape[:3]
    width = heads * dim
    place = lax.axis_index("dp").astype(jnp.int32).reshape(1)
    states = states.reshape(slots, width, dim)

    rate = jnp.repeat(decay_rate, dim).reshape(1, width)
    gain = norm_gain.reshape(1, width)
    query, grown, base, gated, decay, local, here, outer = prepare(
        place, from_slot, projected, rate, gain, states, live
    )

    rows = pick(
        place, from_shard, from_slot, projected, states, shards, live, (-2, 2, -1, 1)
    )
    half_1, half_0 = swapped(rows[1], "dp", 1), swapped(rows[0], "dp", 0)
    near_1, near_0 = swapped(rows[3], "dp", 1), swapped(rows[2], "dp", 0)
    sent = relay(half_0, half_1, decay, heads)
    lead_1, lead_0 = swapped(sent[0], "dp", 1), swapped(sent[1], "dp", 0)
    rest_1, rest_0 = swapped(sent[2], "dp", 1), swapped(sent[3], "dp", 0)

    raw, sums = raw_of(
        place, from_shard, (lead_0, lead_1, near_1, near_0),
        (local, query, grown, base), shards, live, group,
    )
    totals = lax.all_to_all(sums, "tensor", 0, 0)
    final, token = final_of(
        place, from_shard, here, (lead_0, lead_1), (near_1, near_0), (rest_1, rest_0),
        (outer, decay), shards, live,
    )
    attended = attend(totals, raw, gated, token, live, steps, width * group)
    return attended, final.reshape(live, heads, dim, dim)


def solution(mesh):
    return jax.shard_map(
        on_device,
        mesh=mesh,
        in_specs=(
            P("dp", "tensor", None, None),
            P(),
            P(),
            P(None, "dp", None, "tensor"),
            P("tensor"),
            P("tensor"),
        ),
        out_specs=(P(None, "dp", "tensor"), P("dp", "tensor", None, None)),
        check_vma=False,
    )
```

```python
import functools
import jax
import jax.numpy as jnp
from jax import lax
from jax.experimental import pallas as pl
from jax.experimental.pallas import tpu as pltpu
from jax.sharding import PartitionSpec as P

EPS = 1e-05
F32 = jnp.float32
BF16 = jnp.bfloat16
EARLY = 1
TILE = 8
MIB = 1024 * 1024
SMEM = pl.BlockSpec(memory_space=pltpu.SMEM)
VMEM = pl.BlockSpec(memory_space=pltpu.VMEM)
HBM = pl.BlockSpec(memory_space=pltpu.HBM)


def swapped(block, first):
    shards, group = lax.axis_size("dp"), lax.axis_size("tensor")
    route = []
    for i in range(0, shards, 2):
        for j in range(group):
            low = (first + j % 2 + i) % shards
            high = (low + 1) % shards
            route += [
                (low * group + j, high * group + j),
                (high * group + j, low * group + j),
            ]
    return lax.ppermute(block, ("dp", "tensor"), route)


def start_all(copies):
    for copy in copies:
        copy.start()


def wait_all(copies):
    for copy in copies:
        copy.wait()


def in_hbm(*arrays):
    return [pltpu.with_memory_space_constraint(x, pltpu.HBM) for x in arrays]


def products(query, state):
    q_high = query.astype(BF16).astype(F32)
    both = jnp.concatenate([q_high, query - q_high], axis=0).astype(BF16)
    high = state.astype(BF16)
    low = (state - high.astype(F32)).astype(BF16)
    first = jnp.dot(both, high, preferred_element_type=F32)
    second = jnp.dot(both, low, preferred_element_type=F32)
    return first[:TILE] + first[TILE:] + second[:TILE]


def pick_kernel(shards, live, strides, place, shard_hbm, slot_hbm, projected, states, *refs):
    n_rows = len(strides)
    outs = refs[:n_rows]
    shard_ref, slot_ref, inputs, sems = refs[n_rows:]
    rows, dim = outs[-1].shape
    device = place[0]
    plan = [
        pltpu.make_async_copy(shard_hbm, shard_ref, sems.at[n_rows]),
        pltpu.make_async_copy(slot_hbm, slot_ref, sems.at[n_rows + 1]),
    ]
    load = pltpu.make_async_copy(projected, inputs, sems.at[n_rows + 2])
    start_all(plan)
    load.start()
    wait_all(plan)
    copies = []
    for n, stride in enumerate(strides):
        target = lax.rem(device + stride * place[1] + shards, shards)
        slot = jnp.int32(0)
        for row in range(live):
            mine = shard_ref[target * live + row] == device
            slot = jnp.where(mine, slot_ref[target * live + row], slot)
        copies.append(
            pltpu.make_async_copy(states.at[slot], outs[n].at[0:rows], sems.at[n])
        )
    start_all(copies)
    load.wait()
    tile_rows = rows // dim * TILE
    for n in range(2):
        outs[n][rows : rows + tile_rows] = jnp.zeros((tile_rows, dim), F32)
    for step in range(inputs.shape[0]):
        for row in range(live):
            query = jax.nn.silu(inputs[step, row].astype(F32))[0:1]
            for head in range(rows // dim):
                at = rows + head * TILE + step * live + row
                part = query[:, head * dim : (head + 1) * dim]
                for n in range(2):
                    outs[n][at : at + 1] = part
    wait_all(copies)


def pick(place, from_shard, from_slot, projected, states, shards, live, strides):
    rows, dim = states.shape[1:]
    tile_rows = rows // dim * TILE
    return pl.pallas_call(
        functools.partial(pick_kernel, shards, live, strides),
        out_shape=[jax.ShapeDtypeStruct((rows + tile_rows, dim), F32)] * 2
        + [jax.ShapeDtypeStruct((rows, dim), F32)] * (len(strides) - 2),
        in_specs=[SMEM] + [HBM] * 4,
        out_specs=[VMEM] * len(strides),
        scratch_shapes=[
            pltpu.SMEM(from_shard.shape, jnp.int32),
            pltpu.SMEM(from_slot.shape, jnp.int32),
            pltpu.VMEM(projected.shape, projected.dtype),
            pltpu.SemaphoreType.DMA((len(strides) + 3,)),
        ],
        compiler_params=pltpu.CompilerParams(vmem_limit_bytes=6 * MIB),
        name="pick_rows",
    )(place, *in_hbm(from_shard, from_slot, projected, states))


def relay_kernel(from_0, from_1, _, lead_1, lead_0, rest_1, rest_0):
    dim = from_1.shape[1]
    heads = rest_0.shape[0] // dim + EARLY
    rows, early = heads * dim, EARLY * dim
    tile_rows = heads * TILE
    for source, other, lead, rest in (
        (from_0, from_1, lead_1, rest_1),
        (from_1, from_0, lead_0, rest_0),
    ):
        for head in range(heads):
            part = slice(head * TILE, (head + 1) * TILE)
            query = other[rows + head * TILE : rows + (head + 1) * TILE]
            state = source[head * dim : (head + 1) * dim]
            lead[part] = products(query, state)
            if head < EARLY:
                lead[tile_rows + head * dim : tile_rows + (head + 1) * dim] = state
            else:
                rest[(head - EARLY) * dim : (head - EARLY + 1) * dim] = state


def relay(from_0, from_1, after, heads):
    dim = from_0.shape[1]
    lead = jax.ShapeDtypeStruct((heads * TILE + EARLY * dim, dim), F32)
    rest = jax.ShapeDtypeStruct(((heads - EARLY) * dim, dim), F32)
    return pl.pallas_call(
        relay_kernel,
        out_shape=[lead, lead, rest, rest],
        in_specs=[VMEM] * 3,
        out_specs=[VMEM] * 4,
        compiler_params=pltpu.CompilerParams(vmem_limit_bytes=6 * MIB),
        name="relay_rows",
    )(from_0, from_1, after)


def gap_of(row, shards, live, place, shard_ref):
    device = place[0]
    return lax.rem(device - shard_ref[device * live + row] + shards, shards)


def at_stride(gap, stride, shards, place):
    return gap == lax.rem(stride * place[1] + shards, shards)


def prepare_kernel(
    live, place, slot_ref, projected, rate, gain, states,
    query, grown, base, gated, decay, made, here, outer, parts, sems,
):
    rows, dim = here.shape[1:]
    heads = rows // dim
    steps = projected.shape[0]
    copies = [
        pltpu.make_async_copy(
            states.at[slot_ref[place[0] * live + row]], here.at[row], sems.at[row]
        )
        for row in range(live)
    ]
    start_all(copies)
    parts[...] = jnp.zeros_like(parts)
    for step in range(steps):
        for row in range(live):
            block = projected[step, row].astype(F32)
            at = step * live + row
            for n in range(parts.shape[0]):
                parts[n, at : at + 1] = block[n : n + 1]
    queries, keys, values = (jax.nn.silu(parts[n]) for n in range(3))
    index = lax.broadcasted_iota(jnp.int32, queries.shape, 0)
    step_of = (index // live).astype(F32)
    rates = jnp.broadcast_to(rate[...], queries.shape)
    query[...] = queries
    gated[...] = jax.nn.sigmoid(parts[3]) * gain[...]
    grown[...] = jnp.exp(-rates * (step_of + 1.0))
    decay[...] = jnp.exp(-steps * rate[...])
    faded = keys * jnp.exp(-rates * jnp.maximum(steps - 1.0 - step_of, 0.0))
    later = lambda x, count: jnp.concatenate(
        [jnp.zeros((count, rows), F32), x[: TILE - count]], axis=0
    )
    total = jnp.zeros_like(queries)
    for lag in range(steps):
        key = later(keys, lag * live) if lag else keys
        value = later(values, lag * live) if lag else values
        product = queries * key
        match = jnp.concatenate(
            [
                jnp.broadcast_to(
                    jnp.sum(
                        product[:, head * dim : (head + 1) * dim], axis=1, keepdims=True
                    ),
                    (TILE, dim),
                )
                for head in range(heads)
            ],
            axis=1,
        )
        total = total + jnp.exp(-rates * float(lag)) * match * value
    base[...] = total

    def halves(x):
        high = x.astype(BF16).astype(F32)
        return high, x - high

    nothing = jnp.zeros_like(queries)
    v_high, v_low = halves(values)
    right = jnp.concatenate([v_high, v_high, v_low, nothing], axis=0).astype(BF16)
    for row in range(live):
        k_high, k_low = halves(jnp.where(lax.rem(index, live) == row, faded, 0.0))
        left = jnp.concatenate([k_high, k_low, k_high, nothing], axis=0).astype(BF16)
        for head in range(heads):
            span = slice(head * dim, (head + 1) * dim)
            outer[row, span] = lax.dot_general(
                left[:, span],
                right[:, span],
                (((0,), (0,)), ((), ())),
                preferred_element_type=F32,
            )
    wait_all(copies)
    for row in range(live):
        for head in range(heads):
            span = slice(head * dim, (head + 1) * dim)
            made[row, head * TILE : (head + 1) * TILE] = products(
                queries[:, span], here[row, span]
            )


def prepare(place, from_slot, projected, rate, gain, states, live):
    rows, dim = states.shape[1:]
    tile = jax.ShapeDtypeStruct((TILE, rows), F32)
    whole = jax.ShapeDtypeStruct((live, rows, dim), F32)
    return pl.pallas_call(
        functools.partial(prepare_kernel, live),
        out_shape=[tile] * 4
        + [
            jax.ShapeDtypeStruct((1, rows), F32),
            jax.ShapeDtypeStruct((live, rows // dim * TILE, dim), F32),
            whole,
            whole,
        ],
        in_specs=[SMEM] * 2 + [VMEM] * 3 + [HBM],
        out_specs=[VMEM] * 8,
        scratch_shapes=[
            pltpu.VMEM((projected.shape[2], TILE, rows), F32),
            pltpu.SemaphoreType.DMA((live,)),
        ],
        compiler_params=pltpu.CompilerParams(vmem_limit_bytes=6 * MIB),
        name="prepare_rows",
    )(place, from_slot, projected, rate, gain, *in_hbm(states))


def diagonal(dim):
    row = lax.broadcasted_iota(jnp.int32, (TILE, dim), 0)
    return row == lax.broadcasted_iota(jnp.int32, (TILE, dim), 1)


def raw_kernel(
    shards, live, place, shard_ref, lead_0, lead_1, near_1, near_0,
    local, query, grown, base, raw, sums, made, tiles, sem,
):
    rows, dim = near_0.shape
    heads = rows // dim
    tile_rows = heads * TILE
    for row in range(live):
        made[row] = local[row]
    for n, near in enumerate((near_1, near_0)):
        for head in range(heads):
            span = slice(head * dim, (head + 1) * dim)
            made[live + n, head * TILE : (head + 1) * TILE] = products(
                query[:, span], near[span]
            )
    for n, lead in enumerate((lead_1, lead_0)):
        made[live + 2 + n] = lead[0:tile_rows]
    picks = []
    for row in range(live):
        gap = gap_of(row, shards, live, place, shard_ref)
        index = jnp.int32(row)
        for n, stride in enumerate((-1, 1, -2, 2)):
            index = jnp.where(at_stride(gap, stride, shards, place), live + n, index)
        picks.append(index)
    which = lax.rem(lax.broadcasted_iota(jnp.int32, (TILE, dim), 0), live)
    total = jnp.zeros((TILE, dim), F32)
    for head in range(heads):
        span = slice(head * dim, (head + 1) * dim)
        part = slice(head * TILE, (head + 1) * TILE)
        tile = made[picks[0], part]
        for row in range(1, live):
            tile = jnp.where(which == row, made[picks[row], part], tile)
        tile = tile * grown[:, span] + base[:, span]
        raw[:, span] = tile
        total = total + tile * tile
    total = jnp.broadcast_to(jnp.sum(total, axis=1, keepdims=True), (TILE, dim))
    total = jnp.sum(jnp.where(diagonal(dim), total, 0.0), axis=0, keepdims=True)
    for peer in range(sums.shape[0]):
        tiles[peer] = total
    copy = pltpu.make_async_copy(tiles, sums, sem)
    copy.start()
    copy.wait()


def raw_of(place, from_shard, arrived, small, shards, live, group):
    rows, dim = arrived[-1].shape
    return pl.pallas_call(
        functools.partial(raw_kernel, shards, live),
        out_shape=[
            jax.ShapeDtypeStruct((TILE, rows), F32),
            jax.ShapeDtypeStruct((group, 1, dim), F32),
        ],
        in_specs=[SMEM] * 2 + [VMEM] * (len(arrived) + len(small)),
        out_specs=[VMEM, HBM],
        scratch_shapes=[
            pltpu.VMEM((live + 4, rows // dim * TILE, dim), F32),
            pltpu.VMEM((group, 1, dim), F32),
            pltpu.SemaphoreType.DMA(()),
        ],
        compiler_params=pltpu.CompilerParams(vmem_limit_bytes=6 * MIB),
        cost_estimate=pl.CostEstimate(flops=10**12, bytes_accessed=MIB, transcendentals=0),
        name="raw_rows",
    )(place, from_shard, *arrived, *small)


def final_kernel(
    shards, live, place, shard_ref, here, lead_0, lead_1, near_1, near_0,
    rest_1, rest_0, outer, decay, final, token, held, made, sems_in, sems,
):
    rows, dim = here.shape[1:]
    heads = rows // dim
    early, tile_rows = EARLY * dim, heads * TILE
    token[...] = jnp.zeros_like(token)

    def loads(row, lead, rest):
        return [
            pltpu.make_async_copy(
                lead.at[tile_rows : tile_rows + early],
                held.at[row, 0:early],
                sems_in.at[row, 0],
            ),
            pltpu.make_async_copy(rest, held.at[row, early:rows], sems_in.at[row, 1]),
        ]

    cases = []
    for row in range(live):
        gap = gap_of(row, shards, live, place, shard_ref)
        far_0 = at_stride(gap, 2, shards, place)
        far_1 = at_stride(gap, -2, shards, place)
        for found, lead, rest in ((far_0, lead_0, rest_0), (far_1, lead_1, rest_1)):

            @pl.when(found)
            def _():
                start_all(loads(row, lead, rest))

        cases.append(
            [
                (gap == 0, here.at[row]),
                (at_stride(gap, 1, shards, place), near_0),
                (at_stride(gap, -1, shards, place), near_1),
                (jnp.logical_or(far_0, far_1), held.at[row]),
            ]
        )
    copies = []
    for row in range(live):

        @pl.when(cases[row][3][0])
        def _():
            wait_all(loads(row, lead_0, rest_0))

        for half in range(2):
            span = range(half * heads // 2, (half + 1) * heads // 2)
            for found, source in cases[row]:

                @pl.when(found)
                def _():
                    for head in span:
                        block = slice(head * dim, (head + 1) * dim)
                        made[row, block] = (
                            decay[:, block] * source[block] + outer[row, block]
                        )

            block = slice(span.start * dim, span.stop * dim)
            copy = pltpu.make_async_copy(
                made.at[row, block], final.at[row, block], sems.at[row, half]
            )
            copy.start()
            copies.append(copy)
    wait_all(copies)


def final_of(place, from_shard, here, lead, near, rest, small, shards, live):
    rows, dim = here.shape[1:]
    return pl.pallas_call(
        functools.partial(final_kernel, shards, live),
        out_shape=[
            jax.ShapeDtypeStruct((live, rows, dim), F32),
            jax.ShapeDtypeStruct((TILE, dim), F32),
        ],
        in_specs=[SMEM] * 2 + [VMEM] + [HBM] * 2 + [VMEM] * 2 + [HBM] * 2 + [VMEM] * 2,
        out_specs=[pl.BlockSpec(memory_space=pl.ANY), VMEM],
        scratch_shapes=[
            pltpu.VMEM((live, rows, dim), F32),
            pltpu.VMEM((live, rows, dim), F32),
            pltpu.SemaphoreType.DMA((live, 2)),
            pltpu.SemaphoreType.DMA((live, 2)),
        ],
        compiler_params=pltpu.CompilerParams(vmem_limit_bytes=8 * MIB),
        cost_estimate=pl.CostEstimate(flops=10**10, bytes_accessed=MIB, transcendentals=0),
        name="final_rows",
    )(place, from_shard, here, *in_hbm(*lead), *near, *in_hbm(*rest), *small)


def attend_kernel(live, features, totals, raw, gated, _, attended):
    dim = totals.shape[2]
    total = totals[0]
    for peer in range(1, totals.shape[0]):
        total = total + totals[peer]
    total = jnp.where(diagonal(dim), jnp.broadcast_to(total, (TILE, dim)), 0.0)
    total = jnp.sum(total, axis=1, keepdims=True)
    scale = jnp.broadcast_to(lax.rsqrt(total / features + EPS), raw.shape)
    tile = raw[...] * scale * gated[...]
    for step in range(attended.shape[0]):
        attended[step] = tile[step * live : (step + 1) * live].astype(BF16)


def attend(totals, raw, gated, after, live, steps, features):
    return pl.pallas_call(
        functools.partial(attend_kernel, live, features),
        out_shape=jax.ShapeDtypeStruct((steps, live, raw.shape[1]), BF16),
        in_specs=[VMEM] * 4,
        out_specs=VMEM,
        compiler_params=pltpu.CompilerParams(vmem_limit_bytes=4 * MIB),
        name="attend_rows",
    )(totals, raw, gated, after)


def on_device(states, from_shard, from_slot, projected, decay_rate, norm_gain):
    shards, group = lax.axis_size("dp"), lax.axis_size("tensor")
    steps, live = projected.shape[:2]
    slots, heads, dim = states.shape[:3]
    width = heads * dim
    shard = lax.axis_index("dp").astype(jnp.int32)
    side = 2 * ((shard ^ lax.axis_index("tensor").astype(jnp.int32)) & 1) - 1
    place = jnp.stack([shard, side])
    states = states.reshape(slots, width, dim)

    rate = jnp.repeat(decay_rate, dim).reshape(1, width)
    gain = norm_gain.reshape(1, width)
    query, grown, base, gated, decay, local, here, outer = prepare(
        place, from_slot, projected, rate, gain, states, live
    )

    rows = pick(
        place, from_shard, from_slot, projected, states, shards, live, (-2, 2, -1, 1)
    )
    half_1, half_0 = swapped(rows[1], 1), swapped(rows[0], 0)
    near_1, near_0 = swapped(rows[3], 1), swapped(rows[2], 0)
    sent = relay(half_0, half_1, decay, heads)
    lead_1, lead_0 = swapped(sent[0], 1), swapped(sent[1], 0)
    rest_1, rest_0 = swapped(sent[2], 1), swapped(sent[3], 0)

    raw, sums = raw_of(
        place, from_shard, (lead_0, lead_1, near_1, near_0),
        (local, query, grown, base), shards, live, group,
    )
    totals = lax.all_to_all(sums, "tensor", 0, 0)
    final, token = final_of(
        place, from_shard, here, (lead_0, lead_1), (near_1, near_0), (rest_1, rest_0),
        (outer, decay), shards, live,
    )
    attended = attend(totals, raw, gated, token, live, steps, width * group)
    return attended, final.reshape(live, heads, dim, dim)


def solution(mesh):
    return jax.shard_map(
        on_device,
        mesh=mesh,
        in_specs=(
            P("dp", "tensor", None, None),
            P(),
            P(),
            P(None, "dp", None, "tensor"),
            P("tensor"),
            P("tensor"),
        ),
        out_specs=(P(None, "dp", "tensor"), P("dp", "tensor", None, None)),
        check_vma=False,
    )
```

```python
import functools
import jax
import jax.numpy as jnp
from jax import lax
from jax.experimental import pallas as pl
from jax.experimental.pallas import tpu as pltpu
from jax.sharding import PartitionSpec as P

EPS = 1e-05
F32 = jnp.float32
BF16 = jnp.bfloat16
EARLY = 3
TILE = 8
MIB = 1024 * 1024
SMEM = pl.BlockSpec(memory_space=pltpu.SMEM)
VMEM = pl.BlockSpec(memory_space=pltpu.VMEM)
HBM = pl.BlockSpec(memory_space=pltpu.HBM)


def swapped(block, first):
    shards, group = lax.axis_size("dp"), lax.axis_size("tensor")
    route = []
    for i in range(0, shards, 2):
        for j in range(group):
            low = (first + j % 2 + i) % shards
            high = (low + 1) % shards
            route += [
                (low * group + j, high * group + j),
                (high * group + j, low * group + j),
            ]
    return lax.ppermute(block, ("dp", "tensor"), route)


def spot(place, group):
    shard = lax.div(place[0], group)
    return shard, 2 * ((shard ^ lax.rem(place[0], group)) & 1) - 1


def start_all(copies):
    for copy in copies:
        copy.start()


def wait_all(copies):
    for copy in copies:
        copy.wait()


def in_hbm(*arrays):
    return [pltpu.with_memory_space_constraint(x, pltpu.HBM) for x in arrays]


def products(query, state):
    q_high = query.astype(BF16).astype(F32)
    both = jnp.concatenate([q_high, query - q_high], axis=0).astype(BF16)
    high = state.astype(BF16)
    low = (state - high.astype(F32)).astype(BF16)
    first = jnp.dot(both, high, preferred_element_type=F32)
    second = jnp.dot(both, low, preferred_element_type=F32)
    return first[:TILE] + first[TILE:] + second[:TILE]


def pick_kernel(shards, live, group, strides, place, shard_hbm, slot_hbm, projected, states, *refs):
    n_rows = len(strides)
    outs = refs[:n_rows]
    token, shard_ref, slot_ref, inputs, sems = refs[n_rows:]
    dim = outs[0].shape[1]
    rows = states.shape[1]
    device, side = spot(place, group)
    plan = [
        pltpu.make_async_copy(shard_hbm, shard_ref, sems.at[n_rows]),
        pltpu.make_async_copy(slot_hbm, slot_ref, sems.at[n_rows + 1]),
    ]
    load = pltpu.make_async_copy(projected, inputs, sems.at[n_rows + 2])
    start_all(plan)
    load.start()
    wait_all(plan)
    copies = []
    for n, stride in enumerate(strides):
        slot = slot_for(stride, shards, live, device, side, shard_ref, slot_ref)
        copies.append(
            pltpu.make_async_copy(states.at[slot], outs[n].at[0:rows], sems.at[n])
        )
    start_all(copies)
    token[...] = jnp.zeros_like(token)
    load.wait()
    tile_rows = rows // dim * TILE
    for n in range(n_rows):
        outs[n][rows : rows + tile_rows] = jnp.zeros((tile_rows, dim), F32)
    for step in range(inputs.shape[0]):
        for row in range(live):
            query = jax.nn.silu(inputs[step, row].astype(F32))[0:1]
            for head in range(rows // dim):
                at = rows + head * TILE + step * live + row
                part = query[:, head * dim : (head + 1) * dim]
                for n in range(n_rows):
                    outs[n][at : at + 1] = part
    wait_all(copies)


def pick(place, from_shard, from_slot, projected, states, shards, live, group, strides):
    rows, dim = states.shape[1:]
    tile_rows = rows // dim * TILE
    return pl.pallas_call(
        functools.partial(pick_kernel, shards, live, group, strides),
        out_shape=[jax.ShapeDtypeStruct((rows + tile_rows, dim), F32)] * len(strides)
        + [jax.ShapeDtypeStruct((TILE, dim), F32)],
        in_specs=[SMEM] + [HBM] * 4,
        out_specs=[VMEM] * (len(strides) + 1),
        scratch_shapes=[
            pltpu.SMEM(from_shard.shape, jnp.int32),
            pltpu.SMEM(from_slot.shape, jnp.int32),
            pltpu.VMEM(projected.shape, projected.dtype),
            pltpu.SemaphoreType.DMA((len(strides) + 3,)),
        ],
        compiler_params=pltpu.CompilerParams(vmem_limit_bytes=4 * MIB),
        name="pick_rows",
    )(place, *in_hbm(from_shard, from_slot, projected, states))


def relay_kernel(from_0, from_1, _, lead_1, lead_0, rest_1, rest_0):
    dim = from_1.shape[1]
    heads = rest_0.shape[0] // dim + EARLY
    rows, early = heads * dim, EARLY * dim
    tile_rows = heads * TILE
    for source, other, lead, rest in (
        (from_0, from_1, lead_1, rest_1),
        (from_1, from_0, lead_0, rest_0),
    ):
        for head in range(heads):
            part = slice(head * TILE, (head + 1) * TILE)
            query = other[rows + head * TILE : rows + (head + 1) * TILE]
            state = source[head * dim : (head + 1) * dim]
            lead[part] = products(query, state)
            if head < EARLY:
                lead[tile_rows + head * dim : tile_rows + (head + 1) * dim] = state
            else:
                rest[(head - EARLY) * dim : (head - EARLY + 1) * dim] = state


def relay(from_0, from_1, after, heads):
    dim = from_0.shape[1]
    lead = jax.ShapeDtypeStruct((heads * TILE + EARLY * dim, dim), F32)
    rest = jax.ShapeDtypeStruct(((heads - EARLY) * dim, dim), F32)
    return pl.pallas_call(
        relay_kernel,
        out_shape=[lead, lead, rest, rest],
        in_specs=[VMEM] * 3,
        out_specs=[VMEM] * 4,
        compiler_params=pltpu.CompilerParams(vmem_limit_bytes=6 * MIB),
        name="relay_rows",
    )(from_0, from_1, after)


def gap_of(row, shards, live, device, shard_ref):
    return lax.rem(device - shard_ref[device * live + row] + shards, shards)


def at_stride(gap, stride, shards, side):
    return gap == lax.rem(stride * side + shards, shards)


def slot_for(stride, shards, live, device, side, shard_ref, slot_ref):
    target = lax.rem(device + stride * side + shards, shards)
    slot = jnp.int32(0)
    for row in range(live):
        mine = shard_ref[target * live + row] == device
        slot = jnp.where(mine, slot_ref[target * live + row], slot)
    return slot


def prepare_kernel(
    shards, live, group, strides, place, shard_ref, slot_ref, projected, rate, gain, _, states,
    query, grown, base, gated, decay, made, here, outer, token, *refs,
):
    outs, (parts, sems) = refs[:-2], refs[-2:]
    token[...] = jnp.zeros_like(token)
    rows, dim = here.shape[1:]
    heads = rows // dim
    steps = projected.shape[0]
    device, side = spot(place, group)
    copies = [
        pltpu.make_async_copy(
            states.at[slot_ref[device * live + row]], here.at[row], sems.at[row]
        )
        for row in range(live)
    ]
    start_all(copies)
    sends = []
    for n, stride in enumerate(strides):
        slot = slot_for(stride, shards, live, device, side, shard_ref, slot_ref)
        sends.append(pltpu.make_async_copy(states.at[slot], outs[n], sems.at[live + n]))
    start_all(sends)
    parts[...] = jnp.zeros_like(parts)
    for step in range(steps):
        for row in range(live):
            block = projected[step, row].astype(F32)
            at = step * live + row
            for n in range(parts.shape[0]):
                parts[n, at : at + 1] = block[n : n + 1]
    queries, keys, values = (jax.nn.silu(parts[n]) for n in range(3))
    index = lax.broadcasted_iota(jnp.int32, queries.shape, 0)
    step_of = (index // live).astype(F32)
    rates = jnp.broadcast_to(rate[...], queries.shape)
    query[...] = queries
    gated[...] = jax.nn.sigmoid(parts[3]) * gain[...]
    grown[...] = jnp.exp(-rates * (step_of + 1.0))
    decay[...] = jnp.exp(-steps * rate[...])
    faded = keys * jnp.exp(-rates * jnp.maximum(steps - 1.0 - step_of, 0.0))
    later = lambda x, count: jnp.concatenate(
        [jnp.zeros((count, rows), F32), x[: TILE - count]], axis=0
    )
    total = jnp.zeros_like(queries)
    for lag in range(steps):
        key = later(keys, lag * live) if lag else keys
        value = later(values, lag * live) if lag else values
        product = queries * key
        match = jnp.concatenate(
            [
                jnp.broadcast_to(
                    jnp.sum(
                        product[:, head * dim : (head + 1) * dim], axis=1, keepdims=True
                    ),
                    (TILE, dim),
                )
                for head in range(heads)
            ],
            axis=1,
        )
        total = total + jnp.exp(-rates * float(lag)) * match * value
    base[...] = total

    def halves(x):
        high = x.astype(BF16).astype(F32)
        return high, x - high

    nothing = jnp.zeros_like(queries)
    v_high, v_low = halves(values)
    right = jnp.concatenate([v_high, v_high, v_low, nothing], axis=0).astype(BF16)
    for row in range(live):
        k_high, k_low = halves(jnp.where(lax.rem(index, live) == row, faded, 0.0))
        left = jnp.concatenate([k_high, k_low, k_high, nothing], axis=0).astype(BF16)
        for head in range(heads):
            span = slice(head * dim, (head + 1) * dim)
            outer[row, span] = lax.dot_general(
                left[:, span],
                right[:, span],
                (((0,), (0,)), ((), ())),
                preferred_element_type=F32,
            )
    wait_all(copies)
    for row in range(live):
        for head in range(heads):
            span = slice(head * dim, (head + 1) * dim)
            made[row, head * TILE : (head + 1) * TILE] = products(
                queries[:, span], here[row, span]
            )
    wait_all(sends)


def prepare(
    place, from_shard, from_slot, projected, rate, gain, after, states, shards, live, group, strides
):
    rows, dim = states.shape[1:]
    tile = jax.ShapeDtypeStruct((TILE, rows), F32)
    whole = jax.ShapeDtypeStruct((live, rows, dim), F32)
    return pl.pallas_call(
        functools.partial(prepare_kernel, shards, live, group, strides),
        out_shape=[tile] * 4
        + [
            jax.ShapeDtypeStruct((1, rows), F32),
            jax.ShapeDtypeStruct((live, rows // dim * TILE, dim), F32),
            whole,
            whole,
            jax.ShapeDtypeStruct((TILE, dim), F32),
        ]
        + [jax.ShapeDtypeStruct((rows, dim), F32)] * len(strides),
        in_specs=[SMEM] * 3 + [VMEM] * 4 + [HBM],
        out_specs=[VMEM] * (9 + len(strides)),
        scratch_shapes=[
            pltpu.VMEM((projected.shape[2], TILE, rows), F32),
            pltpu.SemaphoreType.DMA((live + len(strides),)),
        ],
        compiler_params=pltpu.CompilerParams(vmem_limit_bytes=8 * MIB),
        name="prepare_rows",
    )(place, from_shard, from_slot, projected, rate, gain, after, *in_hbm(states))


def diagonal(dim):
    row = lax.broadcasted_iota(jnp.int32, (TILE, dim), 0)
    return row == lax.broadcasted_iota(jnp.int32, (TILE, dim), 1)


def raw_kernel(
    shards, live, group, place, shard_ref, lead_0, lead_1, near_1, near_0,
    local, query, grown, base, raw, sums, made, tiles, sem,
):
    rows, dim = near_0.shape
    heads = rows // dim
    tile_rows = heads * TILE
    for row in range(live):
        made[row] = local[row]
    for n, near in enumerate((near_1, near_0)):
        for head in range(heads):
            span = slice(head * dim, (head + 1) * dim)
            made[live + n, head * TILE : (head + 1) * TILE] = products(
                query[:, span], near[span]
            )
    for n, lead in enumerate((lead_1, lead_0)):
        made[live + 2 + n] = lead[0:tile_rows]
    picks = []
    device, side = spot(place, group)
    for row in range(live):
        gap = gap_of(row, shards, live, device, shard_ref)
        index = jnp.int32(row)
        for n, stride in enumerate((-1, 1, -2, 2)):
            index = jnp.where(at_stride(gap, stride, shards, side), live + n, index)
        picks.append(index)
    which = lax.rem(lax.broadcasted_iota(jnp.int32, (TILE, dim), 0), live)
    total = jnp.zeros((TILE, dim), F32)
    for head in range(heads):
        span = slice(head * dim, (head + 1) * dim)
        part = slice(head * TILE, (head + 1) * TILE)
        tile = made[picks[0], part]
        for row in range(1, live):
            tile = jnp.where(which == row, made[picks[row], part], tile)
        tile = tile * grown[:, span] + base[:, span]
        raw[:, span] = tile
        total = total + tile * tile
    total = jnp.broadcast_to(jnp.sum(total, axis=1, keepdims=True), (TILE, dim))
    total = jnp.sum(jnp.where(diagonal(dim), total, 0.0), axis=0, keepdims=True)
    for peer in range(sums.shape[0]):
        tiles[peer] = total
    copy = pltpu.make_async_copy(tiles, sums, sem)
    copy.start()
    copy.wait()


def raw_of(place, from_shard, arrived, small, shards, live, group):
    rows, dim = arrived[-1].shape
    return pl.pallas_call(
        functools.partial(raw_kernel, shards, live, group),
        out_shape=[
            jax.ShapeDtypeStruct((TILE, rows), F32),
            jax.ShapeDtypeStruct((group, 1, dim), F32),
        ],
        in_specs=[SMEM] * 2 + [VMEM] * (len(arrived) + len(small)),
        out_specs=[VMEM, HBM],
        scratch_shapes=[
            pltpu.VMEM((live + 4, rows // dim * TILE, dim), F32),
            pltpu.VMEM((group, 1, dim), F32),
            pltpu.SemaphoreType.DMA(()),
        ],
        compiler_params=pltpu.CompilerParams(vmem_limit_bytes=6 * MIB),
        cost_estimate=pl.CostEstimate(flops=10**12, bytes_accessed=MIB, transcendentals=0),
        name="raw_rows",
    )(place, from_shard, *arrived, *small)


def final_kernel(
    shards, live, group, place, shard_ref, here, lead_0, lead_1, near_1, near_0,
    rest_1, rest_0, outer, decay, final, token, held, made, sems_in, sems,
):
    rows, dim = here.shape[1:]
    heads = rows // dim
    early, tile_rows = EARLY * dim, heads * TILE
    device, side = spot(place, group)
    token[...] = jnp.zeros_like(token)

    def loads(row, lead, rest):
        return [
            pltpu.make_async_copy(
                lead.at[tile_rows : tile_rows + early],
                held.at[row, 0:early],
                sems_in.at[row, 0],
            ),
            pltpu.make_async_copy(rest, held.at[row, early:rows], sems_in.at[row, 1]),
        ]

    cases = []
    for row in range(live):
        gap = gap_of(row, shards, live, device, shard_ref)
        far_0 = at_stride(gap, 2, shards, side)
        far_1 = at_stride(gap, -2, shards, side)
        for found, lead, rest in ((far_0, lead_0, rest_0), (far_1, lead_1, rest_1)):

            @pl.when(found)
            def _():
                start_all(loads(row, lead, rest))

        cases.append(
            [
                (gap == 0, here.at[row]),
                (at_stride(gap, 1, shards, side), near_0),
                (at_stride(gap, -1, shards, side), near_1),
                (jnp.logical_or(far_0, far_1), held.at[row]),
            ]
        )
    copies = []
    for row in range(live):

        @pl.when(cases[row][3][0])
        def _():
            wait_all(loads(row, lead_0, rest_0))

        for half in range(2):
            span = range(half * heads // 2, (half + 1) * heads // 2)
            for found, source in cases[row]:

                @pl.when(found)
                def _():
                    for head in span:
                        block = slice(head * dim, (head + 1) * dim)
                        made[row, block] = (
                            decay[:, block] * source[block] + outer[row, block]
                        )

            block = slice(span.start * dim, span.stop * dim)
            copy = pltpu.make_async_copy(
                made.at[row, block], final.at[row, block], sems.at[row, half]
            )
            copy.start()
            copies.append(copy)
    wait_all(copies)


def final_of(place, from_shard, here, lead, near, rest, small, shards, live, group):
    rows, dim = here.shape[1:]
    return pl.pallas_call(
        functools.partial(final_kernel, shards, live, group),
        out_shape=[
            jax.ShapeDtypeStruct((live, rows, dim), F32),
            jax.ShapeDtypeStruct((TILE, dim), F32),
        ],
        in_specs=[SMEM] * 2 + [VMEM] + [HBM] * 2 + [VMEM] * 2 + [HBM] * 2 + [VMEM] * 2,
        out_specs=[pl.BlockSpec(memory_space=pl.ANY), VMEM],
        scratch_shapes=[
            pltpu.VMEM((live, rows, dim), F32),
            pltpu.VMEM((live, rows, dim), F32),
            pltpu.SemaphoreType.DMA((live, 2)),
            pltpu.SemaphoreType.DMA((live, 2)),
        ],
        compiler_params=pltpu.CompilerParams(vmem_limit_bytes=8 * MIB),
        cost_estimate=pl.CostEstimate(flops=10**10, bytes_accessed=MIB, transcendentals=0),
        name="final_rows",
    )(place, from_shard, here, *in_hbm(*lead), *near, *in_hbm(*rest), *small)


def attend_kernel(live, features, totals, raw, gated, _, attended):
    dim = totals.shape[2]
    total = totals[0]
    for peer in range(1, totals.shape[0]):
        total = total + totals[peer]
    total = jnp.where(diagonal(dim), jnp.broadcast_to(total, (TILE, dim)), 0.0)
    total = jnp.sum(total, axis=1, keepdims=True)
    scale = jnp.broadcast_to(lax.rsqrt(total / features + EPS), raw.shape)
    tile = raw[...] * scale * gated[...]
    for step in range(attended.shape[0]):
        attended[step] = tile[step * live : (step + 1) * live].astype(BF16)


def attend(totals, raw, gated, after, live, steps, features):
    return pl.pallas_call(
        functools.partial(attend_kernel, live, features),
        out_shape=jax.ShapeDtypeStruct((steps, live, raw.shape[1]), BF16),
        in_specs=[VMEM] * 4,
        out_specs=VMEM,
        compiler_params=pltpu.CompilerParams(vmem_limit_bytes=4 * MIB),
        name="attend_rows",
    )(totals, raw, gated, after)


def on_device(states, from_shard, from_slot, projected, decay_rate, norm_gain):
    shards, group = lax.axis_size("dp"), lax.axis_size("tensor")
    steps, live = projected.shape[:2]
    slots, heads, dim = states.shape[:3]
    width = heads * dim
    place = lax.axis_index(("dp", "tensor")).astype(jnp.int32).reshape(1)
    states = states.reshape(slots, width, dim)

    row_0, row_1, after = pick(
        place, from_shard, from_slot, projected, states, shards, live, group, (-2, 2)
    )
    half_1, half_0 = swapped(row_1, 1), swapped(row_0, 0)
    rate = jnp.repeat(decay_rate, dim).reshape(1, width)
    gain = norm_gain.reshape(1, width)
    query, grown, base, gated, decay, local, here, outer, token, row_0, row_1 = prepare(
        place, from_shard, from_slot, projected, rate, gain, after, states, shards, live,
        group, (-1, 1),
    )
    near_1, near_0 = swapped(row_1, 1), swapped(row_0, 0)
    sent = relay(half_0, half_1, token, heads)
    lead_1, lead_0 = swapped(sent[0], 1), swapped(sent[1], 0)
    rest_1, rest_0 = swapped(sent[2], 1), swapped(sent[3], 0)

    raw, sums = raw_of(
        place, from_shard, (lead_0, lead_1, near_1, near_0),
        (local, query, grown, base), shards, live, group,
    )
    totals = lax.all_to_all(sums, "tensor", 0, 0)
    final, token = final_of(
        place, from_shard, here, (lead_0, lead_1), (near_1, near_0), (rest_1, rest_0),
        (outer, decay), shards, live, group,
    )
    attended = attend(totals, raw, gated, token, live, steps, width * group)
    return attended, final.reshape(live, heads, dim, dim)


def solution(mesh):
    return jax.shard_map(
        on_device,
        mesh=mesh,
        in_specs=(
            P("dp", "tensor", None, None),
            P(),
            P(),
            P(None, "dp", None, "tensor"),
            P("tensor"),
            P("tensor"),
        ),
        out_specs=(P(None, "dp", "tensor"), P("dp", "tensor", None, None)),
        check_vma=False,
    )
```

```python
import functools
import jax
import jax.numpy as jnp
from jax import lax
from jax.experimental import pallas as pl
from jax.experimental.pallas import tpu as pltpu
from jax.sharding import PartitionSpec as P

EPS = 1e-05
F32 = jnp.float32
BF16 = jnp.bfloat16
EARLY = 3
TILE = 8
MIB = 1024 * 1024
SMEM = pl.BlockSpec(memory_space=pltpu.SMEM)
VMEM = pl.BlockSpec(memory_space=pltpu.VMEM)
HBM = pl.BlockSpec(memory_space=pltpu.HBM)


def swapped(block, first):
    shards, group = lax.axis_size("dp"), lax.axis_size("tensor")
    route = []
    for i in range(0, shards, 2):
        for j in range(group):
            low = (first + j % 2 + i) % shards
            high = (low + 1) % shards
            route += [
                (low * group + j, high * group + j),
                (high * group + j, low * group + j),
            ]
    return lax.ppermute(block, ("dp", "tensor"), route)


def spot(place, group):
    shard = lax.div(place[0], group)
    return shard, 2 * ((shard ^ lax.rem(place[0], group)) & 1) - 1


def start_all(copies):
    for copy in copies:
        copy.start()


def wait_all(copies):
    for copy in copies:
        copy.wait()


def in_hbm(*arrays):
    return [pltpu.with_memory_space_constraint(x, pltpu.HBM) for x in arrays]


def products(query, state):
    q_high = query.astype(BF16).astype(F32)
    both = jnp.concatenate([q_high, query - q_high], axis=0).astype(BF16)
    high = state.astype(BF16)
    low = (state - high.astype(F32)).astype(BF16)
    first = jnp.dot(both, high, preferred_element_type=F32)
    second = jnp.dot(both, low, preferred_element_type=F32)
    return first[:TILE] + first[TILE:] + second[:TILE]


def pick_kernel(shards, live, group, strides, place, shard_hbm, slot_hbm, projected, states, *refs):
    n_rows = len(strides)
    outs = refs[:n_rows]
    staged, shard_ref, slot_ref, inputs, sems = refs[n_rows:]
    dim = outs[0].shape[1]
    rows = states.shape[1]
    device, side = spot(place, group)
    copies = [
        pltpu.make_async_copy(shard_hbm, shard_ref, sems.at[0]),
        pltpu.make_async_copy(slot_hbm, slot_ref, sems.at[1]),
        pltpu.make_async_copy(projected, inputs, sems.at[2]),
        pltpu.make_async_copy(states, staged, sems.at[3]),
    ]
    start_all(copies)
    tile_rows = rows // dim * TILE
    for n in range(n_rows):
        outs[n][rows : rows + tile_rows] = jnp.zeros((tile_rows, dim), F32)
    copies[2].wait()
    for step in range(inputs.shape[0]):
        for row in range(live):
            query = jax.nn.silu(inputs[step, row].astype(F32))[0:1]
            for head in range(rows // dim):
                at = rows + head * TILE + step * live + row
                part = query[:, head * dim : (head + 1) * dim]
                for n in range(n_rows):
                    outs[n][at : at + 1] = part
    wait_all(copies[:2])
    slots = [
        slot_for(stride, shards, live, device, side, shard_ref, slot_ref)
        for stride in strides
    ]
    copies[3].wait()
    for n, slot in enumerate(slots):
        outs[n][0:rows] = staged[slot]


def pick(place, from_shard, from_slot, projected, states, shards, live, group, strides):
    rows, dim = states.shape[1:]
    tile_rows = rows // dim * TILE
    return pl.pallas_call(
        functools.partial(pick_kernel, shards, live, group, strides),
        out_shape=[jax.ShapeDtypeStruct((rows + tile_rows, dim), F32)] * len(strides)
        + [jax.ShapeDtypeStruct(states.shape, F32)],
        in_specs=[SMEM] + [HBM] * 4,
        out_specs=[VMEM] * (len(strides) + 1),
        scratch_shapes=[
            pltpu.SMEM(from_shard.shape, jnp.int32),
            pltpu.SMEM(from_slot.shape, jnp.int32),
            pltpu.VMEM(projected.shape, projected.dtype),
            pltpu.SemaphoreType.DMA((4,)),
        ],
        compiler_params=pltpu.CompilerParams(vmem_limit_bytes=6 * MIB),
        name="pick_rows",
    )(place, *in_hbm(from_shard, from_slot, projected, states))


def relay_kernel(from_0, from_1, _, lead_1, lead_0, rest_1, rest_0):
    dim = from_1.shape[1]
    heads = rest_0.shape[0] // dim + EARLY
    rows, early = heads * dim, EARLY * dim
    tile_rows = heads * TILE
    for source, other, lead, rest in (
        (from_0, from_1, lead_1, rest_1),
        (from_1, from_0, lead_0, rest_0),
    ):
        for head in range(heads):
            part = slice(head * TILE, (head + 1) * TILE)
            query = other[rows + head * TILE : rows + (head + 1) * TILE]
            state = source[head * dim : (head + 1) * dim]
            lead[part] = products(query, state)
            if head < EARLY:
                lead[tile_rows + head * dim : tile_rows + (head + 1) * dim] = state
            else:
                rest[(head - EARLY) * dim : (head - EARLY + 1) * dim] = state


def relay(from_0, from_1, after, heads):
    dim = from_0.shape[1]
    lead = jax.ShapeDtypeStruct((heads * TILE + EARLY * dim, dim), F32)
    rest = jax.ShapeDtypeStruct(((heads - EARLY) * dim, dim), F32)
    return pl.pallas_call(
        relay_kernel,
        out_shape=[lead, lead, rest, rest],
        in_specs=[VMEM] * 3,
        out_specs=[VMEM] * 4,
        compiler_params=pltpu.CompilerParams(vmem_limit_bytes=6 * MIB),
        name="relay_rows",
    )(from_0, from_1, after)


def gap_of(row, shards, live, device, shard_ref):
    return lax.rem(device - shard_ref[device * live + row] + shards, shards)


def at_stride(gap, stride, shards, side):
    return gap == lax.rem(stride * side + shards, shards)


def slot_for(stride, shards, live, device, side, shard_ref, slot_ref):
    target = lax.rem(device + stride * side + shards, shards)
    slot = jnp.int32(0)
    for row in range(live):
        mine = shard_ref[target * live + row] == device
        slot = jnp.where(mine, slot_ref[target * live + row], slot)
    return slot


def prepare_kernel(
    shards, live, group, strides, place, shard_ref, slot_ref, projected, rate, gain, states,
    query, grown, base, gated, decay, made, here, outer, token, *refs,
):
    outs, parts = refs[:-1], refs[-1]
    token[...] = jnp.zeros_like(token)
    rows, dim = here.shape[1:]
    heads = rows // dim
    steps = projected.shape[0]
    device, side = spot(place, group)
    for n, stride in enumerate(strides):
        slot = slot_for(stride, shards, live, device, side, shard_ref, slot_ref)
        outs[n][...] = states[slot]
    for row in range(live):
        here[row] = states[slot_ref[device * live + row]]
    parts[...] = jnp.zeros_like(parts)
    for step in range(steps):
        for row in range(live):
            block = projected[step, row].astype(F32)
            at = step * live + row
            for n in range(parts.shape[0]):
                parts[n, at : at + 1] = block[n : n + 1]
    queries, keys, values = (jax.nn.silu(parts[n]) for n in range(3))
    index = lax.broadcasted_iota(jnp.int32, queries.shape, 0)
    step_of = (index // live).astype(F32)
    rates = jnp.broadcast_to(rate[...], queries.shape)
    query[...] = queries
    gated[...] = jax.nn.sigmoid(parts[3]) * gain[...]
    grown[...] = jnp.exp(-rates * (step_of + 1.0))
    decay[...] = jnp.exp(-steps * rate[...])
    faded = keys * jnp.exp(-rates * jnp.maximum(steps - 1.0 - step_of, 0.0))
    later = lambda x, count: jnp.concatenate(
        [jnp.zeros((count, rows), F32), x[: TILE - count]], axis=0
    )
    total = jnp.zeros_like(queries)
    for lag in range(steps):
        key = later(keys, lag * live) if lag else keys
        value = later(values, lag * live) if lag else values
        product = queries * key
        match = jnp.concatenate(
            [
                jnp.broadcast_to(
                    jnp.sum(
                        product[:, head * dim : (head + 1) * dim], axis=1, keepdims=True
                    ),
                    (TILE, dim),
                )
                for head in range(heads)
            ],
            axis=1,
        )
        total = total + jnp.exp(-rates * float(lag)) * match * value
    base[...] = total

    def halves(x):
        high = x.astype(BF16).astype(F32)
        return high, x - high

    nothing = jnp.zeros_like(queries)
    v_high, v_low = halves(values)
    right = jnp.concatenate([v_high, v_high, v_low, nothing], axis=0).astype(BF16)
    for row in range(live):
        k_high, k_low = halves(jnp.where(lax.rem(index, live) == row, faded, 0.0))
        left = jnp.concatenate([k_high, k_low, k_high, nothing], axis=0).astype(BF16)
        for head in range(heads):
            span = slice(head * dim, (head + 1) * dim)
            outer[row, span] = lax.dot_general(
                left[:, span],
                right[:, span],
                (((0,), (0,)), ((), ())),
                preferred_element_type=F32,
            )
    for row in range(live):
        for head in range(heads):
            span = slice(head * dim, (head + 1) * dim)
            made[row, head * TILE : (head + 1) * TILE] = products(
                queries[:, span], here[row, span]
            )


def prepare(
    place, from_shard, from_slot, projected, rate, gain, states, shards, live, group, strides
):
    rows, dim = states.shape[1:]
    tile = jax.ShapeDtypeStruct((TILE, rows), F32)
    whole = jax.ShapeDtypeStruct((live, rows, dim), F32)
    return pl.pallas_call(
        functools.partial(prepare_kernel, shards, live, group, strides),
        out_shape=[tile] * 4
        + [
            jax.ShapeDtypeStruct((1, rows), F32),
            jax.ShapeDtypeStruct((live, rows // dim * TILE, dim), F32),
            whole,
            whole,
            jax.ShapeDtypeStruct((TILE, dim), F32),
        ]
        + [jax.ShapeDtypeStruct((rows, dim), F32)] * len(strides),
        in_specs=[SMEM] * 3 + [VMEM] * 4,
        out_specs=[VMEM] * (9 + len(strides)),
        scratch_shapes=[pltpu.VMEM((projected.shape[2], TILE, rows), F32)],
        compiler_params=pltpu.CompilerParams(vmem_limit_bytes=8 * MIB),
        name="prepare_rows",
    )(place, from_shard, from_slot, projected, rate, gain, states)


def diagonal(dim):
    row = lax.broadcasted_iota(jnp.int32, (TILE, dim), 0)
    return row == lax.broadcasted_iota(jnp.int32, (TILE, dim), 1)


def raw_kernel(
    shards, live, group, place, shard_ref, lead_0, lead_1, near_1, near_0,
    local, query, grown, base, raw, sums, made, tiles, sem,
):
    rows, dim = near_0.shape
    heads = rows // dim
    tile_rows = heads * TILE
    for row in range(live):
        made[row] = local[row]
    for n, near in enumerate((near_1, near_0)):
        for head in range(heads):
            span = slice(head * dim, (head + 1) * dim)
            made[live + n, head * TILE : (head + 1) * TILE] = products(
                query[:, span], near[span]
            )
    for n, lead in enumerate((lead_1, lead_0)):
        made[live + 2 + n] = lead[0:tile_rows]
    picks = []
    device, side = spot(place, group)
    for row in range(live):
        gap = gap_of(row, shards, live, device, shard_ref)
        index = jnp.int32(row)
        for n, stride in enumerate((-1, 1, -2, 2)):
            index = jnp.where(at_stride(gap, stride, shards, side), live + n, index)
        picks.append(index)
    which = lax.rem(lax.broadcasted_iota(jnp.int32, (TILE, dim), 0), live)
    total = jnp.zeros((TILE, dim), F32)
    for head in range(heads):
        span = slice(head * dim, (head + 1) * dim)
        part = slice(head * TILE, (head + 1) * TILE)
        tile = made[picks[0], part]
        for row in range(1, live):
            tile = jnp.where(which == row, made[picks[row], part], tile)
        tile = tile * grown[:, span] + base[:, span]
        raw[:, span] = tile
        total = total + tile * tile
    total = jnp.broadcast_to(jnp.sum(total, axis=1, keepdims=True), (TILE, dim))
    total = jnp.sum(jnp.where(diagonal(dim), total, 0.0), axis=0, keepdims=True)
    for peer in range(sums.shape[0]):
        tiles[peer] = total
    copy = pltpu.make_async_copy(tiles, sums, sem)
    copy.start()
    copy.wait()


def raw_of(place, from_shard, arrived, small, shards, live, group):
    rows, dim = arrived[-1].shape
    return pl.pallas_call(
        functools.partial(raw_kernel, shards, live, group),
        out_shape=[
            jax.ShapeDtypeStruct((TILE, rows), F32),
            jax.ShapeDtypeStruct((group, 1, dim), F32),
        ],
        in_specs=[SMEM] * 2 + [VMEM] * (len(arrived) + len(small)),
        out_specs=[VMEM, HBM],
        scratch_shapes=[
            pltpu.VMEM((live + 4, rows // dim * TILE, dim), F32),
            pltpu.VMEM((group, 1, dim), F32),
            pltpu.SemaphoreType.DMA(()),
        ],
        compiler_params=pltpu.CompilerParams(vmem_limit_bytes=6 * MIB),
        cost_estimate=pl.CostEstimate(flops=10**12, bytes_accessed=MIB, transcendentals=0),
        name="raw_rows",
    )(place, from_shard, *arrived, *small)


def final_kernel(
    shards, live, group, place, shard_ref, here, lead_0, lead_1, near_1, near_0,
    rest_1, rest_0, outer, decay, final, token, held, made, sems_in, sems,
):
    rows, dim = here.shape[1:]
    heads = rows // dim
    early, tile_rows = EARLY * dim, heads * TILE
    device, side = spot(place, group)
    token[...] = jnp.zeros_like(token)

    def loads(row, lead, rest):
        return [
            pltpu.make_async_copy(
                lead.at[tile_rows : tile_rows + early],
                held.at[row, 0:early],
                sems_in.at[row, 0],
            ),
            pltpu.make_async_copy(rest, held.at[row, early:rows], sems_in.at[row, 1]),
        ]

    cases = []
    for row in range(live):
        gap = gap_of(row, shards, live, device, shard_ref)
        far_0 = at_stride(gap, 2, shards, side)
        far_1 = at_stride(gap, -2, shards, side)
        for found, lead, rest in ((far_0, lead_0, rest_0), (far_1, lead_1, rest_1)):

            @pl.when(found)
            def _():
                start_all(loads(row, lead, rest))

        cases.append(
            [
                (gap == 0, here.at[row]),
                (at_stride(gap, 1, shards, side), near_0),
                (at_stride(gap, -1, shards, side), near_1),
                (jnp.logical_or(far_0, far_1), held.at[row]),
            ]
        )
    copies = []
    for row in range(live):

        @pl.when(cases[row][3][0])
        def _():
            wait_all(loads(row, lead_0, rest_0))

        for half in range(2):
            span = range(half * heads // 2, (half + 1) * heads // 2)
            for found, source in cases[row]:

                @pl.when(found)
                def _():
                    for head in span:
                        block = slice(head * dim, (head + 1) * dim)
                        made[row, block] = (
                            decay[:, block] * source[block] + outer[row, block]
                        )

            block = slice(span.start * dim, span.stop * dim)
            copy = pltpu.make_async_copy(
                made.at[row, block], final.at[row, block], sems.at[row, half]
            )
            copy.start()
            copies.append(copy)
    wait_all(copies)


def final_of(place, from_shard, here, lead, near, rest, small, shards, live, group):
    rows, dim = here.shape[1:]
    return pl.pallas_call(
        functools.partial(final_kernel, shards, live, group),
        out_shape=[
            jax.ShapeDtypeStruct((live, rows, dim), F32),
            jax.ShapeDtypeStruct((TILE, dim), F32),
        ],
        in_specs=[SMEM] * 2 + [VMEM] + [HBM] * 2 + [VMEM] * 2 + [HBM] * 2 + [VMEM] * 2,
        out_specs=[pl.BlockSpec(memory_space=pl.ANY), VMEM],
        scratch_shapes=[
            pltpu.VMEM((live, rows, dim), F32),
            pltpu.VMEM((live, rows, dim), F32),
            pltpu.SemaphoreType.DMA((live, 2)),
            pltpu.SemaphoreType.DMA((live, 2)),
        ],
        compiler_params=pltpu.CompilerParams(vmem_limit_bytes=8 * MIB),
        cost_estimate=pl.CostEstimate(flops=10**10, bytes_accessed=MIB, transcendentals=0),
        name="final_rows",
    )(place, from_shard, here, *in_hbm(*lead), *near, *in_hbm(*rest), *small)


def attend_kernel(live, features, totals, raw, gated, _, attended):
    dim = totals.shape[2]
    total = totals[0]
    for peer in range(1, totals.shape[0]):
        total = total + totals[peer]
    total = jnp.where(diagonal(dim), jnp.broadcast_to(total, (TILE, dim)), 0.0)
    total = jnp.sum(total, axis=1, keepdims=True)
    scale = jnp.broadcast_to(lax.rsqrt(total / features + EPS), raw.shape)
    tile = raw[...] * scale * gated[...]
    for step in range(attended.shape[0]):
        attended[step] = tile[step * live : (step + 1) * live].astype(BF16)


def attend(totals, raw, gated, after, live, steps, features):
    return pl.pallas_call(
        functools.partial(attend_kernel, live, features),
        out_shape=jax.ShapeDtypeStruct((steps, live, raw.shape[1]), BF16),
        in_specs=[VMEM] * 4,
        out_specs=VMEM,
        compiler_params=pltpu.CompilerParams(vmem_limit_bytes=4 * MIB),
        name="attend_rows",
    )(totals, raw, gated, after)


def on_device(states, from_shard, from_slot, projected, decay_rate, norm_gain):
    shards, group = lax.axis_size("dp"), lax.axis_size("tensor")
    steps, live = projected.shape[:2]
    slots, heads, dim = states.shape[:3]
    width = heads * dim
    place = lax.axis_index(("dp", "tensor")).astype(jnp.int32).reshape(1)
    states = states.reshape(slots, width, dim)

    row_0, row_1, staged = pick(
        place, from_shard, from_slot, projected, states, shards, live, group, (-2, 2)
    )
    half_1, half_0 = swapped(row_1, 1), swapped(row_0, 0)
    rate = jnp.repeat(decay_rate, dim).reshape(1, width)
    gain = norm_gain.reshape(1, width)
    query, grown, base, gated, decay, local, here, outer, token, row_0, row_1 = prepare(
        place, from_shard, from_slot, projected, rate, gain, staged, shards, live,
        group, (-1, 1),
    )
    near_1, near_0 = swapped(row_1, 1), swapped(row_0, 0)
    sent = relay(half_0, half_1, token, heads)
    lead_1, lead_0 = swapped(sent[0], 1), swapped(sent[1], 0)
    rest_1, rest_0 = swapped(sent[2], 1), swapped(sent[3], 0)

    raw, sums = raw_of(
        place, from_shard, (lead_0, lead_1, near_1, near_0),
        (local, query, grown, base), shards, live, group,
    )
    totals = lax.all_to_all(sums, "tensor", 0, 0)
    final, token = final_of(
        place, from_shard, here, (lead_0, lead_1), (near_1, near_0), (rest_1, rest_0),
        (outer, decay), shards, live, group,
    )
    attended = attend(totals, raw, gated, token, live, steps, width * group)
    return attended, final.reshape(live, heads, dim, dim)


def solution(mesh):
    return jax.shard_map(
        on_device,
        mesh=mesh,
        in_specs=(
            P("dp", "tensor", None, None),
            P(),
            P(),
            P(None, "dp", None, "tensor"),
            P("tensor"),
            P("tensor"),
        ),
        out_specs=(P(None, "dp", "tensor"), P("dp", "tensor", None, None)),
        check_vma=False,
    )
```

```python
import functools
import jax
import jax.numpy as jnp
from jax import lax
from jax.experimental import pallas as pl
from jax.experimental.pallas import tpu as pltpu
from jax.sharding import PartitionSpec as P

EPS = 1e-05
F32 = jnp.float32
BF16 = jnp.bfloat16
EARLY = 3
TILE = 8
MIB = 1024 * 1024
SMEM = pl.BlockSpec(memory_space=pltpu.SMEM)
VMEM = pl.BlockSpec(memory_space=pltpu.VMEM)
HBM = pl.BlockSpec(memory_space=pltpu.HBM)


def swapped(block, first):
    shards, group = lax.axis_size("dp"), lax.axis_size("tensor")
    route = []
    for i in range(0, shards, 2):
        for j in range(group):
            low = (first + j % 2 + i) % shards
            high = (low + 1) % shards
            route += [
                (low * group + j, high * group + j),
                (high * group + j, low * group + j),
            ]
    return lax.ppermute(block, ("dp", "tensor"), route)


def spot(place, group):
    shard = lax.div(place[0], group)
    return shard, 2 * ((shard ^ lax.rem(place[0], group)) & 1) - 1


def start_all(copies):
    for copy in copies:
        copy.start()


def wait_all(copies):
    for copy in copies:
        copy.wait()


def in_hbm(*arrays):
    return [pltpu.with_memory_space_constraint(x, pltpu.HBM) for x in arrays]


def products(query, state):
    q_high = query.astype(BF16).astype(F32)
    both = jnp.concatenate([q_high, query - q_high], axis=0).astype(BF16)
    high = state.astype(BF16)
    low = (state - high.astype(F32)).astype(BF16)
    first = jnp.dot(both, high, preferred_element_type=F32)
    second = jnp.dot(both, low, preferred_element_type=F32)
    return first[:TILE] + first[TILE:] + second[:TILE]


def pick_kernel(shards, live, group, strides, place, shard_hbm, slot_hbm, projected, states, *refs):
    n_rows = 2
    outs = refs[: len(strides)]
    refs = refs[len(strides) :]
    staged, shard_ref, slot_ref, inputs, sems = refs
    dim = outs[0].shape[1]
    rows = states.shape[1]
    device, side = spot(place, group)
    copies = [
        pltpu.make_async_copy(shard_hbm, shard_ref, sems.at[0]),
        pltpu.make_async_copy(slot_hbm, slot_ref, sems.at[1]),
        pltpu.make_async_copy(projected, inputs, sems.at[2]),
        pltpu.make_async_copy(states, staged, sems.at[3]),
    ]
    start_all(copies)
    tile_rows = rows // dim * TILE
    for n in range(n_rows):
        outs[n][rows : rows + tile_rows] = jnp.zeros((tile_rows, dim), F32)
    copies[2].wait()
    for step in range(inputs.shape[0]):
        for row in range(live):
            query = jax.nn.silu(inputs[step, row].astype(F32))[0:1]
            for head in range(rows // dim):
                at = rows + head * TILE + step * live + row
                part = query[:, head * dim : (head + 1) * dim]
                for n in range(n_rows):
                    outs[n][at : at + 1] = part
    wait_all(copies[:2])
    slots = [
        slot_for(stride, shards, live, device, side, shard_ref, slot_ref)
        for stride in strides
    ]
    copies[3].wait()
    for n, slot in enumerate(slots):
        outs[n][0:rows] = staged[slot]


def pick(place, from_shard, from_slot, projected, states, shards, live, group, strides):
    rows, dim = states.shape[1:]
    tile_rows = rows // dim * TILE
    return pl.pallas_call(
        functools.partial(pick_kernel, shards, live, group, strides),
        out_shape=[jax.ShapeDtypeStruct((rows + tile_rows, dim), F32)] * 2
        + [jax.ShapeDtypeStruct((rows, dim), F32)] * (len(strides) - 2)
        + [jax.ShapeDtypeStruct(states.shape, F32)],
        in_specs=[SMEM] + [HBM] * 4,
        out_specs=[VMEM] * (len(strides) + 1),
        scratch_shapes=[
            pltpu.SMEM(from_shard.shape, jnp.int32),
            pltpu.SMEM(from_slot.shape, jnp.int32),
            pltpu.VMEM(projected.shape, projected.dtype),
            pltpu.SemaphoreType.DMA((4,)),
        ],
        compiler_params=pltpu.CompilerParams(vmem_limit_bytes=6 * MIB),
        name="pick_rows",
    )(place, *in_hbm(from_shard, from_slot, projected, states))


def relay_kernel(from_0, from_1, _, lead_1, lead_0, rest_1, rest_0):
    dim = from_1.shape[1]
    heads = rest_0.shape[0] // dim + EARLY
    rows, early = heads * dim, EARLY * dim
    tile_rows = heads * TILE
    for source, other, lead, rest in (
        (from_0, from_1, lead_1, rest_1),
        (from_1, from_0, lead_0, rest_0),
    ):
        for head in range(heads):
            part = slice(head * TILE, (head + 1) * TILE)
            query = other[rows + head * TILE : rows + (head + 1) * TILE]
            state = source[head * dim : (head + 1) * dim]
            lead[part] = products(query, state)
            if head < EARLY:
                lead[tile_rows + head * dim : tile_rows + (head + 1) * dim] = state
            else:
                rest[(head - EARLY) * dim : (head - EARLY + 1) * dim] = state


def relay(from_0, from_1, after, heads):
    dim = from_0.shape[1]
    lead = jax.ShapeDtypeStruct((heads * TILE + EARLY * dim, dim), F32)
    rest = jax.ShapeDtypeStruct(((heads - EARLY) * dim, dim), F32)
    return pl.pallas_call(
        relay_kernel,
        out_shape=[lead, lead, rest, rest],
        in_specs=[VMEM] * 3,
        out_specs=[VMEM] * 4,
        compiler_params=pltpu.CompilerParams(vmem_limit_bytes=6 * MIB),
        name="relay_rows",
    )(from_0, from_1, after)


def gap_of(row, shards, live, device, shard_ref):
    return lax.rem(device - shard_ref[device * live + row] + shards, shards)


def at_stride(gap, stride, shards, side):
    return gap == lax.rem(stride * side + shards, shards)


def slot_for(stride, shards, live, device, side, shard_ref, slot_ref):
    target = lax.rem(device + stride * side + shards, shards)
    slot = jnp.int32(0)
    for row in range(live):
        mine = shard_ref[target * live + row] == device
        slot = jnp.where(mine, slot_ref[target * live + row], slot)
    return slot


def prepare_kernel(
    shards, live, group, strides, place, shard_ref, slot_ref, projected, rate, gain, _, states,
    query, grown, base, gated, decay, made, here, outer, token, *refs,
):
    outs, parts = refs[:-1], refs[-1]
    token[...] = jnp.zeros_like(token)
    rows, dim = here.shape[1:]
    heads = rows // dim
    steps = projected.shape[0]
    device, side = spot(place, group)
    for n, stride in enumerate(strides):
        slot = slot_for(stride, shards, live, device, side, shard_ref, slot_ref)
        outs[n][...] = states[slot]
    for row in range(live):
        here[row] = states[slot_ref[device * live + row]]
    parts[...] = jnp.zeros_like(parts)
    for step in range(steps):
        for row in range(live):
            block = projected[step, row].astype(F32)
            at = step * live + row
            for n in range(parts.shape[0]):
                parts[n, at : at + 1] = block[n : n + 1]
    queries, keys, values = (jax.nn.silu(parts[n]) for n in range(3))
    index = lax.broadcasted_iota(jnp.int32, queries.shape, 0)
    step_of = (index // live).astype(F32)
    rates = jnp.broadcast_to(rate[...], queries.shape)
    query[...] = queries
    gated[...] = jax.nn.sigmoid(parts[3]) * gain[...]
    grown[...] = jnp.exp(-rates * (step_of + 1.0))
    decay[...] = jnp.exp(-steps * rate[...])
    faded = keys * jnp.exp(-rates * jnp.maximum(steps - 1.0 - step_of, 0.0))
    later = lambda x, count: jnp.concatenate(
        [jnp.zeros((count, rows), F32), x[: TILE - count]], axis=0
    )
    total = jnp.zeros_like(queries)
    for lag in range(steps):
        key = later(keys, lag * live) if lag else keys
        value = later(values, lag * live) if lag else values
        product = queries * key
        match = jnp.concatenate(
            [
                jnp.broadcast_to(
                    jnp.sum(
                        product[:, head * dim : (head + 1) * dim], axis=1, keepdims=True
                    ),
                    (TILE, dim),
                )
                for head in range(heads)
            ],
            axis=1,
        )
        total = total + jnp.exp(-rates * float(lag)) * match * value
    base[...] = total

    def halves(x):
        high = x.astype(BF16).astype(F32)
        return high, x - high

    nothing = jnp.zeros_like(queries)
    v_high, v_low = halves(values)
    right = jnp.concatenate([v_high, v_high, v_low, nothing], axis=0).astype(BF16)
    for row in range(live):
        k_high, k_low = halves(jnp.where(lax.rem(index, live) == row, faded, 0.0))
        left = jnp.concatenate([k_high, k_low, k_high, nothing], axis=0).astype(BF16)
        for head in range(heads):
            span = slice(head * dim, (head + 1) * dim)
            outer[row, span] = lax.dot_general(
                left[:, span],
                right[:, span],
                (((0,), (0,)), ((), ())),
                preferred_element_type=F32,
            )
    for row in range(live):
        for head in range(heads):
            span = slice(head * dim, (head + 1) * dim)
            made[row, head * TILE : (head + 1) * TILE] = products(
                queries[:, span], here[row, span]
            )


def prepare(
    place, from_shard, from_slot, projected, rate, gain, after, states, shards, live, group, strides
):
    rows, dim = states.shape[1:]
    tile = jax.ShapeDtypeStruct((TILE, rows), F32)
    whole = jax.ShapeDtypeStruct((live, rows, dim), F32)
    return pl.pallas_call(
        functools.partial(prepare_kernel, shards, live, group, strides),
        out_shape=[tile] * 4
        + [
            jax.ShapeDtypeStruct((1, rows), F32),
            jax.ShapeDtypeStruct((live, rows // dim * TILE, dim), F32),
            whole,
            whole,
            jax.ShapeDtypeStruct((TILE, dim), F32),
        ]
        + [jax.ShapeDtypeStruct((rows, dim), F32)] * len(strides),
        in_specs=[SMEM] * 3 + [VMEM] * 5,
        out_specs=[VMEM] * (9 + len(strides)),
        scratch_shapes=[pltpu.VMEM((projected.shape[2], TILE, rows), F32)],
        compiler_params=pltpu.CompilerParams(vmem_limit_bytes=8 * MIB),
        name="prepare_rows",
    )(place, from_shard, from_slot, projected, rate, gain, after, states)


def diagonal(dim):
    row = lax.broadcasted_iota(jnp.int32, (TILE, dim), 0)
    return row == lax.broadcasted_iota(jnp.int32, (TILE, dim), 1)


def raw_kernel(
    shards, live, group, place, shard_ref, lead_0, lead_1, near_1, near_0,
    local, query, grown, base, raw, sums, made, tiles, sem,
):
    rows, dim = near_0.shape
    heads = rows // dim
    tile_rows = heads * TILE
    for row in range(live):
        made[row] = local[row]
    for n, near in enumerate((near_1, near_0)):
        for head in range(heads):
            span = slice(head * dim, (head + 1) * dim)
            made[live + n, head * TILE : (head + 1) * TILE] = products(
                query[:, span], near[span]
            )
    for n, lead in enumerate((lead_1, lead_0)):
        made[live + 2 + n] = lead[0:tile_rows]
    picks = []
    device, side = spot(place, group)
    for row in range(live):
        gap = gap_of(row, shards, live, device, shard_ref)
        index = jnp.int32(row)
        for n, stride in enumerate((-1, 1, -2, 2)):
            index = jnp.where(at_stride(gap, stride, shards, side), live + n, index)
        picks.append(index)
    which = lax.rem(lax.broadcasted_iota(jnp.int32, (TILE, dim), 0), live)
    total = jnp.zeros((TILE, dim), F32)
    for head in range(heads):
        span = slice(head * dim, (head + 1) * dim)
        part = slice(head * TILE, (head + 1) * TILE)
        tile = made[picks[0], part]
        for row in range(1, live):
            tile = jnp.where(which == row, made[picks[row], part], tile)
        tile = tile * grown[:, span] + base[:, span]
        raw[:, span] = tile
        total = total + tile * tile
    total = jnp.broadcast_to(jnp.sum(total, axis=1, keepdims=True), (TILE, dim))
    total = jnp.sum(jnp.where(diagonal(dim), total, 0.0), axis=0, keepdims=True)
    for peer in range(sums.shape[0]):
        tiles[peer] = total
    copy = pltpu.make_async_copy(tiles, sums, sem)
    copy.start()
    copy.wait()


def raw_of(place, from_shard, arrived, small, shards, live, group):
    rows, dim = arrived[-1].shape
    return pl.pallas_call(
        functools.partial(raw_kernel, shards, live, group),
        out_shape=[
            jax.ShapeDtypeStruct((TILE, rows), F32),
            jax.ShapeDtypeStruct((group, 1, dim), F32),
        ],
        in_specs=[SMEM] * 2 + [VMEM] * (len(arrived) + len(small)),
        out_specs=[VMEM, HBM],
        scratch_shapes=[
            pltpu.VMEM((live + 4, rows // dim * TILE, dim), F32),
            pltpu.VMEM((group, 1, dim), F32),
            pltpu.SemaphoreType.DMA(()),
        ],
        compiler_params=pltpu.CompilerParams(vmem_limit_bytes=6 * MIB),
        cost_estimate=pl.CostEstimate(flops=10**12, bytes_accessed=MIB, transcendentals=0),
        name="raw_rows",
    )(place, from_shard, *arrived, *small)


def final_kernel(
    shards, live, group, place, shard_ref, here, lead_0, lead_1, near_1, near_0,
    rest_1, rest_0, outer, decay, final, token, held, made, sems_in, sems,
):
    rows, dim = here.shape[1:]
    heads = rows // dim
    early, tile_rows = EARLY * dim, heads * TILE
    device, side = spot(place, group)
    token[...] = jnp.zeros_like(token)

    def loads(row, lead, rest):
        return [
            pltpu.make_async_copy(
                lead.at[tile_rows : tile_rows + early],
                held.at[row, 0:early],
                sems_in.at[row, 0],
            ),
            pltpu.make_async_copy(rest, held.at[row, early:rows], sems_in.at[row, 1]),
        ]

    cases = []
    for row in range(live):
        gap = gap_of(row, shards, live, device, shard_ref)
        far_0 = at_stride(gap, 2, shards, side)
        far_1 = at_stride(gap, -2, shards, side)
        for found, lead, rest in ((far_0, lead_0, rest_0), (far_1, lead_1, rest_1)):

            @pl.when(found)
            def _():
                start_all(loads(row, lead, rest))

        cases.append(
            [
                (gap == 0, here.at[row]),
                (at_stride(gap, 1, shards, side), near_0),
                (at_stride(gap, -1, shards, side), near_1),
                (jnp.logical_or(far_0, far_1), held.at[row]),
            ]
        )
    copies = []
    for row in range(live):

        @pl.when(cases[row][3][0])
        def _():
            wait_all(loads(row, lead_0, rest_0))

        for half in range(2):
            span = range(half * heads // 2, (half + 1) * heads // 2)
            for found, source in cases[row]:

                @pl.when(found)
                def _():
                    for head in span:
                        block = slice(head * dim, (head + 1) * dim)
                        made[row, block] = (
                            decay[:, block] * source[block] + outer[row, block]
                        )

            block = slice(span.start * dim, span.stop * dim)
            copy = pltpu.make_async_copy(
                made.at[row, block], final.at[row, block], sems.at[row, half]
            )
            copy.start()
            copies.append(copy)
    wait_all(copies)


def final_of(place, from_shard, here, lead, near, rest, small, shards, live, group):
    rows, dim = here.shape[1:]
    return pl.pallas_call(
        functools.partial(final_kernel, shards, live, group),
        out_shape=[
            jax.ShapeDtypeStruct((live, rows, dim), F32),
            jax.ShapeDtypeStruct((TILE, dim), F32),
        ],
        in_specs=[SMEM] * 2 + [VMEM] + [HBM] * 2 + [VMEM] * 2 + [HBM] * 2 + [VMEM] * 2,
        out_specs=[pl.BlockSpec(memory_space=pl.ANY), VMEM],
        scratch_shapes=[
            pltpu.VMEM((live, rows, dim), F32),
            pltpu.VMEM((live, rows, dim), F32),
            pltpu.SemaphoreType.DMA((live, 2)),
            pltpu.SemaphoreType.DMA((live, 2)),
        ],
        compiler_params=pltpu.CompilerParams(vmem_limit_bytes=8 * MIB),
        cost_estimate=pl.CostEstimate(flops=10**10, bytes_accessed=MIB, transcendentals=0),
        name="final_rows",
    )(place, from_shard, here, *in_hbm(*lead), *near, *in_hbm(*rest), *small)


def attend_kernel(live, features, totals, raw, gated, _, attended):
    dim = totals.shape[2]
    total = totals[0]
    for peer in range(1, totals.shape[0]):
        total = total + totals[peer]
    total = jnp.where(diagonal(dim), jnp.broadcast_to(total, (TILE, dim)), 0.0)
    total = jnp.sum(total, axis=1, keepdims=True)
    scale = jnp.broadcast_to(lax.rsqrt(total / features + EPS), raw.shape)
    tile = raw[...] * scale * gated[...]
    for step in range(attended.shape[0]):
        attended[step] = tile[step * live : (step + 1) * live].astype(BF16)


def attend(totals, raw, gated, after, live, steps, features):
    return pl.pallas_call(
        functools.partial(attend_kernel, live, features),
        out_shape=jax.ShapeDtypeStruct((steps, live, raw.shape[1]), BF16),
        in_specs=[VMEM] * 4,
        out_specs=VMEM,
        compiler_params=pltpu.CompilerParams(vmem_limit_bytes=4 * MIB),
        name="attend_rows",
    )(totals, raw, gated, after)


def on_device(states, from_shard, from_slot, projected, decay_rate, norm_gain):
    shards, group = lax.axis_size("dp"), lax.axis_size("tensor")
    steps, live = projected.shape[:2]
    slots, heads, dim = states.shape[:3]
    width = heads * dim
    place = lax.axis_index(("dp", "tensor")).astype(jnp.int32).reshape(1)
    states = states.reshape(slots, width, dim)

    row_0, row_1, next_1, staged = pick(
        place, from_shard, from_slot, projected, states, shards, live, group, (-2, 2, 1)
    )
    half_1, half_0 = swapped(row_1, 1), swapped(row_0, 0)
    rate = jnp.repeat(decay_rate, dim).reshape(1, width)
    gain = norm_gain.reshape(1, width)
    query, grown, base, gated, decay, local, here, outer, token, next_0 = prepare(
        place, from_shard, from_slot, projected, rate, gain, half_0, staged, shards, live,
        group, (-1,),
    )
    near_1, near_0 = swapped(next_1, 1), swapped(next_0, 0)
    sent = relay(half_0, half_1, token, heads)
    lead_1, lead_0 = swapped(sent[0], 1), swapped(sent[1], 0)
    rest_1, rest_0 = swapped(sent[2], 1), swapped(sent[3], 0)

    raw, sums = raw_of(
        place, from_shard, (lead_0, lead_1, near_1, near_0),
        (local, query, grown, base), shards, live, group,
    )
    totals = lax.all_to_all(sums, "tensor", 0, 0)
    final, token = final_of(
        place, from_shard, here, (lead_0, lead_1), (near_1, near_0), (rest_1, rest_0),
        (outer, decay), shards, live, group,
    )
    attended = attend(totals, raw, gated, token, live, steps, width * group)
    return attended, final.reshape(live, heads, dim, dim)


def solution(mesh):
    return jax.shard_map(
        on_device,
        mesh=mesh,
        in_specs=(
            P("dp", "tensor", None, None),
            P(),
            P(),
            P(None, "dp", None, "tensor"),
            P("tensor"),
            P("tensor"),
        ),
        out_specs=(P(None, "dp", "tensor"), P("dp", "tensor", None, None)),
        check_vma=False,
    )
```

```python
import functools
import jax
import jax.numpy as jnp
from jax import lax
from jax.experimental import pallas as pl
from jax.experimental.pallas import tpu as pltpu
from jax.sharding import PartitionSpec as P

EPS = 1e-05
F32 = jnp.float32
BF16 = jnp.bfloat16
EARLY = 3
TILE = 8
MIB = 1024 * 1024
SMEM = pl.BlockSpec(memory_space=pltpu.SMEM)
VMEM = pl.BlockSpec(memory_space=pltpu.VMEM)
HBM = pl.BlockSpec(memory_space=pltpu.HBM)


def swapped(block, first):
    shards, group = lax.axis_size("dp"), lax.axis_size("tensor")
    route = []
    for i in range(0, shards, 2):
        for j in range(group):
            low = (first + j % 2 + i) % shards
            high = (low + 1) % shards
            route += [
                (low * group + j, high * group + j),
                (high * group + j, low * group + j),
            ]
    return lax.ppermute(block, ("dp", "tensor"), route)


def spot(place, group):
    shard = lax.div(place[0], group)
    return shard, 2 * ((shard ^ lax.rem(place[0], group)) & 1) - 1


def start_all(copies):
    for copy in copies:
        copy.start()


def wait_all(copies):
    for copy in copies:
        copy.wait()


def in_hbm(*arrays):
    return [pltpu.with_memory_space_constraint(x, pltpu.HBM) for x in arrays]


def products(query, state):
    q_high = query.astype(BF16).astype(F32)
    both = jnp.concatenate([q_high, query - q_high], axis=0).astype(BF16)
    high = state.astype(BF16)
    low = (state - high.astype(F32)).astype(BF16)
    first = jnp.dot(both, high, preferred_element_type=F32)
    second = jnp.dot(both, low, preferred_element_type=F32)
    return first[:TILE] + first[TILE:] + second[:TILE]


def pick_kernel(shards, live, group, strides, place, shard_hbm, slot_hbm, projected, states, *refs):
    n_rows = 2
    outs = refs[: len(strides)]
    refs = refs[len(strides) :]
    staged, shard_ref, slot_ref, inputs, sems = refs
    dim = outs[0].shape[1]
    rows = states.shape[1]
    device, side = spot(place, group)
    copies = [
        pltpu.make_async_copy(shard_hbm, shard_ref, sems.at[0]),
        pltpu.make_async_copy(slot_hbm, slot_ref, sems.at[1]),
        pltpu.make_async_copy(projected, inputs, sems.at[2]),
        pltpu.make_async_copy(states, staged, sems.at[3]),
    ]
    start_all(copies)
    tile_rows = rows // dim * TILE
    for n in range(n_rows):
        outs[n][rows : rows + tile_rows] = jnp.zeros((tile_rows, dim), F32)
    copies[2].wait()
    for step in range(inputs.shape[0]):
        for row in range(live):
            query = jax.nn.silu(inputs[step, row].astype(F32))[0:1]
            for head in range(rows // dim):
                at = rows + head * TILE + step * live + row
                part = query[:, head * dim : (head + 1) * dim]
                for n in range(n_rows):
                    outs[n][at : at + 1] = part
    wait_all(copies[:2])
    slots = [
        slot_for(stride, shards, live, device, side, shard_ref, slot_ref)
        for stride in strides
    ]
    copies[3].wait()
    for n, slot in enumerate(slots):
        outs[n][0:rows] = staged[slot]


def pick(place, from_shard, from_slot, projected, states, shards, live, group, strides):
    rows, dim = states.shape[1:]
    tile_rows = rows // dim * TILE
    return pl.pallas_call(
        functools.partial(pick_kernel, shards, live, group, strides),
        out_shape=[jax.ShapeDtypeStruct((rows + tile_rows, dim), F32)] * 2
        + [jax.ShapeDtypeStruct((rows, dim), F32)] * (len(strides) - 2)
        + [jax.ShapeDtypeStruct(states.shape, F32)],
        in_specs=[SMEM] + [HBM] * 4,
        out_specs=[VMEM] * (len(strides) + 1),
        scratch_shapes=[
            pltpu.SMEM(from_shard.shape, jnp.int32),
            pltpu.SMEM(from_slot.shape, jnp.int32),
            pltpu.VMEM(projected.shape, projected.dtype),
            pltpu.SemaphoreType.DMA((4,)),
        ],
        compiler_params=pltpu.CompilerParams(vmem_limit_bytes=6 * MIB),
        name="pick_rows",
    )(place, *in_hbm(from_shard, from_slot, projected, states))


def relay_kernel(from_0, from_1, near, lead_1, lead_0, rest_1, rest_0, next_row):
    dim = from_1.shape[1]
    heads = rest_0.shape[0] // dim + EARLY
    rows, early = heads * dim, EARLY * dim
    tile_rows = heads * TILE
    for source, other, lead, rest in (
        (from_0, from_1, lead_1, rest_1),
        (from_1, from_0, lead_0, rest_0),
    ):
        for head in range(heads):
            part = slice(head * TILE, (head + 1) * TILE)
            query = other[rows + head * TILE : rows + (head + 1) * TILE]
            state = source[head * dim : (head + 1) * dim]
            lead[part] = products(query, state)
            if head < EARLY:
                lead[tile_rows + head * dim : tile_rows + (head + 1) * dim] = state
            else:
                rest[(head - EARLY) * dim : (head - EARLY + 1) * dim] = state
    next_row[...] = near[...]


def relay(from_0, from_1, near, heads):
    dim = from_0.shape[1]
    lead = jax.ShapeDtypeStruct((heads * TILE + EARLY * dim, dim), F32)
    rest = jax.ShapeDtypeStruct(((heads - EARLY) * dim, dim), F32)
    return pl.pallas_call(
        relay_kernel,
        out_shape=[lead, lead, rest, rest, jax.ShapeDtypeStruct(near.shape, F32)],
        in_specs=[VMEM] * 3,
        out_specs=[VMEM] * 5,
        compiler_params=pltpu.CompilerParams(vmem_limit_bytes=6 * MIB),
        name="relay_rows",
    )(from_0, from_1, near)


def gap_of(row, shards, live, device, shard_ref):
    return lax.rem(device - shard_ref[device * live + row] + shards, shards)


def at_stride(gap, stride, shards, side):
    return gap == lax.rem(stride * side + shards, shards)


def slot_for(stride, shards, live, device, side, shard_ref, slot_ref):
    target = lax.rem(device + stride * side + shards, shards)
    slot = jnp.int32(0)
    for row in range(live):
        mine = shard_ref[target * live + row] == device
        slot = jnp.where(mine, slot_ref[target * live + row], slot)
    return slot


def prepare_kernel(
    shards, live, group, strides, place, shard_ref, slot_ref, projected, rate, gain, _, states,
    query, grown, base, gated, decay, made, here, outer, token, *refs,
):
    outs, parts = refs[:-1], refs[-1]
    token[...] = jnp.zeros_like(token)
    rows, dim = here.shape[1:]
    heads = rows // dim
    steps = projected.shape[0]
    device, side = spot(place, group)
    for n, stride in enumerate(strides):
        slot = slot_for(stride, shards, live, device, side, shard_ref, slot_ref)
        outs[n][...] = states[slot]
    for row in range(live):
        here[row] = states[slot_ref[device * live + row]]
    parts[...] = jnp.zeros_like(parts)
    for step in range(steps):
        for row in range(live):
            block = projected[step, row].astype(F32)
            at = step * live + row
            for n in range(parts.shape[0]):
                parts[n, at : at + 1] = block[n : n + 1]
    queries, keys, values = (jax.nn.silu(parts[n]) for n in range(3))
    index = lax.broadcasted_iota(jnp.int32, queries.shape, 0)
    step_of = (index // live).astype(F32)
    rates = jnp.broadcast_to(rate[...], queries.shape)
    query[...] = queries
    gated[...] = jax.nn.sigmoid(parts[3]) * gain[...]
    grown[...] = jnp.exp(-rates * (step_of + 1.0))
    decay[...] = jnp.exp(-steps * rate[...])
    faded = keys * jnp.exp(-rates * jnp.maximum(steps - 1.0 - step_of, 0.0))
    later = lambda x, count: jnp.concatenate(
        [jnp.zeros((count, rows), F32), x[: TILE - count]], axis=0
    )
    total = jnp.zeros_like(queries)
    for lag in range(steps):
        key = later(keys, lag * live) if lag else keys
        value = later(values, lag * live) if lag else values
        product = queries * key
        match = jnp.concatenate(
            [
                jnp.broadcast_to(
                    jnp.sum(
                        product[:, head * dim : (head + 1) * dim], axis=1, keepdims=True
                    ),
                    (TILE, dim),
                )
                for head in range(heads)
            ],
            axis=1,
        )
        total = total + jnp.exp(-rates * float(lag)) * match * value
    base[...] = total

    def halves(x):
        high = x.astype(BF16).astype(F32)
        return high, x - high

    nothing = jnp.zeros_like(queries)
    v_high, v_low = halves(values)
    right = jnp.concatenate([v_high, v_high, v_low, nothing], axis=0).astype(BF16)
    for row in range(live):
        k_high, k_low = halves(jnp.where(lax.rem(index, live) == row, faded, 0.0))
        left = jnp.concatenate([k_high, k_low, k_high, nothing], axis=0).astype(BF16)
        for head in range(heads):
            span = slice(head * dim, (head + 1) * dim)
            outer[row, span] = lax.dot_general(
                left[:, span],
                right[:, span],
                (((0,), (0,)), ((), ())),
                preferred_element_type=F32,
            )
    for row in range(live):
        for head in range(heads):
            span = slice(head * dim, (head + 1) * dim)
            made[row, head * TILE : (head + 1) * TILE] = products(
                queries[:, span], here[row, span]
            )


def prepare(
    place, from_shard, from_slot, projected, rate, gain, after, states, shards, live, group, strides
):
    rows, dim = states.shape[1:]
    tile = jax.ShapeDtypeStruct((TILE, rows), F32)
    whole = jax.ShapeDtypeStruct((live, rows, dim), F32)
    return pl.pallas_call(
        functools.partial(prepare_kernel, shards, live, group, strides),
        out_shape=[tile] * 4
        + [
            jax.ShapeDtypeStruct((1, rows), F32),
            jax.ShapeDtypeStruct((live, rows // dim * TILE, dim), F32),
            whole,
            whole,
            jax.ShapeDtypeStruct((TILE, dim), F32),
        ]
        + [jax.ShapeDtypeStruct((rows, dim), F32)] * len(strides),
        in_specs=[SMEM] * 3 + [VMEM] * 5,
        out_specs=[VMEM] * (9 + len(strides)),
        scratch_shapes=[pltpu.VMEM((projected.shape[2], TILE, rows), F32)],
        compiler_params=pltpu.CompilerParams(vmem_limit_bytes=8 * MIB),
        name="prepare_rows",
    )(place, from_shard, from_slot, projected, rate, gain, after, states)


def diagonal(dim):
    row = lax.broadcasted_iota(jnp.int32, (TILE, dim), 0)
    return row == lax.broadcasted_iota(jnp.int32, (TILE, dim), 1)


def raw_kernel(
    shards, live, group, place, shard_ref, lead_0, lead_1, near_1, near_0,
    local, query, grown, base, raw, sums, made, tiles, sem,
):
    rows, dim = near_0.shape
    heads = rows // dim
    tile_rows = heads * TILE
    for row in range(live):
        made[row] = local[row]
    for n, near in enumerate((near_1, near_0)):
        for head in range(heads):
            span = slice(head * dim, (head + 1) * dim)
            made[live + n, head * TILE : (head + 1) * TILE] = products(
                query[:, span], near[span]
            )
    for n, lead in enumerate((lead_1, lead_0)):
        made[live + 2 + n] = lead[0:tile_rows]
    picks = []
    device, side = spot(place, group)
    for row in range(live):
        gap = gap_of(row, shards, live, device, shard_ref)
        index = jnp.int32(row)
        for n, stride in enumerate((-1, 1, -2, 2)):
            index = jnp.where(at_stride(gap, stride, shards, side), live + n, index)
        picks.append(index)
    which = lax.rem(lax.broadcasted_iota(jnp.int32, (TILE, dim), 0), live)
    total = jnp.zeros((TILE, dim), F32)
    for head in range(heads):
        span = slice(head * dim, (head + 1) * dim)
        part = slice(head * TILE, (head + 1) * TILE)
        tile = made[picks[0], part]
        for row in range(1, live):
            tile = jnp.where(which == row, made[picks[row], part], tile)
        tile = tile * grown[:, span] + base[:, span]
        raw[:, span] = tile
        total = total + tile * tile
    total = jnp.broadcast_to(jnp.sum(total, axis=1, keepdims=True), (TILE, dim))
    total = jnp.sum(jnp.where(diagonal(dim), total, 0.0), axis=0, keepdims=True)
    for peer in range(sums.shape[0]):
        tiles[peer] = total
    copy = pltpu.make_async_copy(tiles, sums, sem)
    copy.start()
    copy.wait()


def raw_of(place, from_shard, arrived, small, shards, live, group):
    rows, dim = arrived[-1].shape
    return pl.pallas_call(
        functools.partial(raw_kernel, shards, live, group),
        out_shape=[
            jax.ShapeDtypeStruct((TILE, rows), F32),
            jax.ShapeDtypeStruct((group, 1, dim), F32),
        ],
        in_specs=[SMEM] * 2 + [VMEM] * (len(arrived) + len(small)),
        out_specs=[VMEM, HBM],
        scratch_shapes=[
            pltpu.VMEM((live + 4, rows // dim * TILE, dim), F32),
            pltpu.VMEM((group, 1, dim), F32),
            pltpu.SemaphoreType.DMA(()),
        ],
        compiler_params=pltpu.CompilerParams(vmem_limit_bytes=6 * MIB),
        cost_estimate=pl.CostEstimate(flops=10**12, bytes_accessed=MIB, transcendentals=0),
        name="raw_rows",
    )(place, from_shard, *arrived, *small)


def final_kernel(
    shards, live, group, place, shard_ref, here, lead_0, lead_1, near_1, near_0,
    rest_1, rest_0, outer, decay, final, token, held, made, sems_in, sems,
):
    rows, dim = here.shape[1:]
    heads = rows // dim
    early, tile_rows = EARLY * dim, heads * TILE
    device, side = spot(place, group)
    token[...] = jnp.zeros_like(token)

    def loads(row, lead, rest):
        return [
            pltpu.make_async_copy(
                lead.at[tile_rows : tile_rows + early],
                held.at[row, 0:early],
                sems_in.at[row, 0],
            ),
            pltpu.make_async_copy(rest, held.at[row, early:rows], sems_in.at[row, 1]),
        ]

    cases = []
    for row in range(live):
        gap = gap_of(row, shards, live, device, shard_ref)
        far_0 = at_stride(gap, 2, shards, side)
        far_1 = at_stride(gap, -2, shards, side)
        for found, lead, rest in ((far_0, lead_0, rest_0), (far_1, lead_1, rest_1)):

            @pl.when(found)
            def _():
                start_all(loads(row, lead, rest))

        cases.append(
            [
                (gap == 0, here.at[row]),
                (at_stride(gap, 1, shards, side), near_0),
                (at_stride(gap, -1, shards, side), near_1),
                (jnp.logical_or(far_0, far_1), held.at[row]),
            ]
        )
    copies = []
    for row in range(live):

        @pl.when(cases[row][3][0])
        def _():
            wait_all(loads(row, lead_0, rest_0))

        for half in range(2):
            span = range(half * heads // 2, (half + 1) * heads // 2)
            for found, source in cases[row]:

                @pl.when(found)
                def _():
                    for head in span:
                        block = slice(head * dim, (head + 1) * dim)
                        made[row, block] = (
                            decay[:, block] * source[block] + outer[row, block]
                        )

            block = slice(span.start * dim, span.stop * dim)
            copy = pltpu.make_async_copy(
                made.at[row, block], final.at[row, block], sems.at[row, half]
            )
            copy.start()
            copies.append(copy)
    wait_all(copies)


def final_of(place, from_shard, here, lead, near, rest, small, shards, live, group):
    rows, dim = here.shape[1:]
    return pl.pallas_call(
        functools.partial(final_kernel, shards, live, group),
        out_shape=[
            jax.ShapeDtypeStruct((live, rows, dim), F32),
            jax.ShapeDtypeStruct((TILE, dim), F32),
        ],
        in_specs=[SMEM] * 2 + [VMEM] + [HBM] * 2 + [VMEM] * 2 + [HBM] * 2 + [VMEM] * 2,
        out_specs=[pl.BlockSpec(memory_space=pl.ANY), VMEM],
        scratch_shapes=[
            pltpu.VMEM((live, rows, dim), F32),
            pltpu.VMEM((live, rows, dim), F32),
            pltpu.SemaphoreType.DMA((live, 2)),
            pltpu.SemaphoreType.DMA((live, 2)),
        ],
        compiler_params=pltpu.CompilerParams(vmem_limit_bytes=8 * MIB),
        cost_estimate=pl.CostEstimate(flops=10**10, bytes_accessed=MIB, transcendentals=0),
        name="final_rows",
    )(place, from_shard, here, *in_hbm(*lead), *near, *in_hbm(*rest), *small)


def attend_kernel(live, features, totals, raw, gated, _, attended):
    dim = totals.shape[2]
    total = totals[0]
    for peer in range(1, totals.shape[0]):
        total = total + totals[peer]
    total = jnp.where(diagonal(dim), jnp.broadcast_to(total, (TILE, dim)), 0.0)
    total = jnp.sum(total, axis=1, keepdims=True)
    scale = jnp.broadcast_to(lax.rsqrt(total / features + EPS), raw.shape)
    tile = raw[...] * scale * gated[...]
    for step in range(attended.shape[0]):
        attended[step] = tile[step * live : (step + 1) * live].astype(BF16)


def attend(totals, raw, gated, after, live, steps, features):
    return pl.pallas_call(
        functools.partial(attend_kernel, live, features),
        out_shape=jax.ShapeDtypeStruct((steps, live, raw.shape[1]), BF16),
        in_specs=[VMEM] * 4,
        out_specs=VMEM,
        compiler_params=pltpu.CompilerParams(vmem_limit_bytes=4 * MIB),
        name="attend_rows",
    )(totals, raw, gated, after)


def on_device(states, from_shard, from_slot, projected, decay_rate, norm_gain):
    shards, group = lax.axis_size("dp"), lax.axis_size("tensor")
    steps, live = projected.shape[:2]
    slots, heads, dim = states.shape[:3]
    width = heads * dim
    place = lax.axis_index(("dp", "tensor")).astype(jnp.int32).reshape(1)
    states = states.reshape(slots, width, dim)

    row_0, row_1, next_1, staged = pick(
        place, from_shard, from_slot, projected, states, shards, live, group, (-2, 2, 1)
    )
    half_1, half_0 = swapped(row_1, 1), swapped(row_0, 0)
    rate = jnp.repeat(decay_rate, dim).reshape(1, width)
    gain = norm_gain.reshape(1, width)
    query, grown, base, gated, decay, local, here, outer, token, next_0 = prepare(
        place, from_shard, from_slot, projected, rate, gain, row_0, staged, shards, live,
        group, (-1,),
    )
    sent = relay(half_0, half_1, next_0, heads)
    near_1, near_0 = swapped(next_1, 1), swapped(sent[4], 0)
    lead_1, lead_0 = swapped(sent[0], 1), swapped(sent[1], 0)
    rest_1, rest_0 = swapped(sent[2], 1), swapped(sent[3], 0)

    raw, sums = raw_of(
        place, from_shard, (lead_0, lead_1, near_1, near_0),
        (local, query, grown, base), shards, live, group,
    )
    totals = lax.all_to_all(sums, "tensor", 0, 0)
    final, token = final_of(
        place, from_shard, here, (lead_0, lead_1), (near_1, near_0), (rest_1, rest_0),
        (outer, decay), shards, live, group,
    )
    attended = attend(totals, raw, gated, token, live, steps, width * group)
    return attended, final.reshape(live, heads, dim, dim)


def solution(mesh):
    return jax.shard_map(
        on_device,
        mesh=mesh,
        in_specs=(
            P("dp", "tensor", None, None),
            P(),
            P(),
            P(None, "dp", None, "tensor"),
            P("tensor"),
            P("tensor"),
        ),
        out_specs=(P(None, "dp", "tensor"), P("dp", "tensor", None, None)),
        check_vma=False,
    )
```

```python
import functools
import jax
import jax.numpy as jnp
from jax import lax
from jax.experimental import pallas as pl
from jax.experimental.pallas import tpu as pltpu
from jax.sharding import PartitionSpec as P

EPS = 1e-05
F32 = jnp.float32
BF16 = jnp.bfloat16
EARLY = 2
TILE = 8
MIB = 1024 * 1024
SMEM = pl.BlockSpec(memory_space=pltpu.SMEM)
VMEM = pl.BlockSpec(memory_space=pltpu.VMEM)
HBM = pl.BlockSpec(memory_space=pltpu.HBM)


def swapped(block, first):
    shards, group = lax.axis_size("dp"), lax.axis_size("tensor")
    route = []
    for i in range(0, shards, 2):
        for j in range(group):
            low = (first + j % 2 + i) % shards
            high = (low + 1) % shards
            route += [
                (low * group + j, high * group + j),
                (high * group + j, low * group + j),
            ]
    return lax.ppermute(block, ("dp", "tensor"), route)


def spot(place, group):
    shard = lax.div(place[0], group)
    return shard, 2 * ((shard ^ lax.rem(place[0], group)) & 1) - 1


def start_all(copies):
    for copy in copies:
        copy.start()


def wait_all(copies):
    for copy in copies:
        copy.wait()


def in_hbm(*arrays):
    return [pltpu.with_memory_space_constraint(x, pltpu.HBM) for x in arrays]


def products(query, state):
    q_high = query.astype(BF16).astype(F32)
    both = jnp.concatenate([q_high, query - q_high], axis=0).astype(BF16)
    high = state.astype(BF16)
    low = (state - high.astype(F32)).astype(BF16)
    first = jnp.dot(both, high, preferred_element_type=F32)
    second = jnp.dot(both, low, preferred_element_type=F32)
    return first[:TILE] + first[TILE:] + second[:TILE]


def pick_kernel(shards, live, group, strides, place, shard_hbm, slot_hbm, projected, states, *refs):
    n_rows = len(strides)
    outs = refs[:n_rows]
    staged, shard_ref, slot_ref, inputs, sems = refs[n_rows:]
    dim = outs[0].shape[1]
    rows = states.shape[1]
    device, side = spot(place, group)
    copies = [
        pltpu.make_async_copy(shard_hbm, shard_ref, sems.at[0]),
        pltpu.make_async_copy(slot_hbm, slot_ref, sems.at[1]),
        pltpu.make_async_copy(projected, inputs, sems.at[2]),
        pltpu.make_async_copy(states, staged, sems.at[3]),
    ]
    start_all(copies)
    tile_rows = rows // dim * TILE
    for n in range(n_rows):
        outs[n][rows : rows + tile_rows] = jnp.zeros((tile_rows, dim), F32)
    copies[2].wait()
    for step in range(inputs.shape[0]):
        for row in range(live):
            query = jax.nn.silu(inputs[step, row].astype(F32))[0:1]
            for head in range(rows // dim):
                at = rows + head * TILE + step * live + row
                part = query[:, head * dim : (head + 1) * dim]
                for n in range(n_rows):
                    outs[n][at : at + 1] = part
    wait_all(copies[:2])
    slots = [
        slot_for(stride, shards, live, device, side, shard_ref, slot_ref)
        for stride in strides
    ]
    copies[3].wait()
    for n, slot in enumerate(slots):
        outs[n][0:rows] = staged[slot]


def pick(place, from_shard, from_slot, projected, states, shards, live, group, strides):
    rows, dim = states.shape[1:]
    tile_rows = rows // dim * TILE
    return pl.pallas_call(
        functools.partial(pick_kernel, shards, live, group, strides),
        out_shape=[jax.ShapeDtypeStruct((rows + tile_rows, dim), F32)] * len(strides)
        + [jax.ShapeDtypeStruct(states.shape, F32)],
        in_specs=[SMEM] + [HBM] * 4,
        out_specs=[VMEM] * (len(strides) + 1),
        scratch_shapes=[
            pltpu.SMEM(from_shard.shape, jnp.int32),
            pltpu.SMEM(from_slot.shape, jnp.int32),
            pltpu.VMEM(projected.shape, projected.dtype),
            pltpu.SemaphoreType.DMA((4,)),
        ],
        compiler_params=pltpu.CompilerParams(vmem_limit_bytes=6 * MIB),
        name="pick_rows",
    )(place, *in_hbm(from_shard, from_slot, projected, states))


def relay_kernel(from_0, from_1, _, lead_1, lead_0, rest_1, rest_0):
    dim = from_1.shape[1]
    heads = rest_0.shape[0] // dim + EARLY
    rows, early = heads * dim, EARLY * dim
    tile_rows = heads * TILE
    for source, other, lead, rest in (
        (from_0, from_1, lead_1, rest_1),
        (from_1, from_0, lead_0, rest_0),
    ):
        for head in range(heads):
            part = slice(head * TILE, (head + 1) * TILE)
            query = other[rows + head * TILE : rows + (head + 1) * TILE]
            state = source[head * dim : (head + 1) * dim]
            lead[part] = products(query, state)
            if head < EARLY:
                lead[tile_rows + head * dim : tile_rows + (head + 1) * dim] = state
            else:
                rest[(head - EARLY) * dim : (head - EARLY + 1) * dim] = state


def relay(from_0, from_1, after, heads):
    dim = from_0.shape[1]
    lead = jax.ShapeDtypeStruct((heads * TILE + EARLY * dim, dim), F32)
    rest = jax.ShapeDtypeStruct(((heads - EARLY) * dim, dim), F32)
    return pl.pallas_call(
        relay_kernel,
        out_shape=[lead, lead, rest, rest],
        in_specs=[VMEM] * 3,
        out_specs=[VMEM] * 4,
        compiler_params=pltpu.CompilerParams(vmem_limit_bytes=6 * MIB),
        name="relay_rows",
    )(from_0, from_1, after)


def gap_of(row, shards, live, device, shard_ref):
    return lax.rem(device - shard_ref[device * live + row] + shards, shards)


def at_stride(gap, stride, shards, side):
    return gap == lax.rem(stride * side + shards, shards)


def slot_for(stride, shards, live, device, side, shard_ref, slot_ref):
    target = lax.rem(device + stride * side + shards, shards)
    slot = jnp.int32(0)
    for row in range(live):
        mine = shard_ref[target * live + row] == device
        slot = jnp.where(mine, slot_ref[target * live + row], slot)
    return slot


def prepare_kernel(
    shards, live, group, strides, place, shard_ref, slot_ref, projected, rate, gain, states,
    query, grown, base, gated, decay, made, here, outer, token, *refs,
):
    outs, parts = refs[:-1], refs[-1]
    token[...] = jnp.zeros_like(token)
    rows, dim = here.shape[1:]
    heads = rows // dim
    steps = projected.shape[0]
    device, side = spot(place, group)
    for n, stride in enumerate(strides):
        slot = slot_for(stride, shards, live, device, side, shard_ref, slot_ref)
        outs[n][...] = states[slot]
    for row in range(live):
        here[row] = states[slot_ref[device * live + row]]
    parts[...] = jnp.zeros_like(parts)
    for step in range(steps):
        for row in range(live):
            block = projected[step, row].astype(F32)
            at = step * live + row
            for n in range(parts.shape[0]):
                parts[n, at : at + 1] = block[n : n + 1]
    queries, keys, values = (jax.nn.silu(parts[n]) for n in range(3))
    index = lax.broadcasted_iota(jnp.int32, queries.shape, 0)
    step_of = (index // live).astype(F32)
    rates = jnp.broadcast_to(rate[...], queries.shape)
    query[...] = queries
    gated[...] = jax.nn.sigmoid(parts[3]) * gain[...]
    grown[...] = jnp.exp(-rates * (step_of + 1.0))
    decay[...] = jnp.exp(-steps * rate[...])
    faded = keys * jnp.exp(-rates * jnp.maximum(steps - 1.0 - step_of, 0.0))
    later = lambda x, count: jnp.concatenate(
        [jnp.zeros((count, rows), F32), x[: TILE - count]], axis=0
    )
    total = jnp.zeros_like(queries)
    for lag in range(steps):
        key = later(keys, lag * live) if lag else keys
        value = later(values, lag * live) if lag else values
        product = queries * key
        match = jnp.concatenate(
            [
                jnp.broadcast_to(
                    jnp.sum(
                        product[:, head * dim : (head + 1) * dim], axis=1, keepdims=True
                    ),
                    (TILE, dim),
                )
                for head in range(heads)
            ],
            axis=1,
        )
        total = total + jnp.exp(-rates * float(lag)) * match * value
    base[...] = total

    def halves(x):
        high = x.astype(BF16).astype(F32)
        return high, x - high

    nothing = jnp.zeros_like(queries)
    v_high, v_low = halves(values)
    right = jnp.concatenate([v_high, v_high, v_low, nothing], axis=0).astype(BF16)
    for row in range(live):
        k_high, k_low = halves(jnp.where(lax.rem(index, live) == row, faded, 0.0))
        left = jnp.concatenate([k_high, k_low, k_high, nothing], axis=0).astype(BF16)
        for head in range(heads):
            span = slice(head * dim, (head + 1) * dim)
            outer[row, span] = lax.dot_general(
                left[:, span],
                right[:, span],
                (((0,), (0,)), ((), ())),
                preferred_element_type=F32,
            )
    for row in range(live):
        for head in range(heads):
            span = slice(head * dim, (head + 1) * dim)
            made[row, head * TILE : (head + 1) * TILE] = products(
                queries[:, span], here[row, span]
            )


def prepare(
    place, from_shard, from_slot, projected, rate, gain, states, shards, live, group, strides
):
    rows, dim = states.shape[1:]
    tile = jax.ShapeDtypeStruct((TILE, rows), F32)
    whole = jax.ShapeDtypeStruct((live, rows, dim), F32)
    return pl.pallas_call(
        functools.partial(prepare_kernel, shards, live, group, strides),
        out_shape=[tile] * 4
        + [
            jax.ShapeDtypeStruct((1, rows), F32),
            jax.ShapeDtypeStruct((live, rows // dim * TILE, dim), F32),
            whole,
            whole,
            jax.ShapeDtypeStruct((TILE, dim), F32),
        ]
        + [jax.ShapeDtypeStruct((rows, dim), F32)] * len(strides),
        in_specs=[SMEM] * 3 + [VMEM] * 4,
        out_specs=[VMEM] * (9 + len(strides)),
        scratch_shapes=[pltpu.VMEM((projected.shape[2], TILE, rows), F32)],
        compiler_params=pltpu.CompilerParams(vmem_limit_bytes=8 * MIB),
        name="prepare_rows",
    )(place, from_shard, from_slot, projected, rate, gain, states)


def diagonal(dim):
    row = lax.broadcasted_iota(jnp.int32, (TILE, dim), 0)
    return row == lax.broadcasted_iota(jnp.int32, (TILE, dim), 1)


def raw_kernel(
    shards, live, group, place, shard_ref, lead_0, lead_1, near_1, near_0,
    local, query, grown, base, raw, sums, made, tiles, sem,
):
    rows, dim = near_0.shape
    heads = rows // dim
    tile_rows = heads * TILE
    for row in range(live):
        made[row] = local[row]
    for n, near in enumerate((near_1, near_0)):
        for head in range(heads):
            span = slice(head * dim, (head + 1) * dim)
            made[live + n, head * TILE : (head + 1) * TILE] = products(
                query[:, span], near[span]
            )
    for n, lead in enumerate((lead_1, lead_0)):
        made[live + 2 + n] = lead[0:tile_rows]
    picks = []
    device, side = spot(place, group)
    for row in range(live):
        gap = gap_of(row, shards, live, device, shard_ref)
        index = jnp.int32(row)
        for n, stride in enumerate((-1, 1, -2, 2)):
            index = jnp.where(at_stride(gap, stride, shards, side), live + n, index)
        picks.append(index)
    which = lax.rem(lax.broadcasted_iota(jnp.int32, (TILE, dim), 0), live)
    total = jnp.zeros((TILE, dim), F32)
    for head in range(heads):
        span = slice(head * dim, (head + 1) * dim)
        part = slice(head * TILE, (head + 1) * TILE)
        tile = made[picks[0], part]
        for row in range(1, live):
            tile = jnp.where(which == row, made[picks[row], part], tile)
        tile = tile * grown[:, span] + base[:, span]
        raw[:, span] = tile
        total = total + tile * tile
    total = jnp.broadcast_to(jnp.sum(total, axis=1, keepdims=True), (TILE, dim))
    total = jnp.sum(jnp.where(diagonal(dim), total, 0.0), axis=0, keepdims=True)
    for peer in range(sums.shape[0]):
        tiles[peer] = total
    copy = pltpu.make_async_copy(tiles, sums, sem)
    copy.start()
    copy.wait()


def raw_of(place, from_shard, arrived, small, shards, live, group):
    rows, dim = arrived[-1].shape
    return pl.pallas_call(
        functools.partial(raw_kernel, shards, live, group),
        out_shape=[
            jax.ShapeDtypeStruct((TILE, rows), F32),
            jax.ShapeDtypeStruct((group, 1, dim), F32),
        ],
        in_specs=[SMEM] * 2 + [VMEM] * (len(arrived) + len(small)),
        out_specs=[VMEM, HBM],
        scratch_shapes=[
            pltpu.VMEM((live + 4, rows // dim * TILE, dim), F32),
            pltpu.VMEM((group, 1, dim), F32),
            pltpu.SemaphoreType.DMA(()),
        ],
        compiler_params=pltpu.CompilerParams(vmem_limit_bytes=6 * MIB),
        cost_estimate=pl.CostEstimate(flops=10**12, bytes_accessed=MIB, transcendentals=0),
        name="raw_rows",
    )(place, from_shard, *arrived, *small)


def final_kernel(
    shards, live, group, place, shard_ref, here, lead_0, lead_1, near_1, near_0,
    rest_1, rest_0, outer, decay, final, token, held, made, sems_in, sems,
):
    rows, dim = here.shape[1:]
    heads = rows // dim
    early, tile_rows = EARLY * dim, heads * TILE
    device, side = spot(place, group)
    token[...] = jnp.zeros_like(token)

    def loads(row, lead, rest):
        return [
            pltpu.make_async_copy(
                lead.at[tile_rows : tile_rows + early],
                held.at[row, 0:early],
                sems_in.at[row, 0],
            ),
            pltpu.make_async_copy(rest, held.at[row, early:rows], sems_in.at[row, 1]),
        ]

    cases = []
    for row in range(live):
        gap = gap_of(row, shards, live, device, shard_ref)
        far_0 = at_stride(gap, 2, shards, side)
        far_1 = at_stride(gap, -2, shards, side)
        for found, lead, rest in ((far_0, lead_0, rest_0), (far_1, lead_1, rest_1)):

            @pl.when(found)
            def _():
                start_all(loads(row, lead, rest))

        cases.append(
            [
                (gap == 0, here.at[row]),
                (at_stride(gap, 1, shards, side), near_0),
                (at_stride(gap, -1, shards, side), near_1),
                (jnp.logical_or(far_0, far_1), held.at[row]),
            ]
        )
    copies = []
    for row in range(live):

        @pl.when(cases[row][3][0])
        def _():
            wait_all(loads(row, lead_0, rest_0))

        for half in range(2):
            span = range(half * heads // 2, (half + 1) * heads // 2)
            for found, source in cases[row]:

                @pl.when(found)
                def _():
                    for head in span:
                        block = slice(head * dim, (head + 1) * dim)
                        made[row, block] = (
                            decay[:, block] * source[block] + outer[row, block]
                        )

            block = slice(span.start * dim, span.stop * dim)
            copy = pltpu.make_async_copy(
                made.at[row, block], final.at[row, block], sems.at[row, half]
            )
            copy.start()
            copies.append(copy)
    wait_all(copies)


def final_of(place, from_shard, here, lead, near, rest, small, shards, live, group):
    rows, dim = here.shape[1:]
    return pl.pallas_call(
        functools.partial(final_kernel, shards, live, group),
        out_shape=[
            jax.ShapeDtypeStruct((live, rows, dim), F32),
            jax.ShapeDtypeStruct((TILE, dim), F32),
        ],
        in_specs=[SMEM] * 2 + [VMEM] + [HBM] * 2 + [VMEM] * 2 + [HBM] * 2 + [VMEM] * 2,
        out_specs=[pl.BlockSpec(memory_space=pl.ANY), VMEM],
        scratch_shapes=[
            pltpu.VMEM((live, rows, dim), F32),
            pltpu.VMEM((live, rows, dim), F32),
            pltpu.SemaphoreType.DMA((live, 2)),
            pltpu.SemaphoreType.DMA((live, 2)),
        ],
        compiler_params=pltpu.CompilerParams(vmem_limit_bytes=8 * MIB),
        cost_estimate=pl.CostEstimate(flops=10**10, bytes_accessed=MIB, transcendentals=0),
        name="final_rows",
    )(place, from_shard, here, *in_hbm(*lead), *near, *in_hbm(*rest), *small)


def attend_kernel(live, features, totals, raw, gated, _, attended):
    dim = totals.shape[2]
    total = totals[0]
    for peer in range(1, totals.shape[0]):
        total = total + totals[peer]
    total = jnp.where(diagonal(dim), jnp.broadcast_to(total, (TILE, dim)), 0.0)
    total = jnp.sum(total, axis=1, keepdims=True)
    scale = jnp.broadcast_to(lax.rsqrt(total / features + EPS), raw.shape)
    tile = raw[...] * scale * gated[...]
    for step in range(attended.shape[0]):
        attended[step] = tile[step * live : (step + 1) * live].astype(BF16)


def attend(totals, raw, gated, after, live, steps, features):
    return pl.pallas_call(
        functools.partial(attend_kernel, live, features),
        out_shape=jax.ShapeDtypeStruct((steps, live, raw.shape[1]), BF16),
        in_specs=[VMEM] * 4,
        out_specs=VMEM,
        compiler_params=pltpu.CompilerParams(vmem_limit_bytes=4 * MIB),
        name="attend_rows",
    )(totals, raw, gated, after)


def on_device(states, from_shard, from_slot, projected, decay_rate, norm_gain):
    shards, group = lax.axis_size("dp"), lax.axis_size("tensor")
    steps, live = projected.shape[:2]
    slots, heads, dim = states.shape[:3]
    width = heads * dim
    place = lax.axis_index(("dp", "tensor")).astype(jnp.int32).reshape(1)
    states = states.reshape(slots, width, dim)

    row_0, row_1, staged = pick(
        place, from_shard, from_slot, projected, states, shards, live, group, (-2, 2)
    )
    half_1, half_0 = swapped(row_1, 1), swapped(row_0, 0)
    rate = jnp.repeat(decay_rate, dim).reshape(1, width)
    gain = norm_gain.reshape(1, width)
    query, grown, base, gated, decay, local, here, outer, token, row_0, row_1 = prepare(
        place, from_shard, from_slot, projected, rate, gain, staged, shards, live,
        group, (-1, 1),
    )
    near_1, near_0 = swapped(row_1, 1), swapped(row_0, 0)
    sent = relay(half_0, half_1, token, heads)
    lead_1, lead_0 = swapped(sent[0], 1), swapped(sent[1], 0)
    rest_1, rest_0 = swapped(sent[2], 1), swapped(sent[3], 0)

    raw, sums = raw_of(
        place, from_shard, (lead_0, lead_1, near_1, near_0),
        (local, query, grown, base), shards, live, group,
    )
    totals = lax.all_to_all(sums, "tensor", 0, 0)
    final, token = final_of(
        place, from_shard, here, (lead_0, lead_1), (near_1, near_0), (rest_1, rest_0),
        (outer, decay), shards, live, group,
    )
    attended = attend(totals, raw, gated, token, live, steps, width * group)
    return attended, final.reshape(live, heads, dim, dim)


def solution(mesh):
    return jax.shard_map(
        on_device,
        mesh=mesh,
        in_specs=(
            P("dp", "tensor", None, None),
            P(),
            P(),
            P(None, "dp", None, "tensor"),
            P("tensor"),
            P("tensor"),
        ),
        out_specs=(P(None, "dp", "tensor"), P("dp", "tensor", None, None)),
        check_vma=False,
    )
```

```python
import functools
import jax
import jax.numpy as jnp
from jax import lax
from jax.experimental import pallas as pl
from jax.experimental.pallas import tpu as pltpu
from jax.sharding import PartitionSpec as P

EPS = 1e-05
F32 = jnp.float32
BF16 = jnp.bfloat16
EARLY = 2
TILE = 8
MIB = 1024 * 1024
SMEM = pl.BlockSpec(memory_space=pltpu.SMEM)
VMEM = pl.BlockSpec(memory_space=pltpu.VMEM)
HBM = pl.BlockSpec(memory_space=pltpu.HBM)


def swapped(block, first):
    shards, group = lax.axis_size("dp"), lax.axis_size("tensor")
    route = []
    for i in range(0, shards, 2):
        for j in range(group):
            low = (first + j % 2 + i) % shards
            high = (low + 1) % shards
            route += [
                (low * group + j, high * group + j),
                (high * group + j, low * group + j),
            ]
    return lax.ppermute(block, ("dp", "tensor"), route)


def spot(place, group):
    shard = lax.div(place[0], group)
    return shard, 2 * ((shard ^ lax.rem(place[0], group)) & 1) - 1


def start_all(copies):
    for copy in copies:
        copy.start()


def wait_all(copies):
    for copy in copies:
        copy.wait()


def in_hbm(*arrays):
    return [pltpu.with_memory_space_constraint(x, pltpu.HBM) for x in arrays]


def products(query, state):
    q_high = query.astype(BF16).astype(F32)
    both = jnp.concatenate([q_high, query - q_high], axis=0).astype(BF16)
    high = state.astype(BF16)
    low = (state - high.astype(F32)).astype(BF16)
    first = jnp.dot(both, high, preferred_element_type=F32)
    second = jnp.dot(both, low, preferred_element_type=F32)
    return first[:TILE] + first[TILE:] + second[:TILE]


def pick_kernel(shards, live, group, strides, place, shard_hbm, slot_hbm, projected, states, *refs):
    n_rows = len(strides)
    outs = refs[:n_rows]
    shard_ref, slot_ref, inputs, staged, sems = refs[n_rows:]
    dim = outs[0].shape[1]
    rows = states.shape[1]
    device, side = spot(place, group)
    copies = [
        pltpu.make_async_copy(shard_hbm, shard_ref, sems.at[0]),
        pltpu.make_async_copy(slot_hbm, slot_ref, sems.at[1]),
        pltpu.make_async_copy(projected, inputs, sems.at[2]),
        pltpu.make_async_copy(states, staged, sems.at[3]),
    ]
    start_all(copies)
    tile_rows = rows // dim * TILE
    for n in range(n_rows):
        outs[n][rows : rows + tile_rows] = jnp.zeros((tile_rows, dim), F32)
    copies[2].wait()
    for step in range(inputs.shape[0]):
        for row in range(live):
            query = jax.nn.silu(inputs[step, row].astype(F32))[0:1]
            for head in range(rows // dim):
                at = rows + head * TILE + step * live + row
                part = query[:, head * dim : (head + 1) * dim]
                for n in range(n_rows):
                    outs[n][at : at + 1] = part
    wait_all(copies[:2])
    slots = [
        slot_for(stride, shards, live, device, side, shard_ref, slot_ref)
        for stride in strides
    ]
    copies[3].wait()
    for n, slot in enumerate(slots):
        outs[n][0:rows] = staged[slot]


def pick(place, from_shard, from_slot, projected, states, shards, live, group, strides):
    rows, dim = states.shape[1:]
    tile_rows = rows // dim * TILE
    return pl.pallas_call(
        functools.partial(pick_kernel, shards, live, group, strides),
        out_shape=[jax.ShapeDtypeStruct((rows + tile_rows, dim), F32)] * len(strides),
        in_specs=[SMEM] + [HBM] * 4,
        out_specs=[VMEM] * len(strides),
        scratch_shapes=[
            pltpu.SMEM(from_shard.shape, jnp.int32),
            pltpu.SMEM(from_slot.shape, jnp.int32),
            pltpu.VMEM(projected.shape, projected.dtype),
            pltpu.VMEM(states.shape, F32),
            pltpu.SemaphoreType.DMA((4,)),
        ],
        compiler_params=pltpu.CompilerParams(vmem_limit_bytes=6 * MIB),
        name="pick_rows",
    )(place, *in_hbm(from_shard, from_slot, projected, states))


def relay_kernel(from_0, from_1, _, lead_1, lead_0, rest_1, rest_0):
    dim = from_1.shape[1]
    heads = rest_0.shape[0] // dim + EARLY
    rows, early = heads * dim, EARLY * dim
    tile_rows = heads * TILE
    for source, other, lead, rest in (
        (from_0, from_1, lead_1, rest_1),
        (from_1, from_0, lead_0, rest_0),
    ):
        for head in range(heads):
            part = slice(head * TILE, (head + 1) * TILE)
            query = other[rows + head * TILE : rows + (head + 1) * TILE]
            state = source[head * dim : (head + 1) * dim]
            lead[part] = products(query, state)
            if head < EARLY:
                lead[tile_rows + head * dim : tile_rows + (head + 1) * dim] = state
            else:
                rest[(head - EARLY) * dim : (head - EARLY + 1) * dim] = state


def relay(from_0, from_1, after, heads):
    dim = from_0.shape[1]
    lead = jax.ShapeDtypeStruct((heads * TILE + EARLY * dim, dim), F32)
    rest = jax.ShapeDtypeStruct(((heads - EARLY) * dim, dim), F32)
    return pl.pallas_call(
        relay_kernel,
        out_shape=[lead, lead, rest, rest],
        in_specs=[VMEM] * 3,
        out_specs=[VMEM] * 4,
        compiler_params=pltpu.CompilerParams(vmem_limit_bytes=6 * MIB),
        name="relay_rows",
    )(from_0, from_1, after)


def gap_of(row, shards, live, device, shard_ref):
    return lax.rem(device - shard_ref[device * live + row] + shards, shards)


def at_stride(gap, stride, shards, side):
    return gap == lax.rem(stride * side + shards, shards)


def slot_for(stride, shards, live, device, side, shard_ref, slot_ref):
    target = lax.rem(device + stride * side + shards, shards)
    slot = jnp.int32(0)
    for row in range(live):
        mine = shard_ref[target * live + row] == device
        slot = jnp.where(mine, slot_ref[target * live + row], slot)
    return slot


def prepare_kernel(
    shards, live, group, strides, place, shard_ref, slot_ref, projected, rate, gain, _, states,
    query, grown, base, gated, decay, made, here, outer, token, *refs,
):
    outs, (parts, sems) = refs[:-2], refs[-2:]
    token[...] = jnp.zeros_like(token)
    rows, dim = here.shape[1:]
    heads = rows // dim
    steps = projected.shape[0]
    device, side = spot(place, group)
    copies = [
        pltpu.make_async_copy(
            states.at[slot_ref[device * live + row]], here.at[row], sems.at[row]
        )
        for row in range(live)
    ]
    start_all(copies)
    sends = []
    for n, stride in enumerate(strides):
        slot = slot_for(stride, shards, live, device, side, shard_ref, slot_ref)
        sends.append(pltpu.make_async_copy(states.at[slot], outs[n], sems.at[live + n]))
    start_all(sends)
    parts[...] = jnp.zeros_like(parts)
    for step in range(steps):
        for row in range(live):
            block = projected[step, row].astype(F32)
            at = step * live + row
            for n in range(parts.shape[0]):
                parts[n, at : at + 1] = block[n : n + 1]
    queries, keys, values = (jax.nn.silu(parts[n]) for n in range(3))
    index = lax.broadcasted_iota(jnp.int32, queries.shape, 0)
    step_of = (index // live).astype(F32)
    rates = jnp.broadcast_to(rate[...], queries.shape)
    query[...] = queries
    gated[...] = jax.nn.sigmoid(parts[3]) * gain[...]
    grown[...] = jnp.exp(-rates * (step_of + 1.0))
    decay[...] = jnp.exp(-steps * rate[...])
    faded = keys * jnp.exp(-rates * jnp.maximum(steps - 1.0 - step_of, 0.0))
    later = lambda x, count: jnp.concatenate(
        [jnp.zeros((count, rows), F32), x[: TILE - count]], axis=0
    )
    total = jnp.zeros_like(queries)
    for lag in range(steps):
        key = later(keys, lag * live) if lag else keys
        value = later(values, lag * live) if lag else values
        product = queries * key
        match = jnp.concatenate(
            [
                jnp.broadcast_to(
                    jnp.sum(
                        product[:, head * dim : (head + 1) * dim], axis=1, keepdims=True
                    ),
                    (TILE, dim),
                )
                for head in range(heads)
            ],
            axis=1,
        )
        total = total + jnp.exp(-rates * float(lag)) * match * value
    base[...] = total

    def halves(x):
        high = x.astype(BF16).astype(F32)
        return high, x - high

    nothing = jnp.zeros_like(queries)
    v_high, v_low = halves(values)
    right = jnp.concatenate([v_high, v_high, v_low, nothing], axis=0).astype(BF16)
    for row in range(live):
        k_high, k_low = halves(jnp.where(lax.rem(index, live) == row, faded, 0.0))
        left = jnp.concatenate([k_high, k_low, k_high, nothing], axis=0).astype(BF16)
        for head in range(heads):
            span = slice(head * dim, (head + 1) * dim)
            outer[row, span] = lax.dot_general(
                left[:, span],
                right[:, span],
                (((0,), (0,)), ((), ())),
                preferred_element_type=F32,
            )
    wait_all(copies)
    for row in range(live):
        for head in range(heads):
            span = slice(head * dim, (head + 1) * dim)
            made[row, head * TILE : (head + 1) * TILE] = products(
                queries[:, span], here[row, span]
            )
    wait_all(sends)


def prepare(
    place, from_shard, from_slot, projected, rate, gain, after, states, shards, live, group, strides
):
    rows, dim = states.shape[1:]
    tile = jax.ShapeDtypeStruct((TILE, rows), F32)
    whole = jax.ShapeDtypeStruct((live, rows, dim), F32)
    return pl.pallas_call(
        functools.partial(prepare_kernel, shards, live, group, strides),
        out_shape=[tile] * 4
        + [
            jax.ShapeDtypeStruct((1, rows), F32),
            jax.ShapeDtypeStruct((live, rows // dim * TILE, dim), F32),
            whole,
            whole,
            jax.ShapeDtypeStruct((TILE, dim), F32),
        ]
        + [jax.ShapeDtypeStruct((rows, dim), F32)] * len(strides),
        in_specs=[SMEM] * 3 + [VMEM] * 4 + [HBM],
        out_specs=[VMEM] * (9 + len(strides)),
        scratch_shapes=[
            pltpu.VMEM((projected.shape[2], TILE, rows), F32),
            pltpu.SemaphoreType.DMA((live + len(strides),)),
        ],
        compiler_params=pltpu.CompilerParams(vmem_limit_bytes=8 * MIB),
        name="prepare_rows",
    )(place, from_shard, from_slot, projected, rate, gain, after, *in_hbm(states))


def diagonal(dim):
    row = lax.broadcasted_iota(jnp.int32, (TILE, dim), 0)
    return row == lax.broadcasted_iota(jnp.int32, (TILE, dim), 1)


def raw_kernel(
    shards, live, group, place, shard_ref, lead_0, lead_1, near_1, near_0,
    local, query, grown, base, raw, sums, made, tiles, sem,
):
    rows, dim = near_0.shape
    heads = rows // dim
    tile_rows = heads * TILE
    for row in range(live):
        made[row] = local[row]
    for n, near in enumerate((near_1, near_0)):
        for head in range(heads):
            span = slice(head * dim, (head + 1) * dim)
            made[live + n, head * TILE : (head + 1) * TILE] = products(
                query[:, span], near[span]
            )
    for n, lead in enumerate((lead_1, lead_0)):
        made[live + 2 + n] = lead[0:tile_rows]
    picks = []
    device, side = spot(place, group)
    for row in range(live):
        gap = gap_of(row, shards, live, device, shard_ref)
        index = jnp.int32(row)
        for n, stride in enumerate((-1, 1, -2, 2)):
            index = jnp.where(at_stride(gap, stride, shards, side), live + n, index)
        picks.append(index)
    which = lax.rem(lax.broadcasted_iota(jnp.int32, (TILE, dim), 0), live)
    total = jnp.zeros((TILE, dim), F32)
    for head in range(heads):
        span = slice(head * dim, (head + 1) * dim)
        part = slice(head * TILE, (head + 1) * TILE)
        tile = made[picks[0], part]
        for row in range(1, live):
            tile = jnp.where(which == row, made[picks[row], part], tile)
        tile = tile * grown[:, span] + base[:, span]
        raw[:, span] = tile
        total = total + tile * tile
    total = jnp.broadcast_to(jnp.sum(total, axis=1, keepdims=True), (TILE, dim))
    total = jnp.sum(jnp.where(diagonal(dim), total, 0.0), axis=0, keepdims=True)
    for peer in range(sums.shape[0]):
        tiles[peer] = total
    copy = pltpu.make_async_copy(tiles, sums, sem)
    copy.start()
    copy.wait()


def raw_of(place, from_shard, arrived, small, shards, live, group):
    rows, dim = arrived[-1].shape
    return pl.pallas_call(
        functools.partial(raw_kernel, shards, live, group),
        out_shape=[
            jax.ShapeDtypeStruct((TILE, rows), F32),
            jax.ShapeDtypeStruct((group, 1, dim), F32),
        ],
        in_specs=[SMEM] * 2 + [VMEM] * (len(arrived) + len(small)),
        out_specs=[VMEM, HBM],
        scratch_shapes=[
            pltpu.VMEM((live + 4, rows // dim * TILE, dim), F32),
            pltpu.VMEM((group, 1, dim), F32),
            pltpu.SemaphoreType.DMA(()),
        ],
        compiler_params=pltpu.CompilerParams(vmem_limit_bytes=6 * MIB),
        cost_estimate=pl.CostEstimate(flops=10**12, bytes_accessed=MIB, transcendentals=0),
        name="raw_rows",
    )(place, from_shard, *arrived, *small)


def final_kernel(
    shards, live, group, place, shard_ref, here, lead_0, lead_1, near_1, near_0,
    rest_1, rest_0, outer, decay, final, token, held, made, sems_in, sems,
):
    rows, dim = here.shape[1:]
    heads = rows // dim
    early, tile_rows = EARLY * dim, heads * TILE
    device, side = spot(place, group)
    token[...] = jnp.zeros_like(token)

    def loads(row, lead, rest):
        return [
            pltpu.make_async_copy(
                lead.at[tile_rows : tile_rows + early],
                held.at[row, 0:early],
                sems_in.at[row, 0],
            ),
            pltpu.make_async_copy(rest, held.at[row, early:rows], sems_in.at[row, 1]),
        ]

    cases = []
    for row in range(live):
        gap = gap_of(row, shards, live, device, shard_ref)
        far_0 = at_stride(gap, 2, shards, side)
        far_1 = at_stride(gap, -2, shards, side)
        for found, lead, rest in ((far_0, lead_0, rest_0), (far_1, lead_1, rest_1)):

            @pl.when(found)
            def _():
                start_all(loads(row, lead, rest))

        cases.append(
            [
                (gap == 0, here.at[row]),
                (at_stride(gap, 1, shards, side), near_0),
                (at_stride(gap, -1, shards, side), near_1),
                (jnp.logical_or(far_0, far_1), held.at[row]),
            ]
        )
    copies = []
    for row in range(live):

        @pl.when(cases[row][3][0])
        def _():
            wait_all(loads(row, lead_0, rest_0))

        for half in range(2):
            span = range(half * heads // 2, (half + 1) * heads // 2)
            for found, source in cases[row]:

                @pl.when(found)
                def _():
                    for head in span:
                        block = slice(head * dim, (head + 1) * dim)
                        made[row, block] = (
                            decay[:, block] * source[block] + outer[row, block]
                        )

            block = slice(span.start * dim, span.stop * dim)
            copy = pltpu.make_async_copy(
                made.at[row, block], final.at[row, block], sems.at[row, half]
            )
            copy.start()
            copies.append(copy)
    wait_all(copies)


def final_of(place, from_shard, here, lead, near, rest, small, shards, live, group):
    rows, dim = here.shape[1:]
    return pl.pallas_call(
        functools.partial(final_kernel, shards, live, group),
        out_shape=[
            jax.ShapeDtypeStruct((live, rows, dim), F32),
            jax.ShapeDtypeStruct((TILE, dim), F32),
        ],
        in_specs=[SMEM] * 2 + [VMEM] + [HBM] * 2 + [VMEM] * 2 + [HBM] * 2 + [VMEM] * 2,
        out_specs=[pl.BlockSpec(memory_space=pl.ANY), VMEM],
        scratch_shapes=[
            pltpu.VMEM((live, rows, dim), F32),
            pltpu.VMEM((live, rows, dim), F32),
            pltpu.SemaphoreType.DMA((live, 2)),
            pltpu.SemaphoreType.DMA((live, 2)),
        ],
        compiler_params=pltpu.CompilerParams(vmem_limit_bytes=8 * MIB),
        cost_estimate=pl.CostEstimate(flops=10**10, bytes_accessed=MIB, transcendentals=0),
        name="final_rows",
    )(place, from_shard, here, *in_hbm(*lead), *near, *in_hbm(*rest), *small)


def attend_kernel(live, features, totals, raw, gated, _, attended):
    dim = totals.shape[2]
    total = totals[0]
    for peer in range(1, totals.shape[0]):
        total = total + totals[peer]
    total = jnp.where(diagonal(dim), jnp.broadcast_to(total, (TILE, dim)), 0.0)
    total = jnp.sum(total, axis=1, keepdims=True)
    scale = jnp.broadcast_to(lax.rsqrt(total / features + EPS), raw.shape)
    tile = raw[...] * scale * gated[...]
    for step in range(attended.shape[0]):
        attended[step] = tile[step * live : (step + 1) * live].astype(BF16)


def attend(totals, raw, gated, after, live, steps, features):
    return pl.pallas_call(
        functools.partial(attend_kernel, live, features),
        out_shape=jax.ShapeDtypeStruct((steps, live, raw.shape[1]), BF16),
        in_specs=[VMEM] * 4,
        out_specs=VMEM,
        compiler_params=pltpu.CompilerParams(vmem_limit_bytes=4 * MIB),
        name="attend_rows",
    )(totals, raw, gated, after)


def on_device(states, from_shard, from_slot, projected, decay_rate, norm_gain):
    shards, group = lax.axis_size("dp"), lax.axis_size("tensor")
    steps, live = projected.shape[:2]
    slots, heads, dim = states.shape[:3]
    width = heads * dim
    place = lax.axis_index(("dp", "tensor")).astype(jnp.int32).reshape(1)
    states = states.reshape(slots, width, dim)

    row_0, row_1 = pick(
        place, from_shard, from_slot, projected, states, shards, live, group, (-2, 2)
    )
    half_1, half_0 = swapped(row_1, 1), swapped(row_0, 0)
    rate = jnp.repeat(decay_rate, dim).reshape(1, width)
    gain = norm_gain.reshape(1, width)
    query, grown, base, gated, decay, local, here, outer, token, row_0, row_1 = prepare(
        place, from_shard, from_slot, projected, rate, gain, row_1, states, shards, live,
        group, (-1, 1),
    )
    near_1, near_0 = swapped(row_1, 1), swapped(row_0, 0)
    sent = relay(half_0, half_1, token, heads)
    lead_1, lead_0 = swapped(sent[0], 1), swapped(sent[1], 0)
    rest_1, rest_0 = swapped(sent[2], 1), swapped(sent[3], 0)

    raw, sums = raw_of(
        place, from_shard, (lead_0, lead_1, near_1, near_0),
        (local, query, grown, base), shards, live, group,
    )
    totals = lax.all_to_all(sums, "tensor", 0, 0)
    final, token = final_of(
        place, from_shard, here, (lead_0, lead_1), (near_1, near_0), (rest_1, rest_0),
        (outer, decay), shards, live, group,
    )
    attended = attend(totals, raw, gated, token, live, steps, width * group)
    return attended, final.reshape(live, heads, dim, dim)


def solution(mesh):
    return jax.shard_map(
        on_device,
        mesh=mesh,
        in_specs=(
            P("dp", "tensor", None, None),
            P(),
            P(),
            P(None, "dp", None, "tensor"),
            P("tensor"),
            P("tensor"),
        ),
        out_specs=(P(None, "dp", "tensor"), P("dp", "tensor", None, None)),
        check_vma=False,
    )
```

```python
import functools
import jax
import jax.numpy as jnp
from jax import lax
from jax.experimental import pallas as pl
from jax.experimental.pallas import tpu as pltpu
from jax.sharding import PartitionSpec as P

EPS = 1e-05
F32 = jnp.float32
BF16 = jnp.bfloat16
EARLY = 3
TILE = 8
MIB = 1024 * 1024
SMEM = pl.BlockSpec(memory_space=pltpu.SMEM)
VMEM = pl.BlockSpec(memory_space=pltpu.VMEM)
HBM = pl.BlockSpec(memory_space=pltpu.HBM)


def swapped(block, first):
    shards, group = lax.axis_size("dp"), lax.axis_size("tensor")
    route = []
    for i in range(0, shards, 2):
        for j in range(group):
            low = (first + j % 2 + i) % shards
            high = (low + 1) % shards
            route += [
                (low * group + j, high * group + j),
                (high * group + j, low * group + j),
            ]
    return lax.ppermute(block, ("dp", "tensor"), route)


def spot(place, group):
    shard = lax.div(place[0], group)
    return shard, 2 * ((shard ^ lax.rem(place[0], group)) & 1) - 1


def start_all(copies):
    for copy in copies:
        copy.start()


def wait_all(copies):
    for copy in copies:
        copy.wait()


def in_hbm(*arrays):
    return [pltpu.with_memory_space_constraint(x, pltpu.HBM) for x in arrays]


def products(query, state):
    q_high = query.astype(BF16).astype(F32)
    both = jnp.concatenate([q_high, query - q_high], axis=0).astype(BF16)
    high = state.astype(BF16)
    low = (state - high.astype(F32)).astype(BF16)
    first = jnp.dot(both, high, preferred_element_type=F32)
    second = jnp.dot(both, low, preferred_element_type=F32)
    return first[:TILE] + first[TILE:] + second[:TILE]


def pick_kernel(shards, live, group, strides, place, shard_hbm, slot_hbm, projected, states, *refs):
    n_rows = len(strides)
    outs = refs[:n_rows]
    shard_ref, slot_ref, inputs, staged, sems = refs[n_rows:]
    dim = outs[0].shape[1]
    rows = states.shape[1]
    device, side = spot(place, group)
    copies = [
        pltpu.make_async_copy(shard_hbm, shard_ref, sems.at[0]),
        pltpu.make_async_copy(slot_hbm, slot_ref, sems.at[1]),
        pltpu.make_async_copy(projected, inputs, sems.at[2]),
        pltpu.make_async_copy(states, staged, sems.at[3]),
    ]
    start_all(copies)
    tile_rows = rows // dim * TILE
    for n in range(n_rows):
        outs[n][rows : rows + tile_rows] = jnp.zeros((tile_rows, dim), F32)
    copies[2].wait()
    for step in range(inputs.shape[0]):
        for row in range(live):
            query = jax.nn.silu(inputs[step, row].astype(F32))[0:1]
            for head in range(rows // dim):
                at = rows + head * TILE + step * live + row
                part = query[:, head * dim : (head + 1) * dim]
                for n in range(n_rows):
                    outs[n][at : at + 1] = part
    wait_all(copies[:2])
    slots = [
        slot_for(stride, shards, live, device, side, shard_ref, slot_ref)
        for stride in strides
    ]
    copies[3].wait()
    for n, slot in enumerate(slots):
        outs[n][0:rows] = staged[slot]


def pick(place, from_shard, from_slot, projected, states, shards, live, group, strides):
    rows, dim = states.shape[1:]
    tile_rows = rows // dim * TILE
    return pl.pallas_call(
        functools.partial(pick_kernel, shards, live, group, strides),
        out_shape=[jax.ShapeDtypeStruct((rows + tile_rows, dim), F32)] * len(strides),
        in_specs=[SMEM] + [HBM] * 4,
        out_specs=[VMEM] * len(strides),
        scratch_shapes=[
            pltpu.SMEM(from_shard.shape, jnp.int32),
            pltpu.SMEM(from_slot.shape, jnp.int32),
            pltpu.VMEM(projected.shape, projected.dtype),
            pltpu.VMEM(states.shape, F32),
            pltpu.SemaphoreType.DMA((4,)),
        ],
        compiler_params=pltpu.CompilerParams(vmem_limit_bytes=6 * MIB),
        name="pick_rows",
    )(place, *in_hbm(from_shard, from_slot, projected, states))


def relay_kernel(from_0, from_1, _, lead_1, lead_0, rest_1, rest_0):
    dim = from_1.shape[1]
    heads = rest_0.shape[0] // dim + EARLY
    rows, early = heads * dim, EARLY * dim
    tile_rows = heads * TILE
    for source, other, lead, rest in (
        (from_0, from_1, lead_1, rest_1),
        (from_1, from_0, lead_0, rest_0),
    ):
        for head in range(heads):
            part = slice(head * TILE, (head + 1) * TILE)
            query = other[rows + head * TILE : rows + (head + 1) * TILE]
            state = source[head * dim : (head + 1) * dim]
            lead[part] = products(query, state)
            if head < EARLY:
                lead[tile_rows + head * dim : tile_rows + (head + 1) * dim] = state
            else:
                rest[(head - EARLY) * dim : (head - EARLY + 1) * dim] = state


def relay(from_0, from_1, after, heads):
    dim = from_0.shape[1]
    lead = jax.ShapeDtypeStruct((heads * TILE + EARLY * dim, dim), F32)
    rest = jax.ShapeDtypeStruct(((heads - EARLY) * dim, dim), F32)
    return pl.pallas_call(
        relay_kernel,
        out_shape=[lead, lead, rest, rest],
        in_specs=[VMEM] * 3,
        out_specs=[VMEM] * 4,
        compiler_params=pltpu.CompilerParams(vmem_limit_bytes=6 * MIB),
        name="relay_rows",
    )(from_0, from_1, after)


def gap_of(row, shards, live, device, shard_ref):
    return lax.rem(device - shard_ref[device * live + row] + shards, shards)


def at_stride(gap, stride, shards, side):
    return gap == lax.rem(stride * side + shards, shards)


def slot_for(stride, shards, live, device, side, shard_ref, slot_ref):
    target = lax.rem(device + stride * side + shards, shards)
    slot = jnp.int32(0)
    for row in range(live):
        mine = shard_ref[target * live + row] == device
        slot = jnp.where(mine, slot_ref[target * live + row], slot)
    return slot


def prepare_kernel(
    shards, live, group, strides, place, shard_ref, slot_ref, projected, rate, gain, _, states,
    query, grown, base, gated, decay, made, here, outer, token, *refs,
):
    outs, (parts, sems) = refs[:-2], refs[-2:]
    token[...] = jnp.zeros_like(token)
    rows, dim = here.shape[1:]
    heads = rows // dim
    steps = projected.shape[0]
    device, side = spot(place, group)
    copies = [
        pltpu.make_async_copy(
            states.at[slot_ref[device * live + row]], here.at[row], sems.at[row]
        )
        for row in range(live)
    ]
    start_all(copies)
    sends = []
    for n, stride in enumerate(strides):
        slot = slot_for(stride, shards, live, device, side, shard_ref, slot_ref)
        sends.append(pltpu.make_async_copy(states.at[slot], outs[n], sems.at[live + n]))
    start_all(sends)
    parts[...] = jnp.zeros_like(parts)
    for step in range(steps):
        for row in range(live):
            block = projected[step, row].astype(F32)
            at = step * live + row
            for n in range(parts.shape[0]):
                parts[n, at : at + 1] = block[n : n + 1]
    queries, keys, values = (jax.nn.silu(parts[n]) for n in range(3))
    index = lax.broadcasted_iota(jnp.int32, queries.shape, 0)
    step_of = (index // live).astype(F32)
    rates = jnp.broadcast_to(rate[...], queries.shape)
    query[...] = queries
    gated[...] = jax.nn.sigmoid(parts[3]) * gain[...]
    grown[...] = jnp.exp(-rates * (step_of + 1.0))
    decay[...] = jnp.exp(-steps * rate[...])
    faded = keys * jnp.exp(-rates * jnp.maximum(steps - 1.0 - step_of, 0.0))
    later = lambda x, count: jnp.concatenate(
        [jnp.zeros((count, rows), F32), x[: TILE - count]], axis=0
    )
    total = jnp.zeros_like(queries)
    for lag in range(steps):
        key = later(keys, lag * live) if lag else keys
        value = later(values, lag * live) if lag else values
        product = queries * key
        match = jnp.concatenate(
            [
                jnp.broadcast_to(
                    jnp.sum(
                        product[:, head * dim : (head + 1) * dim], axis=1, keepdims=True
                    ),
                    (TILE, dim),
                )
                for head in range(heads)
            ],
            axis=1,
        )
        total = total + jnp.exp(-rates * float(lag)) * match * value
    base[...] = total

    def halves(x):
        high = x.astype(BF16).astype(F32)
        return high, x - high

    nothing = jnp.zeros_like(queries)
    v_high, v_low = halves(values)
    right = jnp.concatenate([v_high, v_high, v_low, nothing], axis=0).astype(BF16)
    for row in range(live):
        k_high, k_low = halves(jnp.where(lax.rem(index, live) == row, faded, 0.0))
        left = jnp.concatenate([k_high, k_low, k_high, nothing], axis=0).astype(BF16)
        for head in range(heads):
            span = slice(head * dim, (head + 1) * dim)
            outer[row, span] = lax.dot_general(
                left[:, span],
                right[:, span],
                (((0,), (0,)), ((), ())),
                preferred_element_type=F32,
            )
    wait_all(copies)
    for row in range(live):
        for head in range(heads):
            span = slice(head * dim, (head + 1) * dim)
            made[row, head * TILE : (head + 1) * TILE] = products(
                queries[:, span], here[row, span]
            )
    wait_all(sends)


def prepare(
    place, from_shard, from_slot, projected, rate, gain, after, states, shards, live, group, strides
):
    rows, dim = states.shape[1:]
    tile = jax.ShapeDtypeStruct((TILE, rows), F32)
    whole = jax.ShapeDtypeStruct((live, rows, dim), F32)
    return pl.pallas_call(
        functools.partial(prepare_kernel, shards, live, group, strides),
        out_shape=[tile] * 4
        + [
            jax.ShapeDtypeStruct((1, rows), F32),
            jax.ShapeDtypeStruct((live, rows // dim * TILE, dim), F32),
            whole,
            whole,
            jax.ShapeDtypeStruct((TILE, dim), F32),
        ]
        + [jax.ShapeDtypeStruct((rows, dim), F32)] * len(strides),
        in_specs=[SMEM] * 3 + [VMEM] * 4 + [HBM],
        out_specs=[VMEM] * (9 + len(strides)),
        scratch_shapes=[
            pltpu.VMEM((projected.shape[2], TILE, rows), F32),
            pltpu.SemaphoreType.DMA((live + len(strides),)),
        ],
        compiler_params=pltpu.CompilerParams(vmem_limit_bytes=8 * MIB),
        name="prepare_rows",
    )(place, from_shard, from_slot, projected, rate, gain, after, *in_hbm(states))


def diagonal(dim):
    row = lax.broadcasted_iota(jnp.int32, (TILE, dim), 0)
    return row == lax.broadcasted_iota(jnp.int32, (TILE, dim), 1)


def raw_kernel(
    shards, live, group, place, shard_ref, lead_0, lead_1, near_1, near_0,
    local, query, grown, base, raw, sums, made, tiles, sem,
):
    rows, dim = near_0.shape
    heads = rows // dim
    tile_rows = heads * TILE
    for row in range(live):
        made[row] = local[row]
    for n, near in enumerate((near_1, near_0)):
        for head in range(heads):
            span = slice(head * dim, (head + 1) * dim)
            made[live + n, head * TILE : (head + 1) * TILE] = products(
                query[:, span], near[span]
            )
    for n, lead in enumerate((lead_1, lead_0)):
        made[live + 2 + n] = lead[0:tile_rows]
    picks = []
    device, side = spot(place, group)
    for row in range(live):
        gap = gap_of(row, shards, live, device, shard_ref)
        index = jnp.int32(row)
        for n, stride in enumerate((-1, 1, -2, 2)):
            index = jnp.where(at_stride(gap, stride, shards, side), live + n, index)
        picks.append(index)
    which = lax.rem(lax.broadcasted_iota(jnp.int32, (TILE, dim), 0), live)
    total = jnp.zeros((TILE, dim), F32)
    for head in range(heads):
        span = slice(head * dim, (head + 1) * dim)
        part = slice(head * TILE, (head + 1) * TILE)
        tile = made[picks[0], part]
        for row in range(1, live):
            tile = jnp.where(which == row, made[picks[row], part], tile)
        tile = tile * grown[:, span] + base[:, span]
        raw[:, span] = tile
        total = total + tile * tile
    total = jnp.broadcast_to(jnp.sum(total, axis=1, keepdims=True), (TILE, dim))
    total = jnp.sum(jnp.where(diagonal(dim), total, 0.0), axis=0, keepdims=True)
    for peer in range(sums.shape[0]):
        tiles[peer] = total
    copy = pltpu.make_async_copy(tiles, sums, sem)
    copy.start()
    copy.wait()


def raw_of(place, from_shard, arrived, small, shards, live, group):
    rows, dim = arrived[-1].shape
    return pl.pallas_call(
        functools.partial(raw_kernel, shards, live, group),
        out_shape=[
            jax.ShapeDtypeStruct((TILE, rows), F32),
            jax.ShapeDtypeStruct((group, 1, dim), F32),
        ],
        in_specs=[SMEM] * 2 + [VMEM] * (len(arrived) + len(small)),
        out_specs=[VMEM, HBM],
        scratch_shapes=[
            pltpu.VMEM((live + 4, rows // dim * TILE, dim), F32),
            pltpu.VMEM((group, 1, dim), F32),
            pltpu.SemaphoreType.DMA(()),
        ],
        compiler_params=pltpu.CompilerParams(vmem_limit_bytes=6 * MIB),
        cost_estimate=pl.CostEstimate(flops=10**12, bytes_accessed=MIB, transcendentals=0),
        name="raw_rows",
    )(place, from_shard, *arrived, *small)


def final_kernel(
    shards, live, group, place, shard_ref, here, lead_0, lead_1, near_1, near_0,
    rest_1, rest_0, outer, decay, final, token, held, made, sems_in, sems,
):
    rows, dim = here.shape[1:]
    heads = rows // dim
    early, tile_rows = EARLY * dim, heads * TILE
    device, side = spot(place, group)
    token[...] = jnp.zeros_like(token)

    def loads(row, lead, rest):
        return [
            pltpu.make_async_copy(
                lead.at[tile_rows : tile_rows + early],
                held.at[row, 0:early],
                sems_in.at[row, 0],
            ),
            pltpu.make_async_copy(rest, held.at[row, early:rows], sems_in.at[row, 1]),
        ]

    cases = []
    for row in range(live):
        gap = gap_of(row, shards, live, device, shard_ref)
        far_0 = at_stride(gap, 2, shards, side)
        far_1 = at_stride(gap, -2, shards, side)
        for found, lead, rest in ((far_0, lead_0, rest_0), (far_1, lead_1, rest_1)):

            @pl.when(found)
            def _():
                start_all(loads(row, lead, rest))

        cases.append(
            [
                (gap == 0, here.at[row]),
                (at_stride(gap, 1, shards, side), near_0),
                (at_stride(gap, -1, shards, side), near_1),
                (jnp.logical_or(far_0, far_1), held.at[row]),
            ]
        )
    copies = []
    for row in range(live):

        @pl.when(cases[row][3][0])
        def _():
            wait_all(loads(row, lead_0, rest_0))

        for half in range(2):
            span = range(half * heads // 2, (half + 1) * heads // 2)
            for found, source in cases[row]:

                @pl.when(found)
                def _():
                    for head in span:
                        block = slice(head * dim, (head + 1) * dim)
                        made[row, block] = (
                            decay[:, block] * source[block] + outer[row, block]
                        )

            block = slice(span.start * dim, span.stop * dim)
            copy = pltpu.make_async_copy(
                made.at[row, block], final.at[row, block], sems.at[row, half]
            )
            copy.start()
            copies.append(copy)
    wait_all(copies)


def final_of(place, from_shard, here, lead, near, rest, small, shards, live, group):
    rows, dim = here.shape[1:]
    return pl.pallas_call(
        functools.partial(final_kernel, shards, live, group),
        out_shape=[
            jax.ShapeDtypeStruct((live, rows, dim), F32),
            jax.ShapeDtypeStruct((TILE, dim), F32),
        ],
        in_specs=[SMEM] * 2 + [VMEM] + [HBM] * 2 + [VMEM] * 2 + [HBM] * 2 + [VMEM] * 2,
        out_specs=[pl.BlockSpec(memory_space=pl.ANY), VMEM],
        scratch_shapes=[
            pltpu.VMEM((live, rows, dim), F32),
            pltpu.VMEM((live, rows, dim), F32),
            pltpu.SemaphoreType.DMA((live, 2)),
            pltpu.SemaphoreType.DMA((live, 2)),
        ],
        compiler_params=pltpu.CompilerParams(vmem_limit_bytes=8 * MIB),
        cost_estimate=pl.CostEstimate(flops=10**10, bytes_accessed=MIB, transcendentals=0),
        name="final_rows",
    )(place, from_shard, here, *in_hbm(*lead), *near, *in_hbm(*rest), *small)


def attend_kernel(live, features, totals, raw, gated, _, attended):
    dim = totals.shape[2]
    total = totals[0]
    for peer in range(1, totals.shape[0]):
        total = total + totals[peer]
    total = jnp.where(diagonal(dim), jnp.broadcast_to(total, (TILE, dim)), 0.0)
    total = jnp.sum(total, axis=1, keepdims=True)
    scale = jnp.broadcast_to(lax.rsqrt(total / features + EPS), raw.shape)
    tile = raw[...] * scale * gated[...]
    for step in range(attended.shape[0]):
        attended[step] = tile[step * live : (step + 1) * live].astype(BF16)


def attend(totals, raw, gated, after, live, steps, features):
    return pl.pallas_call(
        functools.partial(attend_kernel, live, features),
        out_shape=jax.ShapeDtypeStruct((steps, live, raw.shape[1]), BF16),
        in_specs=[VMEM] * 4,
        out_specs=VMEM,
        compiler_params=pltpu.CompilerParams(vmem_limit_bytes=4 * MIB),
        name="attend_rows",
    )(totals, raw, gated, after)


def on_device(states, from_shard, from_slot, projected, decay_rate, norm_gain):
    shards, group = lax.axis_size("dp"), lax.axis_size("tensor")
    steps, live = projected.shape[:2]
    slots, heads, dim = states.shape[:3]
    width = heads * dim
    place = lax.axis_index(("dp", "tensor")).astype(jnp.int32).reshape(1)
    states = states.reshape(slots, width, dim)

    row_0, row_1 = pick(
        place, from_shard, from_slot, projected, states, shards, live, group, (-2, 2)
    )
    half_1, half_0 = swapped(row_1, 1), swapped(row_0, 0)
    rate = jnp.repeat(decay_rate, dim).reshape(1, width)
    gain = norm_gain.reshape(1, width)
    query, grown, base, gated, decay, local, here, outer, token, row_0, row_1 = prepare(
        place, from_shard, from_slot, projected, rate, gain, row_1, states, shards, live,
        group, (-1, 1),
    )
    near_1, near_0 = swapped(row_1, 1), swapped(row_0, 0)
    sent = relay(half_0, half_1, token, heads)
    lead_1, lead_0 = swapped(sent[0], 1), swapped(sent[1], 0)
    rest_1, rest_0 = swapped(sent[2], 1), swapped(sent[3], 0)

    raw, sums = raw_of(
        place, from_shard, (lead_0, lead_1, near_1, near_0),
        (local, query, grown, base), shards, live, group,
    )
    totals = lax.all_to_all(sums, "tensor", 0, 0)
    final, token = final_of(
        place, from_shard, here, (lead_0, lead_1), (near_1, near_0), (rest_1, rest_0),
        (outer, decay), shards, live, group,
    )
    attended = attend(totals, raw, gated, token, live, steps, width * group)
    return attended, final.reshape(live, heads, dim, dim)


def solution(mesh):
    return jax.shard_map(
        on_device,
        mesh=mesh,
        in_specs=(
            P("dp", "tensor", None, None),
            P(),
            P(),
            P(None, "dp", None, "tensor"),
            P("tensor"),
            P("tensor"),
        ),
        out_specs=(P(None, "dp", "tensor"), P("dp", "tensor", None, None)),
        check_vma=False,
    )
```
